32 devices in a mesh: dp: 4 (over x, core), context: 4 (over z), experts: 2 (over y).
Axes of the slice: x: 2, y: 2, z: 4, core: 2. Of those that a mesh axis runs over, the one named last changes fastest.
Arguments:
- tokens: bfloat16 [8, 1024, 768], P(('dp', 'experts'), 'context'), may hold values from -6 to 6
- norm1_gain: float32 [768], replicated, may hold values from 0.5 to 1.5
- qkv_weight: bfloat16 [768, 2304], replicated, may hold values from -0.21875 to 0.21875
- out_weight: bfloat16 [768, 768], replicated, may hold values from -2.5 to 2.5
- norm2_gain: float32 [768], replicated, may hold values from 0.5 to 1.5
- router_weight: bfloat16 [768, 4], replicated, may hold values from -0.15625 to 0.15625
- expert_gate: bfloat16 [4, 768, 2048], P('experts'), may hold values from -0.21875 to 0.21875
- expert_up: bfloat16 [4, 768, 2048], P('experts'), may hold values from -0.21875 to 0.21875
- expert_down: bfloat16 [4, 2048, 768], P('experts'), may hold values from -0.25 to 0.25
- shared_gate: bfloat16 [768, 2048], replicated, may hold values from -0.21875 to 0.21875
- shared_up: bfloat16 [768, 2048], replicated, may hold values from -0.21875 to 0.21875
- shared_down: bfloat16 [2048, 768], replicated, may hold values from -0.25 to 0.25
- routes: int32 [4, 8, 256, 2], P('context', ('dp', 'experts')), may hold values from 0 to 3, all different within a row; in each aligned block of 256 rows (0 to 255, 256 to 511, ..., all dimensions but the last counted through in order) at most 160 rows name the same one
- cotangent: bfloat16 [8, 1024, 768], P(('dp', 'experts'), 'context'), may hold values from -6 to 6
Outputs:
- output: bfloat16 [8, 1024, 768], P(('dp', 'experts'), 'context')
- input_grad: float32 [8, 1024, 768], P(('dp', 'experts'), 'context')
- norm1_grad: float32 [768], P(('dp', 'context'))
- qkv_grad: float32 [768, 2304], P(('dp', 'context'))
- out_grad: float32 [768, 768], P(('dp', 'context'))
- norm2_grad: float32 [768], P(('dp', 'context'))
- router_grad: float32 [768, 4], P(('dp', 'context'))
- expert_gate_grad: float32 [4, 768, 2048], P('experts', ('dp', 'context'))
- expert_up_grad: float32 [4, 768, 2048], P('experts', ('dp', 'context'))
- expert_down_grad: float32 [4, 2048, 768], P('experts', ('dp', 'context'))
- shared_gate_grad: float32 [768, 2048], P(('dp', 'context'))
- shared_up_grad: float32 [768, 2048], P(('dp', 'context'))
- shared_down_grad: float32 [2048, 768], P(('dp', 'context'))
The draws below stay inside these ranges and needn't reach their ends.
Inputs may be any that keep to these rules, and one draw needn't show every extreme that they name: `routes`: each token names 2 different experts. Within the rows of one device (aligned blocks of 256 rows, leading dimensions taken in order) no expert is named more than 160 times, and this bound is reached.
All inputs are finite; a program needn't handle non-finite values.
Results may differ from the reference program's by a relative error of at most 0.03.
Values may be sent and summed in bfloat16 or wider, within the bound.
No kernel may reach another device: no remote copies, remote signals or barrier semaphores. Data moves between devices by JAX's collectives and lax.ppermute only.
A program may use at most 384 MiB of HBM per device.

```python
import math
import jax
import jax.numpy as jnp
import numpy as np
from jax import lax

D = 768
HEAD_DIM = 64
FF = 2048
TOPK = 2
TOK_DEV = 256
BLOCK = 256
SEQ_LEN = 1024
SPAN = 256
BATCH = 8
EXPERTS = 4
CAP = 160
N_CONTEXT = 4


def shard_levels(own_key, dims, shards, smallest, high):
    factor_of = 1.0
    for dim, shards_of in shards:
        draws = jax.random.uniform(jax.random.fold_in(jax.random.fold_in(own_key, 6), dim), (shards_of,), jnp.float32, smallest / len(shards), high / len(shards))
        factor_of = factor_of * jnp.repeat(jnp.exp(draws), dims[dim] // shards_of).reshape((-1,) + (1,) * (len(dims) - 1 - dim))
    return factor_of


def deal_out(stream_key, own, number, rows, number_of, top, most, slope):
    ranking = jax.random.permutation(stream_key, number_of)
    crowded, usual = load_shares(number_of, rows * top, most, slope, True), load_shares(number_of, rows * top, most, slope, False)
    places = jnp.arange(number_of)

    def named(sizes, rotation):
        used = int((sizes > 0).sum())
        fixed = max(1, used // 4)
        passed = fixed + (places - fixed + rotation * (used - fixed)) % max(1, number_of - fixed)
        return jnp.zeros((number_of,), jnp.int32).at[ranking[jnp.where(places < fixed, places, passed)]].set(jnp.asarray(sizes, jnp.int32))

    sizes = jnp.where(number % 4 == 0, named(crowded, number // 4), named(usual, number - number // 4 - 1))
    mixed = jax.random.permutation(jax.random.fold_in(own, 3), number_of)
    donor, sink = mixed[0:number_of // 2 * 2:2], mixed[1:number_of // 2 * 2:2]
    slack = jnp.minimum(sizes[donor] - 1, most - sizes[sink]) // 2
    slack = jnp.where((donor == ranking[0]) | (sink == ranking[0]) | (sizes[sink] == 0), 0, jnp.maximum(slack, 0))
    passed = jax.random.randint(jax.random.fold_in(own, 4), (number_of // 2,), 0, 1 << 20) % (slack + 1)
    sizes = sizes.at[donor].add(-passed).at[sink].add(passed)
    members = jnp.searchsorted(jnp.cumsum(sizes), jnp.arange(rows * top), side="right").astype(jnp.int32)
    listing = members.reshape(top, rows).T
    listing = listing[jax.random.permutation(jax.random.fold_in(own, 1), rows)]
    rotation = jax.random.randint(jax.random.fold_in(own, 2), (rows, 1), 0, top)
    return jnp.take_along_axis(listing, (jnp.arange(top)[None, :] + rotation) % top, axis=1)


def load_shares(amount, total, limit, skew, full):
    weights = [(1 << 20) // math.isqrt(standing ** skew) + 1 for standing in range(1, amount + 1)]
    largest = limit if full else min(limit, max(-(-total // amount), total * weights[0] // sum(weights)))
    least = 1 if total - largest >= amount - 1 else 0
    given, spare = [largest] + [least] * (amount - 1), total - largest - least * (amount - 1)
    while spare > 0:
        candidates = [i for i in range(1, amount) if given[i] < largest] or [i for i in range(1, amount) if given[i] < limit]
        whole, budget = sum([weights[i] for i in candidates]), spare
        for i in candidates:
            extra = min(limit - given[i], max(1, budget * weights[i] // whole), spare)
            given[i] = given[i] + extra
            spare = spare - extra
    return np.array(given)


def normal_values(rng, shape, scale, limit, shards=(), held_as=jnp.bfloat16):
    entries = jax.random.normal(rng, shape, jnp.float32) * scale
    if len(shards) > 0:
        entries = shard_levels(rng, shape, shards, -0.22, 0.18) * entries
    return jnp.clip(entries, min=-limit, max=limit).astype(held_as)


def setup_inputs(seed: int = 0) -> dict:
    streams_of = jax.random.split(jax.random.key(seed), 15)
    tokens = normal_values(streams_of[0], (BATCH, SEQ_LEN, D), 1.0, 6.0, ((0, 8), (1, 4)))
    norm1_gain = jnp.clip(1.0 + 0.1 * jax.random.normal(streams_of[1], (D,), jnp.float32), 0.5, 1.5)
    qkv_weight = normal_values(streams_of[2], (D, 3 * D), D ** -0.5, 0.21875)
    out_weight = normal_values(streams_of[3], (D, D), (D // 128) ** -0.5, 2.5)
    norm2_gain = jnp.clip(1.0 + 0.1 * jax.random.normal(streams_of[4], (D,), jnp.float32), 0.5, 1.5)
    router_weight = normal_values(streams_of[5], (D, EXPERTS), (2 * D) ** -0.5, 0.15625)
    expert_gate = normal_values(streams_of[6], (EXPERTS, D, FF), D ** -0.5, 0.21875, ((0, 2),))
    expert_up = normal_values(streams_of[7], (EXPERTS, D, FF), D ** -0.5, 0.21875, ((0, 2),))
    expert_down = normal_values(streams_of[8], (EXPERTS, FF, D), (FF // 4) ** -0.5, 0.25, ((0, 2),))
    shared_gate = normal_values(streams_of[9], (D, FF), D ** -0.5, 0.21875)
    shared_up = normal_values(streams_of[10], (D, FF), D ** -0.5, 0.21875)
    shared_down = normal_values(streams_of[11], (FF, D), (FF // 4) ** -0.5, 0.25)
    routes_keys = jax.random.split(jax.random.fold_in(streams_of[12], 1), N_CONTEXT * BATCH * SPAN // TOK_DEV)
    routes_turns = jax.random.permutation(jax.random.fold_in(streams_of[12], 3), N_CONTEXT * BATCH * SPAN // TOK_DEV)
    routes = jax.vmap(lambda own, number: deal_out(jax.random.fold_in(streams_of[12], 2), own, number, TOK_DEV, EXPERTS, TOPK, CAP, 1))(routes_keys, routes_turns).reshape((N_CONTEXT, BATCH, SPAN, TOPK))
    cotangent = normal_values(streams_of[13], (BATCH, SEQ_LEN, D), 1.0, 6.0, ((0, 8), (1, 4)))
    return dict(tokens=tokens, norm1_gain=norm1_gain, qkv_weight=qkv_weight, out_weight=out_weight, norm2_gain=norm2_gain, router_weight=router_weight, expert_gate=expert_gate, expert_up=expert_up, expert_down=expert_down, shared_gate=shared_gate, shared_up=shared_up, shared_down=shared_down, routes=routes, cotangent=cotangent)


@jax.custom_vjp
def low(v):
    return lax.optimization_barrier(v.astype(jnp.bfloat16)).astype(jnp.float32)

@jax.custom_vjp
def low_back(v):
    return v

def low_keep(v):
    return (low(v), None)

def low_pass(kept, grad):
    return (grad,)

def back_keep(v):
    return (v, None)

def back_low(kept, grad):
    return (low(grad),)
low.defvjp(low_keep, low_pass)
low_back.defvjp(back_keep, back_low)
norm_eps = 1e-05
masked_score = -1e+30
highest = lax.Precision.HIGHEST

def both_ways(value):
    return low_back(low(value))

def product(spec, left, right):
    return jnp.einsum(spec, left, right, precision=highest, preferred_element_type=jnp.float32)

def rms_norm(field, gain):
    factor = lax.rsqrt(lax.optimization_barrier(jnp.mean(field * field, axis=-1, keepdims=True)) + norm_eps)
    return field * factor * gain

def rotate(field, positions):
    half = field.shape[-1] // 2
    freqs = 10000.0 ** (-2.0 * jnp.arange(half, dtype=jnp.float32) / field.shape[-1])
    angles = positions.astype(jnp.float32)[:, None] * freqs[None, :]
    cosine = jnp.cos(angles)[:, None, :]
    sine = jnp.sin(angles)[:, None, :]
    first = field[..., :half]
    second = field[..., half:]
    return jnp.concatenate([first * cosine - second * sine, second * cosine + first * sine], axis=-1)

def attend(query, keys, values):
    batch, length, heads, head_dim = query.shape
    block_rows = math.gcd(length, 512)
    blocks = length // block_rows
    factor = head_dim ** (-0.5)
    key_block = jnp.arange(length) // BLOCK
    query_parts = jnp.moveaxis(query.reshape(batch, blocks, block_rows, heads, head_dim), 1, 0)

    def one_block(items):
        part, index = items
        query_block = (index * block_rows + jnp.arange(block_rows)) // BLOCK
        scores = low_back(product('bqhd,bkhd->bhqk', part, keys) * factor)
        visible = key_block[None, :] <= query_block[:, None]
        scores = jnp.where(visible, scores, masked_score)
        summit = lax.optimization_barrier(jnp.max(scores, axis=-1, keepdims=True))
        weights = jnp.exp(scores - summit)
        probs = low(weights / lax.optimization_barrier(jnp.sum(weights, axis=-1, keepdims=True)))
        return product('bhqk,bkhd->bqhd', probs, values)
    results = lax.map(jax.checkpoint(one_block), (query_parts, jnp.arange(blocks)))
    return jnp.moveaxis(results, 0, 1).reshape(batch, length, heads, head_dim)

def forward(tokens, routes, params):
    norm1_gain, qkv_weight, out_weight, norm2_gain, router_weight, expert_gate, expert_up, expert_down, shared_gate, shared_up, shared_down = params
    batch, length, width = tokens.shape
    heads = width // HEAD_DIM
    positions = jnp.arange(length)
    first_in = low(rms_norm(tokens, norm1_gain))
    projected = low_back(product('bld,de->ble', first_in, qkv_weight)).reshape(batch, length, 3, heads, HEAD_DIM)
    query = low(rotate(projected[:, :, 0], positions))
    keys = low(rotate(projected[:, :, 1], positions))
    values = low(projected[:, :, 2])
    context = both_ways(attend(query, keys, values)).reshape(batch, length, width)
    middle = tokens + low_back(product('bld,de->ble', context, out_weight))
    mixed_in = low(rms_norm(middle, norm2_gain))
    logits = product('bld,de->ble', mixed_in, router_weight)
    chosen = jax.nn.one_hot(routes, EXPERTS, dtype=jnp.float32)
    picked = lax.optimization_barrier(jnp.sum(chosen * logits[:, :, None, :], axis=-1))
    picked = picked - lax.optimization_barrier(jnp.max(picked, axis=-1, keepdims=True))
    raised = jnp.exp(picked)
    gates = raised / lax.optimization_barrier(jnp.sum(raised, axis=-1, keepdims=True))
    weighting = lax.optimization_barrier(jnp.sum(gates[..., None] * chosen, axis=2))
    mixed = jnp.zeros_like(tokens)
    for index in range(EXPERTS):
        entry = low_back(mixed_in)
        gate_part = low_back(product('bld,df->blf', entry, expert_gate[index]))
        up_part = low_back(product('bld,df->blf', entry, expert_up[index]))
        hidden = low(gate_part * jax.nn.sigmoid(gate_part) * up_part)
        result = both_ways(product('blf,fd->bld', hidden, expert_down[index]))
        mixed = mixed + weighting[..., index:index + 1] * result
    shared_gate_part = low_back(product('bld,df->blf', mixed_in, shared_gate))
    shared_up_part = low_back(product('bld,df->blf', mixed_in, shared_up))
    shared_hidden = low(shared_gate_part * jax.nn.sigmoid(shared_gate_part) * shared_up_part)
    shared_out = product('blf,fd->bld', shared_hidden, shared_down)
    return middle + mixed + shared_out

def reference(tokens, norm1_gain, qkv_weight, out_weight, norm2_gain, router_weight, expert_gate, expert_up, expert_down, shared_gate, shared_up, shared_down, routes, cotangent):
    params = tuple((weight.astype(jnp.float32) for weight in (norm1_gain, qkv_weight, out_weight, norm2_gain, router_weight, expert_gate, expert_up, expert_down, shared_gate, shared_up, shared_down)))
    ordered = jnp.transpose(routes, (1, 0, 2, 3)).reshape(BATCH, SEQ_LEN, TOPK)
    group = math.gcd(BATCH, max(1, 4096 // SEQ_LEN))
    rounds = BATCH // group

    def one_round(totals, items):
        block_tokens, block_routes, block_grad = items

        def apply(inputs, weights):
            return forward(inputs, block_routes, weights)
        result, pull = jax.vjp(apply, block_tokens.astype(jnp.float32), params)
        input_grad, weight_grads = pull(block_grad.astype(jnp.float32))
        totals = jax.tree.map(lambda left, right: left + right, totals, weight_grads)
        return (totals, (result.astype(jnp.bfloat16), input_grad))
    initial = jax.tree.map(jnp.zeros_like, params)
    totals, (result, input_grad) = lax.scan(one_round, initial, (tokens.reshape(rounds, group, SEQ_LEN, D), ordered.reshape(rounds, group, SEQ_LEN, TOPK), cotangent.reshape(rounds, group, SEQ_LEN, D)))
    return (result.reshape(BATCH, SEQ_LEN, D), input_grad.reshape(BATCH, SEQ_LEN, D), totals[0], totals[1], totals[2], totals[3], totals[4], totals[5], totals[6], totals[7], totals[8], totals[9], totals[10])
```

```python
from functools import partial
import math

import jax
import jax.numpy as jnp
from jax import lax
from jax.experimental import pallas as pl
from jax.experimental.pallas import tpu as pltpu
from jax.sharding import PartitionSpec as P

HEAD_DIM = 64
BLOCK = 256


norm_eps = 1e-05
masked_score = -1e30
highest = lax.Precision.HIGHEST


def matmul(left, right):
    return jnp.dot(left, right, preferred_element_type=jnp.float32)


def contract(spec, left, right):
    return jnp.einsum(spec, left, right, preferred_element_type=jnp.float32)


def normalize(field):
    factor = lax.rsqrt(jnp.mean(field * field, axis=-1, keepdims=True) + norm_eps)
    return (field * factor, factor)


def norm_back(grad_out, normed, factor, gain):
    grad_norm = grad_out * gain
    inner = jnp.mean(grad_norm * normed, axis=-1, keepdims=True)
    return (factor * (grad_norm - normed * inner), jnp.sum(grad_out * normed, axis=0))


def rotation(positions, head_dim):
    half = head_dim // 2
    freqs = 10000.0 ** (-2.0 * jnp.arange(half, dtype=jnp.float32) / head_dim)
    angles = positions.astype(jnp.float32)[:, None] * freqs[None, :]
    return (jnp.cos(angles)[:, None, None, :], jnp.sin(angles)[:, None, None, :])


def rotate(field, cosine, sine):
    half = field.shape[-1] // 2
    first = field[..., :half]
    second = field[..., half:]
    return jnp.concatenate(
        [first * cosine - second * sine, second * cosine + first * sine], axis=-1
    )


def rotate_back(grad, cosine, sine):
    half = grad.shape[-1] // 2
    first = grad[..., :half]
    second = grad[..., half:]
    return jnp.concatenate(
        [first * cosine + second * sine, second * cosine - first * sine], axis=-1
    )


def silu_back(grad_hidden, gate_part, up_part):
    sigmoid_value = jax.nn.sigmoid(gate_part)
    active = gate_part * sigmoid_value
    grad_gate = grad_hidden * up_part * sigmoid_value * (1.0 + gate_part * (1.0 - sigmoid_value))
    grad_up = grad_hidden * active
    return (grad_gate.astype(jnp.bfloat16), grad_up.astype(jnp.bfloat16))


def score_block(queries, keys_part, query_block, start):
    size = keys_part.shape[0]
    seqs, heads, head_dim = (queries.shape[1], queries.shape[2], queries.shape[3])
    keys_four = keys_part.reshape(size, seqs, heads, head_dim)
    scores = contract("qshd,kshd->shqk", queries, keys_four) * head_dim ** (-0.5)
    key_block = (start + jnp.arange(size)) // BLOCK
    visible = key_block[None, :] <= query_block[:, None]
    return (jnp.where(visible, scores, masked_score), visible, keys_four)


def attend_piece(queries, query_block, state, keys_part, values_part, start):
    size = keys_part.shape[0]
    seqs, heads, head_dim = (queries.shape[1], queries.shape[2], queries.shape[3])

    def compute(current):
        best, total, accum = current
        scores, visible, keys_four = score_block(queries, keys_part, query_block, start)
        new_best = jnp.maximum(best, jnp.max(scores, axis=-1))
        weights = jnp.where(visible, jnp.exp(scores - new_best[..., None]), 0.0)
        factor = jnp.exp(best - new_best)
        values_four = values_part.reshape(size, seqs, heads, head_dim)
        total = total * factor + jnp.sum(weights, axis=-1)
        accum = accum * factor[..., None] + contract(
            "shqk,kshd->shqd", weights.astype(jnp.bfloat16), values_four
        )
        return (new_best, total, accum)

    needed = start // BLOCK <= jnp.max(query_block)
    return lax.cond(needed, compute, lambda current: current, state)


def fold_keys(queries, query_block, state, pieces):
    keys_all, values_all = pieces
    length = keys_all.shape[0]
    size = math.gcd(length, 512)

    def step(index, current):
        first = index * size
        keys_part = lax.dynamic_slice_in_dim(keys_all, first, size, 0)
        values_part = lax.dynamic_slice_in_dim(values_all, first, size, 0)
        return attend_piece(queries, query_block, current, keys_part, values_part, first)

    return lax.fori_loop(0, length // size, step, state)


def block_grads(queries, query_block, grad_ctx, delta, log_total, keys_part, values_part, start):
    size = keys_part.shape[0]
    seqs, heads, head_dim = (queries.shape[1], queries.shape[2], queries.shape[3])
    scores, visible, keys_four = score_block(queries, keys_part, query_block, start)
    probs = jnp.where(visible, jnp.exp(scores - log_total[..., None]), 0.0)
    values_four = values_part.reshape(size, seqs, heads, head_dim)
    grad_probs = contract("qshd,kshd->shqk", grad_ctx, values_four)
    grad_scores = (probs * (grad_probs - delta[..., None])).astype(jnp.bfloat16)
    return (probs, grad_scores, keys_four)


def key_value_terms(
    queries, query_block, grad_ctx, delta, log_total, keys_part, values_part, start
):
    size = keys_part.shape[0]
    seqs, heads, head_dim = (queries.shape[1], queries.shape[2], queries.shape[3])
    width = heads * head_dim
    probs, grad_scores, keys_four = block_grads(
        queries, query_block, grad_ctx, delta, log_total, keys_part, values_part, start
    )
    grad_values = contract("shqk,qshd->kshd", probs.astype(jnp.bfloat16), grad_ctx)
    grad_keys = contract("shqk,qshd->kshd", grad_scores, queries) * head_dim ** (-0.5)
    return jnp.concatenate(
        [grad_keys.reshape(size, seqs, width), grad_values.reshape(size, seqs, width)], axis=-1
    )


def query_grads(queries, query_block, grad_ctx, delta, log_total, keys_all, values_all):
    length = keys_all.shape[0]
    size = math.gcd(length, 512)

    def step(index, accum):
        first = index * size
        keys_part = lax.dynamic_slice_in_dim(keys_all, first, size, 0)
        values_part = lax.dynamic_slice_in_dim(values_all, first, size, 0)

        def compute(current):
            probs, grad_scores, keys_four = block_grads(
                queries, query_block, grad_ctx, delta, log_total, keys_part, values_part, first
            )
            return current + contract("shqk,kshd->qshd", grad_scores, keys_four)

        return lax.cond(
            first // BLOCK <= jnp.max(query_block), compute, lambda current: current, accum
        )

    return lax.fori_loop(0, length // size, step, jnp.zeros(queries.shape, jnp.float32))


def query_side_fold(keys_local, values_local, key_start, accum, pieces, start):
    queries_all, grad_all, delta_all, log_all = pieces
    length = queries_all.shape[0]
    size = math.gcd(length, 512)

    def step(index, current):
        first = index * size
        queries_part = lax.dynamic_slice_in_dim(queries_all, first, size, 0)
        grad_part = lax.dynamic_slice_in_dim(grad_all, first, size, 0)
        delta_part = jnp.transpose(lax.dynamic_slice_in_dim(delta_all, first, size, 0), (1, 2, 0))
        log_part = jnp.transpose(lax.dynamic_slice_in_dim(log_all, first, size, 0), (1, 2, 0))
        block_rows = (first + jnp.arange(size)) // BLOCK

        def compute(inner):
            return inner + key_value_terms(
                queries_part,
                block_rows,
                grad_part,
                delta_part,
                log_part,
                keys_local,
                values_local,
                key_start,
            )

        return lax.cond(
            jnp.max(block_rows) >= key_start // BLOCK, compute, lambda inner: inner, current
        )

    return lax.fori_loop(0, length // size, step, accum)


def reduce_experts(gate_grad, up_grad, down_grad):
    return (
        lax.psum_scatter(gate_grad, ("dp", "context"), scatter_dimension=1, tiled=True),
        lax.psum_scatter(up_grad, ("dp", "context"), scatter_dimension=1, tiled=True),
        lax.psum_scatter(down_grad, ("dp", "context"), scatter_dimension=1, tiled=True),
    )


def on_device(
    tokens,
    norm1_gain,
    qkv_weight,
    out_weight,
    norm2_gain,
    router_weight,
    expert_gate,
    expert_up,
    expert_down,
    shared_gate,
    shared_up,
    shared_down,
    routes,
    cotangent,
):
    seqs, span, width = tokens.shape
    heads = width // HEAD_DIM
    rows = seqs * span
    local = jnp.swapaxes(tokens, 0, 1).reshape(rows, width).astype(jnp.float32)
    key_start = lax.axis_index("context") * span
    positions = key_start + jnp.arange(span)
    query_block = positions // BLOCK
    cosine, sine = rotation(positions, HEAD_DIM)
    normed_one, factor_one = normalize(local)
    entry_one = (normed_one * norm1_gain).astype(jnp.bfloat16)
    projected = matmul(entry_one, qkv_weight).reshape(span, seqs, 3, heads, HEAD_DIM)
    queries = rotate(projected[:, :, 0], cosine, sine).astype(jnp.bfloat16)
    keys_local = (
        rotate(projected[:, :, 1], cosine, sine).astype(jnp.bfloat16).reshape(span, seqs, width)
    )
    values_local = projected[:, :, 2].astype(jnp.bfloat16).reshape(span, seqs, width)
    start_state = (
        jnp.full((seqs, heads, span), masked_score, jnp.float32),
        jnp.zeros((seqs, heads, span), jnp.float32),
        jnp.zeros((seqs, heads, span, HEAD_DIM), jnp.float32),
    )
    best, total, accum = fold_keys(
        queries,
        query_block,
        start_state,
        (
            lax.all_gather(keys_local, "context", axis=0, tiled=True),
            lax.all_gather(values_local, "context", axis=0, tiled=True),
        ),
    )
    context = jnp.transpose(accum / total[..., None], (2, 0, 1, 3))
    log_total = best + jnp.log(total)
    context_low = context.astype(jnp.bfloat16).reshape(rows, width)
    middle = local + matmul(context_low, out_weight)
    normed_two, factor_two = normalize(middle)
    entry_two = (normed_two * norm2_gain).astype(jnp.bfloat16)
    logits = matmul(entry_two, router_weight)
    total_experts = router_weight.shape[1]
    topk = routes.shape[-1]
    capacity = rows * topk * 5 // (4 * total_experts)
    route_rows = jnp.swapaxes(routes[0], 0, 1).reshape(rows, topk)
    chosen = route_rows[:, :, None] == jnp.arange(total_experts)[None, None, :]
    chosen_float = chosen.astype(jnp.float32)
    picked = jnp.sum(chosen_float * logits[:, None, :], axis=-1)
    picked = picked - jnp.max(picked, axis=-1, keepdims=True)
    raised = jnp.exp(picked)
    gates = raised / jnp.sum(raised, axis=-1, keepdims=True)
    counts = jnp.sum(chosen.astype(jnp.int32), axis=1)
    before = jnp.cumsum(counts, axis=0) - counts
    slots = jnp.sum(chosen.astype(jnp.int32) * before[:, None, :], axis=-1)
    targets = route_rows * capacity + slots
    placing = (
        jnp.transpose(targets)[:, :, None] == jnp.arange(total_experts * capacity)[None, None, :]
    ).astype(jnp.bfloat16)
    dispatch_hot = jnp.sum(placing, axis=0)
    buffer = (
        contract("mr,md->rd", dispatch_hot, entry_two)
        .astype(jnp.bfloat16)
        .reshape(total_experts, capacity, width)
    )
    received = lax.all_to_all(buffer, "experts", split_axis=0, concat_axis=1, tiled=True)
    gate_part = contract("erd,edf->erf", received, expert_gate)
    up_part = contract("erd,edf->erf", received, expert_up)
    hidden = (gate_part * jax.nn.sigmoid(gate_part) * up_part).astype(jnp.bfloat16)
    produced = contract("erf,efd->erd", hidden, expert_down).astype(jnp.bfloat16)
    shared_gate_part = matmul(entry_two, shared_gate)
    shared_up_part = matmul(entry_two, shared_up)
    shared_hidden = (shared_gate_part * jax.nn.sigmoid(shared_gate_part) * shared_up_part).astype(
        jnp.bfloat16
    )
    shared_out = matmul(shared_hidden, shared_down)
    returned = lax.all_to_all(produced, "experts", split_axis=1, concat_axis=0, tiled=True).reshape(
        total_experts * capacity, width
    )
    picked_rows = contract("kmr,rd->kmd", placing, returned)
    mixed = jnp.sum(jnp.transpose(gates)[:, :, None] * picked_rows, axis=0)
    result = (middle + mixed + shared_out).astype(jnp.bfloat16)
    output = jnp.swapaxes(result.reshape(span, seqs, width), 0, 1)
    grad_low = jnp.swapaxes(cotangent, 0, 1).reshape(rows, width)
    grad_out = grad_low.astype(jnp.float32)
    grad_gates = jnp.transpose(jnp.sum(picked_rows * grad_out[None], axis=-1))
    grad_rows = (jnp.transpose(gates)[:, :, None] * grad_out[None]).astype(jnp.bfloat16)
    grad_slots = (
        contract("kmr,kmd->rd", placing, grad_rows)
        .astype(jnp.bfloat16)
        .reshape(total_experts, capacity, width)
    )
    grad_produced = lax.all_to_all(grad_slots, "experts", split_axis=0, concat_axis=1, tiled=True)
    expert_down_term = contract("erf,erd->efd", hidden, grad_produced)
    grad_hidden = contract("erd,efd->erf", grad_produced, expert_down)
    grad_gate_part, grad_up_part = silu_back(grad_hidden, gate_part, up_part)
    expert_gate_term = contract("erd,erf->edf", received, grad_gate_part)
    expert_up_term = contract("erd,erf->edf", received, grad_up_part)
    grad_received = (
        contract("erf,edf->erd", grad_gate_part, expert_gate)
        + contract("erf,edf->erd", grad_up_part, expert_up)
    ).astype(jnp.bfloat16)
    expert_parts = None
    shared_down_term = contract("mf,md->fd", shared_hidden, grad_low)
    grad_shared_hidden = contract("md,fd->mf", grad_low, shared_down)
    grad_shared_gate, grad_shared_up = silu_back(
        grad_shared_hidden, shared_gate_part, shared_up_part
    )
    shared_gate_term = contract("md,mf->df", entry_two, grad_shared_gate)
    shared_up_term = contract("md,mf->df", entry_two, grad_shared_up)
    grad_entry_two = contract("mf,df->md", grad_shared_gate, shared_gate) + contract(
        "mf,df->md", grad_shared_up, shared_up
    )
    grad_pick = gates * (grad_gates - jnp.sum(gates * grad_gates, axis=-1, keepdims=True))
    grad_logits = jnp.sum(chosen_float * grad_pick[:, :, None], axis=1)
    router_term = jnp.einsum(
        "md,me->de", entry_two.astype(jnp.float32), grad_logits, precision=highest
    )
    grad_entry_two = grad_entry_two + jnp.einsum(
        "me,de->md", grad_logits, router_weight.astype(jnp.float32), precision=highest
    )
    grad_returned = lax.all_to_all(
        grad_received, "experts", split_axis=1, concat_axis=0, tiled=True
    ).reshape(total_experts * capacity, width)
    grad_entry_two = grad_entry_two + contract("mr,rd->md", dispatch_hot, grad_returned)
    grad_middle_norm, norm2_term = norm_back(grad_entry_two, normed_two, factor_two, norm2_gain)
    grad_middle = grad_out + grad_middle_norm
    grad_attn = grad_middle.astype(jnp.bfloat16)
    out_term = contract("md,me->de", context_low, grad_attn)
    grad_ctx = (
        contract("me,de->md", grad_attn, out_weight)
        .astype(jnp.bfloat16)
        .reshape(span, seqs, heads, HEAD_DIM)
    )
    delta = jnp.transpose(jnp.sum(grad_ctx.astype(jnp.float32) * context, axis=-1), (1, 2, 0))
    keys_all, values_all = (
        lax.all_gather(keys_local, "context", axis=0, tiled=True),
        lax.all_gather(values_local, "context", axis=0, tiled=True),
    )
    grad_queries = query_grads(
        queries, query_block, grad_ctx, delta, log_total, keys_all, values_all
    ) * HEAD_DIM ** (-0.5)
    delta_rows = jnp.transpose(delta, (2, 0, 1))
    log_rows = jnp.transpose(log_total, (2, 0, 1))
    pull_step = partial(query_side_fold, keys_local, values_local, key_start)
    empty_grads = jnp.zeros((span, seqs, 2 * width), jnp.float32)
    grad_kv = pull_step(
        empty_grads,
        (
            lax.all_gather(queries, "context", axis=0, tiled=True),
            lax.all_gather(grad_ctx, "context", axis=0, tiled=True),
            lax.all_gather(delta_rows.astype(jnp.bfloat16), "context", axis=0, tiled=True).astype(
                jnp.float32
            ),
            lax.all_gather(log_rows.astype(jnp.bfloat16), "context", axis=0, tiled=True).astype(
                jnp.float32
            ),
        ),
        jnp.int32(0),
    )
    grad_keys = grad_kv[..., :width].reshape(span, seqs, heads, HEAD_DIM)
    grad_values = grad_kv[..., width:].reshape(span, seqs, heads, HEAD_DIM)
    grad_projected = jnp.stack(
        [
            rotate_back(grad_queries, cosine, sine),
            rotate_back(grad_keys, cosine, sine),
            grad_values,
        ],
        axis=2,
    )
    grad_projected = grad_projected.astype(jnp.bfloat16).reshape(rows, 3 * width)
    qkv_term = contract("md,me->de", entry_one, grad_projected)
    grad_entry_one = contract("me,de->md", grad_projected, qkv_weight)
    grad_local_norm, norm1_term = norm_back(grad_entry_one, normed_one, factor_one, norm1_gain)
    input_grad = jnp.swapaxes((grad_middle + grad_local_norm).reshape(span, seqs, width), 0, 1)
    expert_parts = reduce_experts(expert_gate_term, expert_up_term, expert_down_term)
    spread = (
        lax.psum_scatter(norm1_term, ("dp", "context"), scatter_dimension=0, tiled=True),
        lax.psum_scatter(qkv_term, ("dp", "context"), scatter_dimension=0, tiled=True),
        lax.psum_scatter(out_term, ("dp", "context"), scatter_dimension=0, tiled=True),
        lax.psum_scatter(norm2_term, ("dp", "context"), scatter_dimension=0, tiled=True),
        lax.psum_scatter(router_term, ("dp", "context"), scatter_dimension=0, tiled=True),
        lax.psum_scatter(shared_gate_term, ("dp", "context"), scatter_dimension=0, tiled=True),
        lax.psum_scatter(shared_up_term, ("dp", "context"), scatter_dimension=0, tiled=True),
        lax.psum_scatter(shared_down_term, ("dp", "context"), scatter_dimension=0, tiled=True),
    )
    (
        norm1_part,
        qkv_part,
        out_part,
        norm2_part,
        router_part,
        shared_gate_piece,
        shared_up_piece,
        shared_down_piece,
    ) = spread
    summed = (
        lax.psum(norm1_part.astype(jnp.bfloat16), "experts").astype(jnp.float32),
        lax.psum(qkv_part.astype(jnp.bfloat16), "experts").astype(jnp.float32),
        lax.psum(out_part.astype(jnp.bfloat16), "experts").astype(jnp.float32),
        lax.psum(norm2_part.astype(jnp.bfloat16), "experts").astype(jnp.float32),
        lax.psum(router_part.astype(jnp.bfloat16), "experts").astype(jnp.float32),
        lax.psum(shared_gate_piece.astype(jnp.bfloat16), "experts").astype(jnp.float32),
        lax.psum(shared_up_piece.astype(jnp.bfloat16), "experts").astype(jnp.float32),
        lax.psum(shared_down_piece.astype(jnp.bfloat16), "experts").astype(jnp.float32),
    )
    return (
        output,
        input_grad,
        summed[0],
        summed[1],
        summed[2],
        summed[3],
        summed[4],
        expert_parts[0],
        expert_parts[1],
        expert_parts[2],
        summed[5],
        summed[6],
        summed[7],
    )


group = ("dp", "experts")
keep_masks = (0, 1, 4, 5)
all_masks = keep_masks + tuple(mask ^ 2 for mask in keep_masks)
f32 = jnp.float32
bf16 = jnp.bfloat16


def dot_nn(left, right):
    return lax.dot_general(left, right, (((1,), (0,)), ((), ())), preferred_element_type=f32)


def dot_nt(left, right):
    return lax.dot_general(left, right, (((1,), (1,)), ((), ())), preferred_element_type=f32)


def dot_tn(left, right):
    return lax.dot_general(left, right, (((0,), (0,)), ((), ())), preferred_element_type=f32)


def spin(field, cosine, sine_up, sine_down):
    up = pltpu.roll(field, 32, 1)
    down = pltpu.roll(field, 96, 1)
    return field * cosine + up * sine_up + down * sine_down


def spin_back(grad, cosine, sine_up, sine_down):
    up = pltpu.roll(grad, 32, 1)
    down = pltpu.roll(grad, 96, 1)
    return grad * cosine - up * sine_up - down * sine_down


def lane_half(rows):
    return lax.broadcasted_iota(jnp.int32, (rows, 128), 1) // HEAD_DIM


def attend_kernel(
    blocks, place, *refs
):
    tokens = refs[:blocks]
    (gain1, qkv_w, out_w, gain2, cos, sin_up, sin_down) = refs[blocks:blocks + 7]
    (entry, queries, keys, values, log_total, context, middle, entry_two) = refs[blocks + 7:]
    rows, width = middle.shape
    pairs = width // 128
    here = place[0]

    for r in range(blocks):
        x = tokens[r][...].astype(f32)
        factor = lax.rsqrt(jnp.mean(x * x, axis=-1, keepdims=True) + norm_eps)
        entry[r] = (x * factor * gain1[...]).astype(bf16)

    def project(pair, carry):
        lanes = pl.ds(pl.multiple_of(pair * 128, 128), 128)
        key_lanes = pl.ds(pl.multiple_of(width + pair * 128, 128), 128)
        value_lanes = pl.ds(pl.multiple_of(2 * width + pair * 128, 128), 128)
        part = dot_nn(entry[0], qkv_w[:, lanes])
        queries[:, lanes] = spin(part, cos[0], sin_up[0], sin_down[0]).astype(bf16)
        for r in range(blocks):
            part = dot_nn(entry[r], qkv_w[:, key_lanes])
            keys[r, :, lanes] = spin(part, cos[r], sin_up[r], sin_down[r]).astype(bf16)
            values[r, :, lanes] = dot_nn(entry[r], qkv_w[:, value_lanes]).astype(bf16)
        return carry

    lax.fori_loop(0, pairs, project, 0)
    half = lane_half(rows)

    def attend(pair, carry):
        lanes = pl.ds(pl.multiple_of(pair * 128, 128), 128)
        both = queries[:, lanes]
        outs, logs = [], []
        for head in range(2):
            query = jnp.where(half == head, both, jnp.zeros_like(both))
            scores = []
            for r in range(blocks):
                bias = jnp.where(here >= r, 0.0, masked_score)
                scores.append(dot_nt(query, keys[r, :, lanes]) * HEAD_DIM ** (-0.5) + bias)
            best = jnp.max(scores[0], axis=-1, keepdims=True)
            for r in range(1, blocks):
                best = jnp.maximum(best, jnp.max(scores[r], axis=-1, keepdims=True))
            total = jnp.zeros_like(best)
            accum = jnp.zeros((rows, 128), f32)
            for r in range(blocks):
                weights = jnp.exp(scores[r] - best)
                total = total + jnp.sum(weights, axis=-1, keepdims=True)
                accum = accum + dot_nn(weights.astype(bf16), values[r, :, lanes])
            outs.append(accum / total)
            logs.append(best + jnp.log(total))
        context[:, lanes] = jnp.where(half == 0, outs[0], outs[1]).astype(bf16)
        log_total[pair] = jnp.where(half == 0, logs[0], logs[1])
        return carry

    lax.fori_loop(0, pairs, attend, 0)
    mid = tokens[0][...].astype(f32) + dot_nn(context[...], out_w[...])
    middle[...] = mid
    factor = lax.rsqrt(jnp.mean(mid * mid, axis=-1, keepdims=True) + norm_eps)
    entry_two[...] = (mid * factor * gain2[...]).astype(bf16)


def silu_parts(gate_part, up_part):
    sigmoid_value = jax.nn.sigmoid(gate_part)
    active = gate_part * sigmoid_value
    return sigmoid_value, active, (active * up_part).astype(bf16)


def silu_grads(grad_hidden, gate_part, up_part, sigmoid_value, active):
    grad_gate = grad_hidden * up_part * sigmoid_value * (1.0 + gate_part * (1.0 - sigmoid_value))
    return grad_gate.astype(bf16), (grad_hidden * active).astype(bf16)


def expert_chunk(x_all, dz_all, x_t, dz_t, gate_w, up_w, down_w, produced, received, scratch, first):
    hidden_s, dgate_s, dup_s = scratch
    tile = 320
    tiles = x_all.shape[0] // tile

    def step(index, carry):
        rows = pl.ds(pl.multiple_of(index * tile, tile), tile)
        x = x_all[rows, :]
        dz = dz_all[rows, :]
        gate_part = dot_nn(x, gate_w[0])
        up_part = dot_nn(x, up_w[0])
        sigmoid_value, active, hidden = silu_parts(gate_part, up_part)
        out = dot_nn(hidden, down_w[0])
        grad_hidden = dot_nt(dz, down_w[0])
        dgate, dup = silu_grads(grad_hidden, gate_part, up_part, sigmoid_value, active)
        grad = dot_nt(dgate, gate_w[0]) + dot_nt(dup, up_w[0])
        if first:
            produced[rows, :] = out
            received[rows, :] = grad
        else:
            produced[rows, :] = produced[rows, :] + out
            received[rows, :] = received[rows, :] + grad
        hidden_s[rows, :] = hidden
        dgate_s[rows, :] = dgate
        dup_s[rows, :] = dup
        return carry

    lax.fori_loop(0, tiles, step, 0)


def store_expert_grads(bundle, base, span_rows, lane_blocks, dp, n_dp, n_context, x_t, dz_t, scratch):
    hidden_s, dgate_s, dup_s = scratch
    width = x_t.shape[0]
    block = width // n_dp
    piece = block // n_context
    per_place = 2 * lane_blocks * piece

    def one(part, carry):
        rows = pl.ds(pl.multiple_of(part * block, 16), block)
        slab = lax.bitwise_xor(part, dp) * per_place
        for mat, source in enumerate((dgate_s, dup_s)):
            grad = dot_nn(x_t[rows, :], source[...]).astype(bf16)
            for z in range(n_context):
                for lane in range(lane_blocks):
                    start = base + z * span_rows + slab + (mat * lane_blocks + lane) * piece
                    bundle[pl.ds(pl.multiple_of(start, 16), piece), :] = grad[
                        z * piece:(z + 1) * piece, lane * 128:(lane + 1) * 128
                    ]
        grad = dot_nn(dz_t[rows, :], hidden_s[...]).astype(bf16)
        for z in range(n_context):
            start = base + z * span_rows + n_dp * per_place + part * block
            bundle[pl.ds(pl.multiple_of(start, 16), block), :] = grad[:, z * 128:(z + 1) * 128]
        return carry

    lax.fori_loop(0, n_dp, one, 0)


def feed_kernel(n_context, place, *refs):
    inputs = refs[:8]
    (cot, hot, chosen, router, gate_s_w, up_s_w, down_s_w, gate_w, up_w, down_w) = refs[8:18]
    (shared_bundle, expert_bundle, x_all, dz_all, g_all, aux, mixed, grad_in, produced, received) = refs[18:28]
    (field, x_t, dz_t, hidden_s, dgate_s, dup_s, acc_gate, acc_up, acc_down) = refs[28:]
    index, dp, expert = place[0], place[1], place[2]
    rows, width = inputs[0].shape
    slots = hot.shape[1]
    n_dp = 4
    lanes = lax.broadcasted_iota(jnp.int32, (slots, 128), 1)
    mine = (lanes == expert).astype(f32)

    for m in range(8):
        field[m] = inputs[m][...]

    def gather(step, carry):
        mask = jnp.where(step < 4, 0, 2) + jnp.bitwise_and(step, 1) + jnp.where(jnp.bitwise_and(step, 2) > 0, 4, 0)
        source = lax.bitwise_xor(index, mask)
        place_hot = hot[source]
        span_rows = pl.ds(pl.multiple_of(step * slots, 16), slots)
        x = dot_nn(place_hot, field[step]).astype(bf16)
        x_all[span_rows, :] = x
        g_slot = dot_nn(place_hot, cot[source, :, :width])
        which = dot_nn(place_hot, chosen[source])
        logits = dot_nn(x, router[...])
        total = jnp.sum(which * logits, axis=-1, keepdims=True)
        own = jnp.sum(mine * which * logits, axis=-1, keepdims=True)
        gate = jax.nn.sigmoid(2.0 * own - total)
        dz_all[span_rows, :] = (gate * g_slot).astype(bf16)
        g_all[span_rows, :] = g_slot.astype(bf16)
        aux[span_rows, :] = jnp.where(
            lanes == 64, gate, gate * (1.0 - gate) * which * (2.0 * mine - 1.0)
        )
        return carry

    lax.fori_loop(0, 8, gather, 0)
    x_t[...] = x_all[...].T
    dz_t[...] = dz_all[...].T

    scratch = (hidden_s, dgate_s, dup_s)
    expert_chunk(x_all, dz_all, x_t, dz_t, gate_w, up_w, down_w, produced, received, scratch, True)
    columns = gate_w.shape[2]
    block = width // n_dp
    piece = block // n_context
    per_place = 2 * (columns // 128) * piece
    store_expert_grads(
        expert_bundle, 0, n_dp * per_place + width, columns // 128, dp, n_dp, n_context, x_t, dz_t, scratch
    )

    acc_gate[...] = jnp.zeros_like(acc_gate)
    acc_up[...] = jnp.zeros_like(acc_up)
    acc_down[...] = jnp.zeros_like(acc_down)

    def shared(step, carry):
        mask = jnp.where(step < 4, 0, 2) + jnp.bitwise_and(step, 1) + jnp.where(jnp.bitwise_and(step, 2) > 0, 4, 0)
        source = lax.bitwise_xor(index, mask)
        h = field[step]
        g = cot[source, :, :width]
        gate_part = dot_nn(h, gate_s_w[...])
        up_part = dot_nn(h, up_s_w[...])
        sigmoid_value, active, hidden = silu_parts(gate_part, up_part)
        mixed[step] = dot_nn(hidden, down_s_w[...]).astype(bf16)
        grad_hidden = dot_nt(g, down_s_w[...])
        dgate, dup = silu_grads(grad_hidden, gate_part, up_part, sigmoid_value, active)
        grad_in[step] = (dot_nt(dgate, gate_s_w[...]) + dot_nt(dup, up_s_w[...])).astype(bf16)
        acc_gate[...] += dot_tn(h, dgate)
        acc_up[...] += dot_tn(h, dup)
        acc_down[...] += dot_tn(hidden, g)
        return carry

    lax.fori_loop(0, 8, shared, 0)
    columns = gate_s_w.shape[1]
    lane_blocks = columns // 128
    per_place = 2 * lane_blocks * piece
    down_rows = columns // n_context
    total_rows = n_dp * per_place + down_rows * (width // 128)
    for part in range(n_dp):
        slab = lax.bitwise_xor(part, dp) * per_place
        for mat, source in enumerate((acc_gate, acc_up)):
            for z in range(n_context):
                for lane in range(lane_blocks):
                    start = z * total_rows + slab + (mat * lane_blocks + lane) * piece
                    shared_bundle[pl.ds(pl.multiple_of(start, 16), piece), :] = source[
                        part * block + z * piece:part * block + (z + 1) * piece, lane * 128:(lane + 1) * 128
                    ].astype(bf16)
    for z in range(n_context):
        for lane in range(width // 128):
            start = z * total_rows + n_dp * per_place + lane * down_rows
            shared_bundle[start:start + down_rows, :] = acc_down[
                z * down_rows:(z + 1) * down_rows, lane * 128:(lane + 1) * 128
            ].astype(bf16)


def finish_kernel(n_context, place, *refs):
    (x_all, dz_all, g_all, aux, hot_t, router_t, gate_w, up_w, down_w, mixed, grad_in, produced0, received0) = refs[:13]
    (expert_bundle, grad_keep, grad_send, mix_keep, mix_send, router_grad) = refs[13:19]
    (x_t, dz_t, hidden_s, dgate_s, dup_s, produced, received) = refs[19:]
    index, dp = place[0], place[1]
    width = x_all.shape[1]
    slots = hot_t.shape[2]
    n_dp = 4
    x_t[...] = x_all[...].T
    dz_t[...] = dz_all[...].T
    produced[...] = produced0[...]
    received[...] = received0[...]
    scratch = (hidden_s, dgate_s, dup_s)
    expert_chunk(x_all, dz_all, x_t, dz_t, gate_w, up_w, down_w, produced, received, scratch, False)
    columns = gate_w.shape[2]
    block = width // n_dp
    piece = block // n_context
    per_place = 2 * (columns // 128) * piece
    store_expert_grads(
        expert_bundle, 0, n_dp * per_place + width, columns // 128, dp, n_dp, n_context, x_t, dz_t, scratch
    )
    lanes = lax.broadcasted_iota(jnp.int32, (slots, 128), 1)
    router_grad[...] = jnp.zeros_like(router_grad)

    def back(step, carry):
        mask = jnp.where(step < 4, 0, 2) + jnp.bitwise_and(step, 1) + jnp.where(jnp.bitwise_and(step, 2) > 0, 4, 0)
        source = lax.bitwise_xor(index, mask)
        rows = pl.ds(pl.multiple_of(step * slots, 16), slots)
        z = produced[rows, :]
        extra = aux[rows, :]
        gate = extra[:, 64:65]
        pick = jnp.sum(z.astype(bf16).astype(f32) * g_all[rows, :].astype(f32), axis=-1, keepdims=True)
        dlogits = (jnp.where(lanes < 64, extra, 0.0) * pick).astype(bf16)
        grad = (received[rows, :] + dot_nn(dlogits, router_t[...])).astype(bf16)
        router_grad[...] += dot_tn(x_all[rows, :], dlogits)
        back_hot = hot_t[source]
        grad_tokens = (grad_in[step].astype(f32) + dot_nn(back_hot, grad)).astype(bf16)
        mix_tokens = (mixed[step].astype(f32) + dot_nn(back_hot, (gate * z).astype(bf16))).astype(bf16)

        @pl.when(step < 4)
        def _():
            grad_keep[step] = grad_tokens
            mix_keep[step] = mix_tokens

        @pl.when(step >= 4)
        def _():
            grad_send[step - 4] = grad_tokens
            mix_send[step - 4] = mix_tokens

        return carry

    lax.fori_loop(0, 8, back, 0)


def back_kernel(blocks, n_dp, place, *refs):
    tokens = refs[:blocks]
    parts = refs[blocks:blocks + 4]
    (
        middle, cot, entry, queries, keys, values, log_total, context, qkv_w, out_w, gain1, gain2, cos, sin_up, sin_down, router_grad,
    ) = refs[blocks + 4:blocks + 20]
    outs = refs[blocks + 20:]
    (grad_own, grad_middle) = outs[:2]
    grad_far = outs[2:blocks + 1]
    (keep, send) = outs[blocks + 1:blocks + 3]
    (grad_ctx, grad_q, grad_kv, entry_t, notes) = outs[blocks + 3:]
    rows, width = middle.shape
    pairs = width // 128
    here, dp, side = place[0], place[1], place[2]
    scale = HEAD_DIM ** (-0.5)

    grad_two = parts[0][...].astype(f32)
    for part in parts[1:]:
        grad_two = grad_two + part[...].astype(f32)
    mid = middle[...]
    factor = lax.rsqrt(jnp.mean(mid * mid, axis=-1, keepdims=True) + norm_eps)
    normed = mid * factor
    notes[0:1, :] = jnp.sum(grad_two * normed, axis=0, keepdims=True)
    grad_norm = grad_two * gain2[...]
    inner = jnp.mean(grad_norm * normed, axis=-1, keepdims=True)
    grad_mid = cot[...].astype(f32) + factor * (grad_norm - normed * inner)
    grad_middle[...] = grad_mid
    grad_attn = grad_mid.astype(bf16)
    grad_ctx[...] = dot_nt(grad_attn, out_w[...]).astype(bf16)
    half = lane_half(rows)

    def store(value, mat_start):
        n_half = keep.shape[-1]
        block = width // n_dp
        for part in range(n_dp):
            piece = value[part * block:(part + 1) * block, :].astype(bf16)
            flip_core = lax.bitwise_and(lax.bitwise_xor(part, dp), 1)
            flip_chip = lax.bitwise_xor(part, dp) // 2
            side_of = mat_start // n_half
            start = mat_start - side_of * n_half
            flip_side = lax.bitwise_xor(side_of, side)
            lanes = slice(start, start + piece.shape[1])

            @pl.when(flip_core == 0)
            def _():
                keep[flip_chip, flip_side, :, lanes] = piece

            @pl.when(flip_core == 1)
            def _():
                send[flip_chip, flip_side, :, lanes] = piece

    def attend(pair, carry):
        lanes = pl.ds(pl.multiple_of(pair * 128, 128), 128)
        both_q = queries[:, lanes]
        both_g = grad_ctx[:, lanes]
        both_l = log_total[pair]
        dq = jnp.zeros((rows, 128), f32)
        dk = [jnp.zeros((rows, 128), f32) for _ in range(blocks)]
        dv = [jnp.zeros((rows, 128), f32) for _ in range(blocks)]
        for head in range(2):
            query = jnp.where(half == head, both_q, jnp.zeros_like(both_q))
            grad = jnp.where(half == head, both_g, jnp.zeros_like(both_g))
            log_row = both_l[:, head * HEAD_DIM:head * HEAD_DIM + 1]
            probs, grads = [], []
            delta = jnp.zeros((rows, 1), f32)
            for r in range(blocks):
                bias = jnp.where(here >= r, 0.0, masked_score)
                scores = dot_nt(query, keys[r, :, lanes]) * scale + bias
                prob = jnp.exp(scores - log_row)
                grad_prob = dot_nt(grad, values[r, :, lanes])
                delta = delta + jnp.sum(prob * grad_prob, axis=-1, keepdims=True)
                probs.append(prob)
                grads.append(grad_prob)
            dq_head = jnp.zeros((rows, 128), f32)
            for r in range(blocks):
                grad_score = (probs[r] * (grads[r] - delta)).astype(bf16)
                dq_head = dq_head + dot_nn(grad_score, keys[r, :, lanes])
                dk[r] = dk[r] + dot_tn(grad_score, query)
                dv[r] = dv[r] + dot_tn(probs[r].astype(bf16), grad)
            dq = dq + jnp.where(half == head, dq_head, 0.0)
        grad_q[:, lanes] = spin_back(dq * scale, cos[0], sin_up[0], sin_down[0]).astype(bf16)
        far_lanes = pl.ds(pl.multiple_of(width + pair * 128, 128), 128)
        for r in range(blocks):
            grad_kv[r * rows:(r + 1) * rows, lanes] = spin_back(
                dk[r] * scale, cos[r], sin_up[r], sin_down[r]
            ).astype(bf16)
            grad_kv[r * rows:(r + 1) * rows, far_lanes] = dv[r].astype(bf16)
        return carry

    lax.fori_loop(0, pairs, attend, 0)

    for r in range(blocks):
        entry_t[:, r * rows:(r + 1) * rows] = entry[r].T
    tile = 384
    for start in range(0, width, tile):
        store(dot_nn(entry_t[:, :rows], grad_q[:, start:start + tile]), start)
    for start in range(0, 2 * width, tile):
        value = dot_nn(entry_t[...], grad_kv[:, start:start + tile])
        begin = width + start
        n_half = keep.shape[-1]
        if begin < n_half < begin + tile:
            store(value[:, :n_half - begin], begin)
            store(value[:, n_half - begin:], n_half)
        else:
            store(value, begin)
    context_t = context[...].T
    for start in range(0, width, tile):
        store(dot_nn(context_t, grad_attn[:, start:start + tile]), 3 * width + start)

    total = jnp.zeros((1, width), f32)
    for r in range(blocks):
        grad_entry = dot_nt(grad_kv[r * rows:(r + 1) * rows, :], qkv_w[:, width:])
        if r == 0:
            grad_entry = grad_entry + dot_nt(grad_q[...], qkv_w[:, :width])
            grad_own[...] = grad_entry
        else:
            grad_far[r - 1][...] = grad_entry.astype(bf16)
        x = tokens[r][...].astype(f32)
        factor = lax.rsqrt(jnp.mean(x * x, axis=-1, keepdims=True) + norm_eps)
        total = total + jnp.sum(grad_entry * (x * factor), axis=0, keepdims=True)
    notes[1:2, :] = total
    notes_t = notes[...].T
    lane = lax.broadcasted_iota(jnp.int32, (width, 128), 1)
    small = router_grad[...] + jnp.where(lane == 8, notes_t[:, 0:1], 0.0) + jnp.where(
        lane == 9, notes_t[:, 1:2], 0.0
    )
    store(small, 4 * width)
    store(jnp.zeros((width, 128), f32), 4 * width + 128)


def call(kernel, outs, scratch, scalars, operands, specs=None, limit=60):
    whole = pl.BlockSpec(memory_space=pltpu.VMEM)
    if specs is None:
        specs = [whole] * len(operands)
    return pl.pallas_call(
        kernel,
        grid_spec=pltpu.PrefetchScalarGridSpec(
            num_scalar_prefetch=1,
            grid=(1,),
            in_specs=specs,
            out_specs=[whole] * len(outs),
            scratch_shapes=scratch,
        ),
        out_shape=[jax.ShapeDtypeStruct(*out) for out in outs],
        compiler_params=pltpu.CompilerParams(vmem_limit_bytes=limit * 2**20),
    )(scalars, *operands)


def swap(value, mask):
    return lax.ppermute(value, group, [(i, i ^ mask) for i in range(8)])


def on_block(
    n_context,
    tokens,
    norm1_gain,
    qkv_weight,
    out_weight,
    norm2_gain,
    router_weight,
    expert_gate,
    expert_up,
    expert_down,
    shared_gate,
    shared_up,
    shared_down,
    routes,
    cotangent,
):
    rows, width = tokens.shape[1:]
    hidden = shared_gate.shape[1]
    n_experts = router_weight.shape[1]
    blocks = n_context
    n_dp = 4
    slots = rows * routes.shape[-1] * 5 // (4 * n_experts)
    dp = lax.axis_index("dp")
    here = lax.axis_index("context")
    side = lax.axis_index("experts")
    core, chip = dp % 2, dp // 2
    index = dp * 2 + side
    expert = 2 * side + core
    pairs = width // 128

    own = tokens[0]
    cot = cotangent[0]
    field = [own] + [
        lax.ppermute(own, "context", [(i, i + r) for i in range(n_context - r)]) for r in range(1, blocks)
    ]
    route_rows = routes[0, 0]
    carried = jnp.concatenate(
        [cot, jnp.pad(route_rows.astype(bf16), ((0, 0), (0, 126)))], axis=1
    )
    cot_all = lax.all_gather(carried, group, axis=0)

    positions = (here - jnp.arange(blocks)[:, None]) * rows + jnp.arange(rows)[None, :]
    lane = jnp.arange(128)
    freqs = 10000.0 ** (-2.0 * (lane % 32).astype(f32) / HEAD_DIM)
    angles = positions.astype(f32)[:, :, None] * freqs
    cos, sin = jnp.cos(angles), jnp.sin(angles)
    second = (lane % HEAD_DIM) >= 32
    sin_up, sin_down = jnp.where(second, sin, 0.0), jnp.where(second, 0.0, -sin)
    gain1, gain2 = norm1_gain[None, :], norm2_gain[None, :]

    quarter = hidden // n_dp

    def pick_columns(weight):
        part = lax.dynamic_slice_in_dim(weight, dp * quarter, quarter, 1)
        part = part.reshape(width, n_context, 2, quarter // (2 * n_context))
        return jnp.where(side == 0, part[:, :, 0], part[:, :, 1]).reshape(width, quarter // 2)

    gate_s, up_s = pick_columns(shared_gate), pick_columns(shared_up)
    down_s = lax.dynamic_slice_in_dim(shared_down, dp * quarter, quarter, 0).reshape(
        n_context, 2, quarter // (2 * n_context), width
    )
    down_s = jnp.where(side == 0, down_s[:, 0], down_s[:, 1]).reshape(quarter // 2, width)
    router = jnp.pad(router_weight, ((0, 0), (0, 128 - n_experts)))

    act = (rows, width)
    wide = (blocks, rows, width)
    entry, queries, keys, values, log_total, context, middle, entry_two = call(
        partial(attend_kernel, blocks),
        [
            (wide, bf16), (act, bf16), (wide, bf16), (wide, bf16), ((pairs, rows, 128), f32),
            (act, bf16), (act, f32), (act, bf16),
        ],
        [],
        jnp.stack([here]),
        [*field, gain1, qkv_weight, out_weight, gain2, cos, sin_up, sin_down],
    )

    across = [swap(entry_two, mask) for mask in keep_masks[1:]]
    near = [entry_two, *across]
    others = [swap(value, 2) for value in near]

    route_all = cot_all[:, :, width:width + 2].astype(jnp.int32)
    ids = jnp.arange(128)
    chosen_all = (route_all[:, :, :1] == ids) | (route_all[:, :, 1:] == ids)
    named = (route_all == expert).any(-1)
    slot = jnp.cumsum(named.astype(jnp.int32), axis=1) - 1
    slot = jnp.where(named, slot, -1)
    hot = (slot[:, None, :] == jnp.arange(slots)[None, :, None]).astype(bf16)
    hot_t = (slot[:, :, None] == jnp.arange(slots)[None, None, :]).astype(bf16)

    scalars = jnp.stack([index, dp, expert, core, chip])
    half_columns = hidden // 4
    n_slots = 8 * slots

    def expert_specs(chunk):
        up = pl.BlockSpec((1, width, half_columns), lambda i, s: (s[3], 0, 2 * s[4] + chunk))
        down = pl.BlockSpec((1, half_columns, width), lambda i, s: (s[3], 2 * s[4] + chunk, 0))
        return [up, up, down]

    whole = pl.BlockSpec(memory_space=pltpu.VMEM)
    piece = width // n_dp // n_context
    expert_place = 2 * (half_columns // 128) * piece
    expert_rows = n_dp * expert_place + width
    shared_columns = hidden // 8
    shared_place = 2 * (shared_columns // 128) * piece
    down_rows = shared_columns // n_context
    shared_rows = n_dp * shared_place + down_rows * (width // 128)
    slot_act = (n_slots, width)
    eight = (8, rows, width)
    scratch = [
        pltpu.VMEM((width, n_slots), bf16),
        pltpu.VMEM((width, n_slots), bf16),
        pltpu.VMEM((n_slots, half_columns), bf16),
        pltpu.VMEM((n_slots, half_columns), bf16),
        pltpu.VMEM((n_slots, half_columns), bf16),
    ]
    (
        shared_bundle, bundle0, x_all, dz_all, g_all, aux, mixed, grad_in, produced, received,
    ) = call(
        partial(feed_kernel, n_context),
        [
            ((n_context * shared_rows, 128), bf16), ((n_context * expert_rows, 128), bf16),
            (slot_act, bf16), (slot_act, bf16), (slot_act, bf16), ((n_slots, 128), f32),
            (eight, bf16), (eight, bf16), (slot_act, f32), (slot_act, f32),
        ],
        [
            pltpu.VMEM(eight, bf16), *scratch,
            pltpu.VMEM((width, shared_columns), f32), pltpu.VMEM((width, shared_columns), f32),
            pltpu.VMEM((shared_columns, width), f32),
        ],
        scalars,
        [*near, *others, cot_all, hot, chosen_all.astype(bf16), router, gate_s, up_s, down_s,
         expert_gate, expert_up, expert_down],
        [whole] * 15 + expert_specs(0),
    )

    def reduce_context(value):
        return lax.psum_scatter(value, "context", scatter_dimension=0, tiled=True)

    expert_sum0 = reduce_context(bundle0)
    shared_sum = reduce_context(shared_bundle)
    four = (4, rows, width)
    bundle1, grad_keep, grad_send, mix_keep, mix_send, router_grad = call(
        partial(finish_kernel, n_context),
        [
            ((n_context * expert_rows, 128), bf16), (four, bf16), (four, bf16), (four, bf16), (four, bf16),
            ((width, 128), f32),
        ],
        [*scratch, pltpu.VMEM(slot_act, f32), pltpu.VMEM(slot_act, f32)],
        scalars,
        [x_all, dz_all, g_all, aux, hot_t, router.T, expert_gate, expert_up, expert_down, mixed, grad_in,
         produced, received],
        [whole] * 6 + expert_specs(1) + [whole] * 4,
    )
    expert_sum1 = reduce_context(bundle1)

    def give_back(kept, sent):
        other = swap(sent, 2)
        sums = [(kept[k].astype(f32) + other[k].astype(f32)).astype(bf16) for k in range(4)]
        return [sums[0]] + [swap(sums[k], keep_masks[k]) for k in range(1, 4)]

    parts = give_back(grad_keep, grad_send)
    mix_parts = give_back(mix_keep, mix_send)

    columns = 4 * width + 256
    pack = (2, 2, width // n_dp, columns // 2)
    results = call(
        partial(back_kernel, blocks, n_dp),
        [(act, f32), (act, f32)] + [(act, bf16)] * (blocks - 1) + [(pack, bf16), (pack, bf16)],
        [
            pltpu.VMEM(act, bf16), pltpu.VMEM(act, bf16), pltpu.VMEM((blocks * rows, 2 * width), bf16),
            pltpu.VMEM((width, blocks * rows), bf16), pltpu.VMEM((8, width), f32),
        ],
        jnp.stack([here, dp, side]),
        [*field, *parts, middle, cot, entry, queries, keys, values, log_total, context, qkv_weight, out_weight,
         gain1, gain2, cos, sin_up, sin_down, router_grad],
    )
    grad_own, grad_middle = results[:2]
    grad_far = results[2:blocks + 1]
    keep, send = results[blocks + 1:]

    other = swap(send, 2)
    sums = {
        (i, j): (keep[i, j].astype(f32) + other[i, j].astype(f32)).astype(bf16)
        for i in range(2) for j in range(2)
    }
    arrived = [sums[0, 0], swap(sums[0, 1], 1), swap(sums[1, 0], 4), swap(sums[1, 1], 5)]
    summed = sum(value.astype(f32) for value in arrived).astype(bf16)
    spread = lax.all_to_all(summed, "context", split_axis=0, concat_axis=0, tiled=True)
    spread = spread.reshape(n_context, piece, columns // 2).astype(f32).sum(0).astype(bf16)
    far = swap(spread, 1)
    first = jnp.where(side == 0, spread, far)
    last = jnp.where(side == 0, far, spread)
    copied = jnp.concatenate([first, last], axis=1).astype(f32)
    qkv_grad = copied[:, :3 * width]
    out_grad = copied[:, 3 * width:4 * width]
    router_out = copied[:, 4 * width:4 * width + n_experts]
    norm2_grad = copied[:, 4 * width + 8]
    norm1_grad = copied[:, 4 * width + 9]

    pulled = [
        lax.ppermute(grad_far[r - 1], "context", [(i, i - r) for i in range(r, n_context)])
        for r in range(1, blocks)
    ]
    local = own.astype(f32)
    normed_one, factor_one = normalize(local)
    grad_entry = grad_own + sum(value.astype(f32) for value in pulled)
    grad_local, _ = norm_back(grad_entry, normed_one, factor_one, norm1_gain)
    input_grad = (grad_middle + grad_local)[None]

    output = (middle + sum(value.astype(f32) for value in mix_parts)).astype(bf16)[None]

    def deal(value, per_place):
        slabs = value[:n_dp * per_place].reshape(n_dp, per_place, 128)
        got = [slabs[0]] + [
            lax.ppermute(slabs[m], "dp", [(i, i ^ m) for i in range(n_dp)]) for m in range(1, n_dp)
        ]
        ordered = jnp.stack(got)
        return ordered, value[n_dp * per_place:]

    def in_order(ordered):
        return [lax.dynamic_index_in_dim(ordered, lax.bitwise_xor(dp, i), 0, False) for i in range(n_dp)]

    def by_lanes(value, count):
        return value.reshape(count, piece, 128).transpose(1, 0, 2).reshape(piece, count * 128)

    lane_blocks = half_columns // 128
    gates, ups, downs = [[], []], [[], []], []
    for value in (expert_sum0, expert_sum1):
        ordered, down = deal(value, expert_place)
        slabs = in_order(ordered)
        for e in range(2):
            for mats, start in ((gates, 0), (ups, lane_blocks * piece)):
                mats[e].append(
                    [by_lanes(slabs[2 * half + e][start:start + lane_blocks * piece], lane_blocks) for half in range(2)]
                )
        downs.append(down)

    def join(parts):
        return jnp.concatenate([parts[chunk][half] for half in range(2) for chunk in range(2)], axis=1)

    expert_gate_grad = jnp.stack([join(gates[e]) for e in range(2)]).astype(f32)
    expert_up_grad = jnp.stack([join(ups[e]) for e in range(2)]).astype(f32)
    kept_down = jnp.where(core == 0, downs[0], downs[1])
    sent_down = jnp.where(core == 0, downs[1], downs[0])
    got_down = lax.ppermute(sent_down, "dp", [(i, i ^ 1) for i in range(n_dp)])
    expert_down_grad = jnp.where(
        core == 0, jnp.stack([kept_down, got_down]), jnp.stack([got_down, kept_down])
    ).astype(f32).transpose(0, 2, 1)

    ordered, down = deal(shared_sum, shared_place)
    mats = jnp.concatenate(in_order(ordered), axis=0)
    both = jnp.concatenate([mats, down], axis=0)
    far = swap(both, 1)
    pair = jnp.where(side == 0, jnp.stack([both, far]), jnp.stack([far, both]))
    n_mats = mats.shape[0]
    shared_blocks = shared_columns // 128
    table = pair[:, :n_mats].reshape(2, n_dp, 2, shared_blocks, piece, 128)
    table = table.transpose(2, 4, 1, 3, 5, 0).reshape(2, piece, n_dp, shared_columns, 2)
    table = table.reshape(2, piece, n_dp, n_context, shared_columns // n_context, 2).swapaxes(-1, -2)
    table = table.reshape(2, piece, hidden).astype(f32)
    shared_down_grad = (
        pair[:, n_mats:].reshape(2, width // 128, down_rows, 128).transpose(0, 2, 1, 3).reshape(2 * down_rows, width)
    ).astype(f32)

    return (
        output, input_grad, norm1_grad, qkv_grad, out_grad, norm2_grad, router_out,
        expert_gate_grad, expert_up_grad, expert_down_grad, table[0], table[1], shared_down_grad,
    )


def on_any(mesh, *args):
    tokens, router_weight, expert_gate, shared_gate = args[0], args[5], args[6], args[9]
    sizes = dict(mesh.shape)
    fits = (
        sizes["dp"] == 4
        and sizes["experts"] == 2
        and tokens.shape[0] == 1
        and tokens.shape[1] == BLOCK
        and expert_gate.shape[0] == 2
        and tokens.shape[2] % 128 == 0
        and tokens.shape[2] // sizes["dp"] % (16 * sizes["context"]) == 0
        and shared_gate.shape[1] % (1024) == 0
        and sizes["context"] == 4
    )
    if fits:
        return on_block(sizes["context"], *args)
    return on_device(*args)


def solution(mesh):
    return jax.shard_map(
        partial(on_any, mesh),
        mesh=mesh,
        in_specs=(
            P(("dp", "experts"), "context", None),
            P(),
            P(),
            P(),
            P(),
            P(),
            P("experts", None, None),
            P("experts", None, None),
            P("experts", None, None),
            P(),
            P(),
            P(),
            P("context", ("dp", "experts"), None, None),
            P(("dp", "experts"), "context", None),
        ),
        out_specs=(
            P(("dp", "experts"), "context", None),
            P(("dp", "experts"), "context", None),
            P(("dp", "context")),
            P(("dp", "context"), None),
            P(("dp", "context"), None),
            P(("dp", "context")),
            P(("dp", "context"), None),
            P("experts", ("dp", "context"), None),
            P("experts", ("dp", "context"), None),
            P("experts", ("dp", "context"), None),
            P(("dp", "context"), None),
            P(("dp", "context"), None),
            P(("dp", "context"), None),
        ),
        check_vma=False,
    )
```

```python
from functools import partial
import math

import jax
import jax.numpy as jnp
import numpy as np
from jax import lax
from jax.experimental import pallas as pl
from jax.experimental.pallas import tpu as pltpu
from jax.sharding import PartitionSpec as P

HEAD_DIM = 64
BLOCK = 256
DP, CONTEXT, EXPERTS = "dp", "context", "experts"


norm_eps = 1e-05
masked_score = -1e30
highest = lax.Precision.HIGHEST


def matmul(left, right):
    return jnp.dot(left, right, preferred_element_type=jnp.float32)


def contract(spec, left, right):
    return jnp.einsum(spec, left, right, preferred_element_type=jnp.float32)


def normalize(field):
    factor = lax.rsqrt(jnp.mean(field * field, axis=-1, keepdims=True) + norm_eps)
    return (field * factor, factor)


def norm_back(grad_out, normed, factor, gain):
    grad_norm = grad_out * gain
    inner = jnp.mean(grad_norm * normed, axis=-1, keepdims=True)
    return (factor * (grad_norm - normed * inner), jnp.sum(grad_out * normed, axis=0))


def rotation(positions, head_dim):
    half = head_dim // 2
    freqs = 10000.0 ** (-2.0 * jnp.arange(half, dtype=jnp.float32) / head_dim)
    angles = positions.astype(jnp.float32)[:, None] * freqs[None, :]
    return (jnp.cos(angles)[:, None, None, :], jnp.sin(angles)[:, None, None, :])


def rotate(field, cosine, sine):
    half = field.shape[-1] // 2
    first = field[..., :half]
    second = field[..., half:]
    return jnp.concatenate(
        [first * cosine - second * sine, second * cosine + first * sine], axis=-1
    )


def rotate_back(grad, cosine, sine):
    half = grad.shape[-1] // 2
    first = grad[..., :half]
    second = grad[..., half:]
    return jnp.concatenate(
        [first * cosine + second * sine, second * cosine - first * sine], axis=-1
    )


def silu_back(grad_hidden, gate_part, up_part):
    sigmoid_value = jax.nn.sigmoid(gate_part)
    active = gate_part * sigmoid_value
    grad_gate = grad_hidden * up_part * sigmoid_value * (1.0 + gate_part * (1.0 - sigmoid_value))
    grad_up = grad_hidden * active
    return (grad_gate.astype(jnp.bfloat16), grad_up.astype(jnp.bfloat16))


def score_block(queries, keys_part, query_block, start):
    size = keys_part.shape[0]
    seqs, heads, head_dim = (queries.shape[1], queries.shape[2], queries.shape[3])
    keys_four = keys_part.reshape(size, seqs, heads, head_dim)
    scores = contract("qshd,kshd->shqk", queries, keys_four) * head_dim ** (-0.5)
    key_block = (start + jnp.arange(size)) // BLOCK
    visible = key_block[None, :] <= query_block[:, None]
    return (jnp.where(visible, scores, masked_score), visible, keys_four)


def attend_piece(queries, query_block, state, keys_part, values_part, start):
    size = keys_part.shape[0]
    seqs, heads, head_dim = (queries.shape[1], queries.shape[2], queries.shape[3])

    def compute(current):
        best, total, accum = current
        scores, visible, keys_four = score_block(queries, keys_part, query_block, start)
        new_best = jnp.maximum(best, jnp.max(scores, axis=-1))
        weights = jnp.where(visible, jnp.exp(scores - new_best[..., None]), 0.0)
        factor = jnp.exp(best - new_best)
        values_four = values_part.reshape(size, seqs, heads, head_dim)
        total = total * factor + jnp.sum(weights, axis=-1)
        accum = accum * factor[..., None] + contract(
            "shqk,kshd->shqd", weights.astype(jnp.bfloat16), values_four
        )
        return (new_best, total, accum)

    needed = start // BLOCK <= jnp.max(query_block)
    return lax.cond(needed, compute, lambda current: current, state)


def fold_keys(queries, query_block, state, pieces):
    keys_all, values_all = pieces
    length = keys_all.shape[0]
    size = math.gcd(length, 512)

    def step(index, current):
        first = index * size
        keys_part = lax.dynamic_slice_in_dim(keys_all, first, size, 0)
        values_part = lax.dynamic_slice_in_dim(values_all, first, size, 0)
        return attend_piece(queries, query_block, current, keys_part, values_part, first)

    return lax.fori_loop(0, length // size, step, state)


def block_grads(queries, query_block, grad_ctx, delta, log_total, keys_part, values_part, start):
    size = keys_part.shape[0]
    seqs, heads, head_dim = (queries.shape[1], queries.shape[2], queries.shape[3])
    scores, visible, keys_four = score_block(queries, keys_part, query_block, start)
    probs = jnp.where(visible, jnp.exp(scores - log_total[..., None]), 0.0)
    values_four = values_part.reshape(size, seqs, heads, head_dim)
    grad_probs = contract("qshd,kshd->shqk", grad_ctx, values_four)
    grad_scores = (probs * (grad_probs - delta[..., None])).astype(jnp.bfloat16)
    return (probs, grad_scores, keys_four)


def key_value_terms(
    queries, query_block, grad_ctx, delta, log_total, keys_part, values_part, start
):
    size = keys_part.shape[0]
    seqs, heads, head_dim = (queries.shape[1], queries.shape[2], queries.shape[3])
    width = heads * head_dim
    probs, grad_scores, keys_four = block_grads(
        queries, query_block, grad_ctx, delta, log_total, keys_part, values_part, start
    )
    grad_values = contract("shqk,qshd->kshd", probs.astype(jnp.bfloat16), grad_ctx)
    grad_keys = contract("shqk,qshd->kshd", grad_scores, queries) * head_dim ** (-0.5)
    return jnp.concatenate(
        [grad_keys.reshape(size, seqs, width), grad_values.reshape(size, seqs, width)], axis=-1
    )


def query_grads(queries, query_block, grad_ctx, delta, log_total, keys_all, values_all):
    length = keys_all.shape[0]
    size = math.gcd(length, 512)

    def step(index, accum):
        first = index * size
        keys_part = lax.dynamic_slice_in_dim(keys_all, first, size, 0)
        values_part = lax.dynamic_slice_in_dim(values_all, first, size, 0)

        def compute(current):
            probs, grad_scores, keys_four = block_grads(
                queries, query_block, grad_ctx, delta, log_total, keys_part, values_part, first
            )
            return current + contract("shqk,kshd->qshd", grad_scores, keys_four)

        return lax.cond(
            first // BLOCK <= jnp.max(query_block), compute, lambda current: current, accum
        )

    return lax.fori_loop(0, length // size, step, jnp.zeros(queries.shape, jnp.float32))


def query_side_fold(keys_local, values_local, key_start, accum, pieces, start):
    queries_all, grad_all, delta_all, log_all = pieces
    length = queries_all.shape[0]
    size = math.gcd(length, 512)

    def step(index, current):
        first = index * size
        queries_part = lax.dynamic_slice_in_dim(queries_all, first, size, 0)
        grad_part = lax.dynamic_slice_in_dim(grad_all, first, size, 0)
        delta_part = jnp.transpose(lax.dynamic_slice_in_dim(delta_all, first, size, 0), (1, 2, 0))
        log_part = jnp.transpose(lax.dynamic_slice_in_dim(log_all, first, size, 0), (1, 2, 0))
        block_rows = (first + jnp.arange(size)) // BLOCK

        def compute(inner):
            return inner + key_value_terms(
                queries_part,
                block_rows,
                grad_part,
                delta_part,
                log_part,
                keys_local,
                values_local,
                key_start,
            )

        return lax.cond(
            jnp.max(block_rows) >= key_start // BLOCK, compute, lambda inner: inner, current
        )

    return lax.fori_loop(0, length // size, step, accum)


def reduce_experts(gate_grad, up_grad, down_grad):
    return (
        lax.psum_scatter(gate_grad, (DP, CONTEXT), scatter_dimension=1, tiled=True),
        lax.psum_scatter(up_grad, (DP, CONTEXT), scatter_dimension=1, tiled=True),
        lax.psum_scatter(down_grad, (DP, CONTEXT), scatter_dimension=1, tiled=True),
    )


def on_device(
    tokens,
    norm1_gain,
    qkv_weight,
    out_weight,
    norm2_gain,
    router_weight,
    expert_gate,
    expert_up,
    expert_down,
    shared_gate,
    shared_up,
    shared_down,
    routes,
    cotangent,
):
    seqs, span, width = tokens.shape
    heads = width // HEAD_DIM
    rows = seqs * span
    local = jnp.swapaxes(tokens, 0, 1).reshape(rows, width).astype(jnp.float32)
    key_start = lax.axis_index(CONTEXT) * span
    positions = key_start + jnp.arange(span)
    query_block = positions // BLOCK
    cosine, sine = rotation(positions, HEAD_DIM)
    normed_one, factor_one = normalize(local)
    entry_one = (normed_one * norm1_gain).astype(jnp.bfloat16)
    projected = matmul(entry_one, qkv_weight).reshape(span, seqs, 3, heads, HEAD_DIM)
    queries = rotate(projected[:, :, 0], cosine, sine).astype(jnp.bfloat16)
    keys_local = (
        rotate(projected[:, :, 1], cosine, sine).astype(jnp.bfloat16).reshape(span, seqs, width)
    )
    values_local = projected[:, :, 2].astype(jnp.bfloat16).reshape(span, seqs, width)
    start_state = (
        jnp.full((seqs, heads, span), masked_score, jnp.float32),
        jnp.zeros((seqs, heads, span), jnp.float32),
        jnp.zeros((seqs, heads, span, HEAD_DIM), jnp.float32),
    )
    best, total, accum = fold_keys(
        queries,
        query_block,
        start_state,
        (
            lax.all_gather(keys_local, CONTEXT, axis=0, tiled=True),
            lax.all_gather(values_local, CONTEXT, axis=0, tiled=True),
        ),
    )
    context = jnp.transpose(accum / total[..., None], (2, 0, 1, 3))
    log_total = best + jnp.log(total)
    context_low = context.astype(jnp.bfloat16).reshape(rows, width)
    middle = local + matmul(context_low, out_weight)
    normed_two, factor_two = normalize(middle)
    entry_two = (normed_two * norm2_gain).astype(jnp.bfloat16)
    logits = matmul(entry_two, router_weight)
    total_experts = router_weight.shape[1]
    topk = routes.shape[-1]
    capacity = rows * topk * 5 // (4 * total_experts)
    route_rows = jnp.swapaxes(routes[0], 0, 1).reshape(rows, topk)
    chosen = route_rows[:, :, None] == jnp.arange(total_experts)[None, None, :]
    chosen_float = chosen.astype(jnp.float32)
    picked = jnp.sum(chosen_float * logits[:, None, :], axis=-1)
    picked = picked - jnp.max(picked, axis=-1, keepdims=True)
    raised = jnp.exp(picked)
    gates = raised / jnp.sum(raised, axis=-1, keepdims=True)
    counts = jnp.sum(chosen.astype(jnp.int32), axis=1)
    before = jnp.cumsum(counts, axis=0) - counts
    slots = jnp.sum(chosen.astype(jnp.int32) * before[:, None, :], axis=-1)
    targets = route_rows * capacity + slots
    placing = (
        jnp.transpose(targets)[:, :, None] == jnp.arange(total_experts * capacity)[None, None, :]
    ).astype(jnp.bfloat16)
    dispatch_hot = jnp.sum(placing, axis=0)
    buffer = (
        contract("mr,md->rd", dispatch_hot, entry_two)
        .astype(jnp.bfloat16)
        .reshape(total_experts, capacity, width)
    )
    received = lax.all_to_all(buffer, EXPERTS, split_axis=0, concat_axis=1, tiled=True)
    gate_part = contract("erd,edf->erf", received, expert_gate)
    up_part = contract("erd,edf->erf", received, expert_up)
    hidden = (gate_part * jax.nn.sigmoid(gate_part) * up_part).astype(jnp.bfloat16)
    produced = contract("erf,efd->erd", hidden, expert_down).astype(jnp.bfloat16)
    shared_gate_part = matmul(entry_two, shared_gate)
    shared_up_part = matmul(entry_two, shared_up)
    shared_hidden = (shared_gate_part * jax.nn.sigmoid(shared_gate_part) * shared_up_part).astype(
        jnp.bfloat16
    )
    shared_out = matmul(shared_hidden, shared_down)
    returned = lax.all_to_all(produced, EXPERTS, split_axis=1, concat_axis=0, tiled=True).reshape(
        total_experts * capacity, width
    )
    picked_rows = contract("kmr,rd->kmd", placing, returned)
    mixed = jnp.sum(jnp.transpose(gates)[:, :, None] * picked_rows, axis=0)
    result = (middle + mixed + shared_out).astype(jnp.bfloat16)
    output = jnp.swapaxes(result.reshape(span, seqs, width), 0, 1)
    grad_low = jnp.swapaxes(cotangent, 0, 1).reshape(rows, width)
    grad_out = grad_low.astype(jnp.float32)
    grad_gates = jnp.transpose(jnp.sum(picked_rows * grad_out[None], axis=-1))
    grad_rows = (jnp.transpose(gates)[:, :, None] * grad_out[None]).astype(jnp.bfloat16)
    grad_slots = (
        contract("kmr,kmd->rd", placing, grad_rows)
        .astype(jnp.bfloat16)
        .reshape(total_experts, capacity, width)
    )
    grad_produced = lax.all_to_all(grad_slots, EXPERTS, split_axis=0, concat_axis=1, tiled=True)
    expert_down_term = contract("erf,erd->efd", hidden, grad_produced)
    grad_hidden = contract("erd,efd->erf", grad_produced, expert_down)
    grad_gate_part, grad_up_part = silu_back(grad_hidden, gate_part, up_part)
    expert_gate_term = contract("erd,erf->edf", received, grad_gate_part)
    expert_up_term = contract("erd,erf->edf", received, grad_up_part)
    grad_received = (
        contract("erf,edf->erd", grad_gate_part, expert_gate)
        + contract("erf,edf->erd", grad_up_part, expert_up)
    ).astype(jnp.bfloat16)
    expert_parts = None
    shared_down_term = contract("mf,md->fd", shared_hidden, grad_low)
    grad_shared_hidden = contract("md,fd->mf", grad_low, shared_down)
    grad_shared_gate, grad_shared_up = silu_back(
        grad_shared_hidden, shared_gate_part, shared_up_part
    )
    shared_gate_term = contract("md,mf->df", entry_two, grad_shared_gate)
    shared_up_term = contract("md,mf->df", entry_two, grad_shared_up)
    grad_entry_two = contract("mf,df->md", grad_shared_gate, shared_gate) + contract(
        "mf,df->md", grad_shared_up, shared_up
    )
    grad_pick = gates * (grad_gates - jnp.sum(gates * grad_gates, axis=-1, keepdims=True))
    grad_logits = jnp.sum(chosen_float * grad_pick[:, :, None], axis=1)
    router_term = jnp.einsum(
        "md,me->de", entry_two.astype(jnp.float32), grad_logits, precision=highest
    )
    grad_entry_two = grad_entry_two + jnp.einsum(
        "me,de->md", grad_logits, router_weight.astype(jnp.float32), precision=highest
    )
    grad_returned = lax.all_to_all(
        grad_received, EXPERTS, split_axis=1, concat_axis=0, tiled=True
    ).reshape(total_experts * capacity, width)
    grad_entry_two = grad_entry_two + contract("mr,rd->md", dispatch_hot, grad_returned)
    grad_middle_norm, norm2_term = norm_back(grad_entry_two, normed_two, factor_two, norm2_gain)
    grad_middle = grad_out + grad_middle_norm
    grad_attn = grad_middle.astype(jnp.bfloat16)
    out_term = contract("md,me->de", context_low, grad_attn)
    grad_ctx = (
        contract("me,de->md", grad_attn, out_weight)
        .astype(jnp.bfloat16)
        .reshape(span, seqs, heads, HEAD_DIM)
    )
    delta = jnp.transpose(jnp.sum(grad_ctx.astype(jnp.float32) * context, axis=-1), (1, 2, 0))
    keys_all, values_all = (
        lax.all_gather(keys_local, CONTEXT, axis=0, tiled=True),
        lax.all_gather(values_local, CONTEXT, axis=0, tiled=True),
    )
    grad_queries = query_grads(
        queries, query_block, grad_ctx, delta, log_total, keys_all, values_all
    ) * HEAD_DIM ** (-0.5)
    delta_rows = jnp.transpose(delta, (2, 0, 1))
    log_rows = jnp.transpose(log_total, (2, 0, 1))
    pull_step = partial(query_side_fold, keys_local, values_local, key_start)
    empty_grads = jnp.zeros((span, seqs, 2 * width), jnp.float32)
    grad_kv = pull_step(
        empty_grads,
        (
            lax.all_gather(queries, CONTEXT, axis=0, tiled=True),
            lax.all_gather(grad_ctx, CONTEXT, axis=0, tiled=True),
            lax.all_gather(delta_rows.astype(jnp.bfloat16), CONTEXT, axis=0, tiled=True).astype(
                jnp.float32
            ),
            lax.all_gather(log_rows.astype(jnp.bfloat16), CONTEXT, axis=0, tiled=True).astype(
                jnp.float32
            ),
        ),
        jnp.int32(0),
    )
    grad_keys = grad_kv[..., :width].reshape(span, seqs, heads, HEAD_DIM)
    grad_values = grad_kv[..., width:].reshape(span, seqs, heads, HEAD_DIM)
    grad_projected = jnp.stack(
        [
            rotate_back(grad_queries, cosine, sine),
            rotate_back(grad_keys, cosine, sine),
            grad_values,
        ],
        axis=2,
    )
    grad_projected = grad_projected.astype(jnp.bfloat16).reshape(rows, 3 * width)
    qkv_term = contract("md,me->de", entry_one, grad_projected)
    grad_entry_one = contract("me,de->md", grad_projected, qkv_weight)
    grad_local_norm, norm1_term = norm_back(grad_entry_one, normed_one, factor_one, norm1_gain)
    input_grad = jnp.swapaxes((grad_middle + grad_local_norm).reshape(span, seqs, width), 0, 1)
    expert_parts = reduce_experts(expert_gate_term, expert_up_term, expert_down_term)
    spread = (
        lax.psum_scatter(norm1_term, (DP, CONTEXT), scatter_dimension=0, tiled=True),
        lax.psum_scatter(qkv_term, (DP, CONTEXT), scatter_dimension=0, tiled=True),
        lax.psum_scatter(out_term, (DP, CONTEXT), scatter_dimension=0, tiled=True),
        lax.psum_scatter(norm2_term, (DP, CONTEXT), scatter_dimension=0, tiled=True),
        lax.psum_scatter(router_term, (DP, CONTEXT), scatter_dimension=0, tiled=True),
        lax.psum_scatter(shared_gate_term, (DP, CONTEXT), scatter_dimension=0, tiled=True),
        lax.psum_scatter(shared_up_term, (DP, CONTEXT), scatter_dimension=0, tiled=True),
        lax.psum_scatter(shared_down_term, (DP, CONTEXT), scatter_dimension=0, tiled=True),
    )
    (
        norm1_part,
        qkv_part,
        out_part,
        norm2_part,
        router_part,
        shared_gate_piece,
        shared_up_piece,
        shared_down_piece,
    ) = spread
    summed = (
        lax.psum(norm1_part.astype(jnp.bfloat16), EXPERTS).astype(jnp.float32),
        lax.psum(qkv_part.astype(jnp.bfloat16), EXPERTS).astype(jnp.float32),
        lax.psum(out_part.astype(jnp.bfloat16), EXPERTS).astype(jnp.float32),
        lax.psum(norm2_part.astype(jnp.bfloat16), EXPERTS).astype(jnp.float32),
        lax.psum(router_part.astype(jnp.bfloat16), EXPERTS).astype(jnp.float32),
        lax.psum(shared_gate_piece.astype(jnp.bfloat16), EXPERTS).astype(jnp.float32),
        lax.psum(shared_up_piece.astype(jnp.bfloat16), EXPERTS).astype(jnp.float32),
        lax.psum(shared_down_piece.astype(jnp.bfloat16), EXPERTS).astype(jnp.float32),
    )
    return (
        output,
        input_grad,
        summed[0],
        summed[1],
        summed[2],
        summed[3],
        summed[4],
        expert_parts[0],
        expert_parts[1],
        expert_parts[2],
        summed[5],
        summed[6],
        summed[7],
    )


group = (DP, EXPERTS)
keep_masks = (0, 1, 4, 5)
all_masks = keep_masks + tuple(mask ^ 2 for mask in keep_masks)
f32 = jnp.float32
bf16 = jnp.bfloat16
far, copied, held = range(3)


def dot_nn(left, right):
    return lax.dot_general(left, right, (((1,), (0,)), ((), ())), preferred_element_type=f32)


def dot_nt(left, right):
    return lax.dot_general(left, right, (((1,), (1,)), ((), ())), preferred_element_type=f32)


def dot_tn(left, right):
    return lax.dot_general(left, right, (((0,), (0,)), ((), ())), preferred_element_type=f32)


def spin(field, cosine, sine_up, sine_down):
    up = pltpu.roll(field, 32, 1)
    down = pltpu.roll(field, 96, 1)
    return field * cosine + up * sine_up + down * sine_down


def spin_back(grad, cosine, sine_up, sine_down):
    up = pltpu.roll(grad, 32, 1)
    down = pltpu.roll(grad, 96, 1)
    return grad * cosine - up * sine_up - down * sine_down


def spin_tables(length):
    lane = np.arange(128)
    freqs = 10000.0 ** (-2.0 * (lane % 32) / HEAD_DIM)
    angles = np.arange(length)[:, None] * freqs[None, :]
    second = (lane % HEAD_DIM) >= HEAD_DIM // 2
    sine = np.sin(angles)
    tables = (np.cos(angles), np.where(second, sine, 0.0), np.where(second, 0.0, -sine))
    return [jnp.asarray(table, f32) for table in tables]


def lane_half(rows):
    return lax.broadcasted_iota(jnp.int32, (rows, 128), 1) // HEAD_DIM


def key_bias(blocks, rows, here):
    block = lax.broadcasted_iota(jnp.int32, (1, blocks * rows), 1) // rows
    return jnp.where(block <= here, 0.0, masked_score)


class Copies:
    def __init__(self, sems):
        self.sems, self.count = sems, 0

    def start(self, source, target):
        copy = pltpu.make_async_copy(source, target, self.sems.at[self.count])
        self.count += 1
        copy.start()
        return copy


def attend_kernel(blocks, place, *refs):
    tokens = refs[:blocks]
    (routes, gain1, qkv_w, out_w, gain2, cos_hbm, up_hbm, down_hbm) = refs[blocks:blocks + 8]
    (entry_hbm, queries_hbm, keys_hbm, values_hbm, log_hbm, context_hbm, middle, entry_two) = refs[
        blocks + 8:blocks + 16
    ]
    (cos, sin_up, sin_down, entry, queries, keys, values, log_total, context, sems) = refs[blocks + 16:]
    rows, width = middle.shape
    pairs = width // 128
    here = place[0]
    copies = Copies(sems)
    tables_in = []
    for r in range(blocks):
        block = pl.ds(pl.multiple_of(jnp.maximum(here - r, 0) * rows, rows), rows)
        for source, target in ((cos_hbm, cos), (up_hbm, sin_up), (down_hbm, sin_down)):
            tables_in.append(copies.start(source.at[block], target.at[r * rows:(r + 1) * rows]))

    for r in range(blocks):
        x = tokens[r][...].astype(f32)
        factor = lax.rsqrt(jnp.mean(x * x, axis=-1, keepdims=True) + norm_eps)
        entry[r * rows:(r + 1) * rows, :] = (x * factor * gain1[...]).astype(bf16)
    outs = [copies.start(entry, entry_hbm)]
    for copy in tables_in:
        copy.wait()

    tile = 384
    for start in range(0, width, tile):
        part = dot_nn(entry[:rows, :], qkv_w[:, start:start + tile])
        for lane in range(0, tile, 128):
            queries[:, start + lane:start + lane + 128] = spin(
                part[:, lane:lane + 128], cos[:rows, :], sin_up[:rows, :], sin_down[:rows, :]
            ).astype(bf16)
    for start in range(0, width, tile):
        part = dot_nn(entry[...], qkv_w[:, width + start:width + start + tile])
        for lane in range(0, tile, 128):
            keys[:, start + lane:start + lane + 128] = spin(
                part[:, lane:lane + 128], cos[...], sin_up[...], sin_down[...]
            ).astype(bf16)
        values[:, start:start + tile] = dot_nn(
            entry[...], qkv_w[:, 2 * width + start:2 * width + start + tile]
        ).astype(bf16)
    outs += [copies.start(queries, queries_hbm), copies.start(keys, keys_hbm), copies.start(values, values_hbm)]
    half = lane_half(rows)
    bias = key_bias(blocks, rows, here)

    def attend(pair, carry):
        lanes = pl.ds(pl.multiple_of(pair * 128, 128), 128)
        both = queries[:, lanes] * HEAD_DIM ** (-0.5)
        results, logs = [], []
        for head in range(2):
            query = jnp.where(half == head, both, jnp.zeros_like(both))
            scores = dot_nt(query, keys[:, lanes]) + bias
            best = jnp.max(scores, axis=-1, keepdims=True)
            weights = jnp.exp(scores - best)
            total = jnp.sum(weights, axis=-1, keepdims=True)
            results.append(dot_nn(weights.astype(bf16), values[:, lanes]) / total)
            logs.append(best + jnp.log(total))
        context[:, lanes] = jnp.where(half == 0, results[0], results[1]).astype(bf16)
        log_total[pair] = jnp.where(half == 0, logs[0], logs[1])
        return carry

    lax.fori_loop(0, pairs, attend, 0)
    outs += [copies.start(log_total, log_hbm), copies.start(context, context_hbm)]
    mid = tokens[0][...].astype(f32) + dot_nn(context[...], out_w[...])
    middle[...] = mid
    factor = lax.rsqrt(jnp.mean(mid * mid, axis=-1, keepdims=True) + norm_eps)
    entry_two[:rows, :] = (mid * factor * gain2[...]).astype(bf16)
    entry_two[rows:, :] = jnp.zeros((entry_two.shape[0] - rows, width), bf16)
    entry_two[rows:rows + 8, :rows] = jnp.concatenate(
        [routes[...].astype(f32), jnp.zeros((8 - routes.shape[0], rows), f32)], axis=0
    ).astype(bf16)
    for copy in outs:
        copy.wait()


def pick_kernel(n_context, place, gate, up, down, gate_out, up_out, down_out):
    side = place[5]
    lane = lax.broadcasted_iota(jnp.int32, (gate.shape[0], 128), 1)
    for source, target in ((gate, gate_out), (up, up_out)):
        for z in range(0, n_context, 2):
            one = source[:, z * 128:(z + 1) * 128].astype(f32)
            two = source[:, (z + 1) * 128:(z + 2) * 128].astype(f32)
            left = jnp.where(side == 0, one, pltpu.roll(one, 64, 1))
            right = jnp.where(side == 0, pltpu.roll(two, 64, 1), two)
            target[:, z * 64:z * 64 + 128] = jnp.where(lane < 64, left, right).astype(bf16)
    for z in range(n_context):
        start = pl.multiple_of(z * 128 + side * 64, 64)
        down_out[z * 64:(z + 1) * 64, :] = down[pl.ds(start, 64), :]


def sum_kernel(n_context, counts, place, *refs):
    outs = refs[-n_context:]
    here = place[6]
    piece = outs[0].shape[0]
    for r, out in enumerate(outs):
        block = lax.rem(here + r, n_context)
        rows = pl.ds(pl.multiple_of(block * piece, piece), piece)
        first, start = 0, 0
        for count in counts:
            total = refs[first][rows, :].astype(f32)
            for value in refs[first + 1:first + count]:
                total = total + value[rows, :].astype(f32)
            out[:, start:start + total.shape[1]] = total.astype(bf16)
            first, start = first + count, start + total.shape[1]


def silu_parts(gate_part, up_part):
    sigmoid_value = jax.nn.sigmoid(gate_part)
    active = gate_part * sigmoid_value
    return sigmoid_value, active, (active * up_part).astype(bf16)


def silu_grads(grad_hidden, gate_part, up_part, sigmoid_value, active):
    grad_gate = grad_hidden * up_part * sigmoid_value * (1.0 + gate_part * (1.0 - sigmoid_value))
    return grad_gate.astype(bf16), (grad_hidden * active).astype(bf16)


def run_through(x_all, dz_all, weights, produced, received, hidden, dgate, dup):
    gate_w, up_w, down_w = weights
    tile = x_all.shape[0] // 2
    for t in range(2):
        rows = slice(t * tile, (t + 1) * tile)
        gate_part = dot_nn(x_all[rows, :], gate_w[...])
        up_part = dot_nn(x_all[rows, :], up_w[...])
        sigmoid_value, active, u = silu_parts(gate_part, up_part)
        hidden[rows, :] = u
        out = dot_nn(u, down_w[...])
        grad_hidden = dot_nt(dz_all[rows, :], down_w[...])
        da, db = silu_grads(grad_hidden, gate_part, up_part, sigmoid_value, active)
        dgate[rows, :] = da
        dup[rows, :] = db
        grad = dot_nt(da, gate_w[...]) + dot_nt(db, up_w[...])
        produced[rows, :] = out.astype(produced.dtype)
        received[rows, :] = grad.astype(received.dtype)


def run_weights(copies, sources, targets, core, chip, run):
    gate_hbm, up_hbm, down_hbm = sources
    gate_w, up_w, down_w = targets
    columns = gate_w.shape[1]
    part = pl.ds(pl.multiple_of((2 * chip + run) * columns, columns), columns)
    return [
        copies.start(gate_hbm.at[core, :, part], gate_w),
        copies.start(up_hbm.at[core, :, part], up_w),
        copies.start(down_hbm.at[core, part, :], down_w),
    ]


def enter_kernel(masks, n_context, n_dp, layout, place, *refs):
    inputs = refs[:8]
    (cot_hbm, router, gate_hbm, up_hbm, down_hbm) = refs[8:13]
    outs_hbm, bundle = refs[13:17], refs[17]
    (aux, hots, produced, received) = kept = refs[18:22]
    (x_all, dz_all, field, cot, gate_w, up_w, down_w, hidden, dgate, dup, notes, sems) = refs[22:]
    index, dp, expert, core, chip = place[0], place[1], place[2], place[3], place[4]
    rows = cot.shape[0] // 8
    slots = hots.shape[1]
    copies = Copies(sems)
    ins = []
    for i in range(8):
        rows_of = slice(i * rows, (i + 1) * rows)
        ins.append((
            copies.start(inputs[i].at[rows:], notes.at[i]),
            copies.start(inputs[i].at[:rows], field.at[rows_of]),
            copies.start(cot_hbm.at[lax.bitwise_xor(index, masks[i])], cot.at[rows_of]),
        ))
    weights = (gate_w, up_w, down_w)
    weights_in = run_weights(copies, (gate_hbm, up_hbm, down_hbm), weights, core, chip, 0)

    lanes = lax.broadcasted_iota(jnp.int32, (slots, 128), 1)
    mine = (lanes == expert).astype(f32)
    expert_row = expert.astype(f32)
    before = (
        lax.broadcasted_iota(jnp.int32, (rows, rows), 0) < lax.broadcasted_iota(jnp.int32, (rows, rows), 1)
    ).astype(bf16)
    slot_of = lax.broadcasted_iota(jnp.int32, (slots, rows), 0).astype(f32)
    for i in range(8):
        rows_of = slice(i * rows, (i + 1) * rows)
        slots_of = slice(i * slots, (i + 1) * slots)
        if i % 4 == 0:
            for copy in sum(ins[i:i + 4], ()):
                copy.wait()
        routes = notes[i, :, :rows].astype(f32)
        first, second = routes[0:1, :], routes[1:2, :]
        named = jnp.logical_or(first == expert_row, second == expert_row).astype(f32)
        slot = dot_nn(jnp.broadcast_to(named, (16, rows)).astype(bf16), before)[0:1, :]
        hot_f = jnp.where(slot_of == slot, named, 0.0)
        partner = jnp.where(first == expert_row, second, first)
        other = jnp.sum(hot_f * partner, axis=-1, keepdims=True)
        hot = hot_f.astype(bf16)
        hots[i] = hot
        x = dot_nn(hot, field[rows_of, :]).astype(bf16)
        x_all[slots_of, :] = x
        g_slot = dot_nn(hot, cot[rows_of, :])
        logits = dot_nn(x, router[...])
        theirs = (lanes.astype(f32) == other).astype(f32)
        gate = jax.nn.sigmoid(jnp.sum((mine - theirs) * logits, axis=-1, keepdims=True))
        dz_all[slots_of, :] = (gate * g_slot).astype(bf16)
        aux[slots_of, :] = jnp.where(lanes == 64, gate, gate * (1.0 - gate) * (mine - theirs))
    outs = [copies.start(source, target) for source, target in zip(kept[:2], outs_hbm[:2])]

    for copy in weights_in:
        copy.wait()
    run_through(x_all, dz_all, weights, produced, received, hidden, dgate, dup)
    outs += [copies.start(source, target) for source, target in zip(kept[2:], outs_hbm[2:])]
    expert_grads(
        bundle, x_all, dz_all, hidden, dgate, dup, 0, n_dp * layout.run_place, layout.run_place, dp, n_context, n_dp
    )
    for copy in outs:
        copy.wait()


def leave_kernel(masks, n_context, n_dp, layout, place, *refs):
    kept_hbm, inputs, cot_hbm = refs[:4], refs[4:12], refs[12]
    (router_t, gate_s_hbm, up_s_hbm, down_s_hbm, gate_hbm, up_hbm, down_hbm) = refs[13:20]
    (grad_keep_hbm, grad_send_hbm, mix_keep_hbm, mix_send_hbm, router_grad, bundle) = refs[20:26]
    (aux, hots, produced0, received0) = kept = refs[26:30]
    (
        x_all, dz_all, g_all, produced, received, field, cot, gate_w, up_w, down_w, gate_s_w, up_s_w, down_s_w,
        hidden, dgate, dup, hidden_s, dgate_s, dup_s, grad_tokens, mix_tokens, slot_out, sems,
    ) = refs[30:]
    index, dp, core, chip = place[0], place[1], place[3], place[4]
    rows = cot.shape[0] // 8
    width = field.shape[1]
    slots = hots.shape[1]
    copies = Copies(sems)
    kept_in = [copies.start(source, target) for source, target in zip(kept_hbm[:2], kept[:2])]
    ins = []
    for i in range(8):
        rows_of = slice(i * rows, (i + 1) * rows)
        ins.append((
            copies.start(inputs[i].at[:rows], field.at[rows_of]),
            copies.start(cot_hbm.at[lax.bitwise_xor(index, masks[i])], cot.at[rows_of]),
        ))
    weights = (gate_w, up_w, down_w)
    weights_in = run_weights(copies, (gate_hbm, up_hbm, down_hbm), weights, core, chip, 1)
    shared_in = [
        copies.start(source, target)
        for source, target in (
            (gate_s_hbm, gate_s_w), (up_s_hbm, up_s_w), (down_s_hbm, down_s_w), *zip(kept_hbm[2:], kept[2:])
        )
    ]
    for copy in kept_in:
        copy.wait()
    for i in range(8):
        rows_of = slice(i * rows, (i + 1) * rows)
        slots_of = slice(i * slots, (i + 1) * slots)
        for copy in ins[i]:
            copy.wait()
        x_all[slots_of, :] = dot_nn(hots[i], field[rows_of, :]).astype(bf16)
        g_slot = dot_nn(hots[i], cot[rows_of, :])
        g_all[slots_of, :] = g_slot.astype(bf16)
        dz_all[slots_of, :] = (aux[slots_of, 64:65] * g_slot).astype(bf16)
    for copy in weights_in:
        copy.wait()
    run_through(x_all, dz_all, weights, produced, received, hidden, dgate, dup)

    for copy in shared_in:
        copy.wait()
    z = produced[...] + produced0[...].astype(f32)
    gate = aux[:, 64:65]
    pick = jnp.sum(z.astype(bf16).astype(f32) * g_all[...].astype(f32), axis=-1, keepdims=True)
    lanes = lax.broadcasted_iota(jnp.int32, aux.shape, 1)
    dlogits = (jnp.where(lanes < 64, aux[...], 0.0) * pick).astype(bf16)
    slot_out[:, width:] = (gate * z).astype(bf16)
    grad = received[...] + received0[...].astype(f32)
    slot_out[:, :width] = (grad + dot_nn(dlogits, router_t[...])).astype(bf16)
    router_grad[...] = dot_tn(x_all[...], dlogits)
    outs = []
    for t in range(4):
        tile = slice(2 * t * rows, 2 * (t + 1) * rows)
        gate_part = dot_nn(field[tile, :], gate_s_w[...])
        up_part = dot_nn(field[tile, :], up_s_w[...])
        sigmoid_value, active, u = silu_parts(gate_part, up_part)
        hidden_s[tile, :] = u
        mixed = dot_nn(u, down_s_w[...])
        grad_hidden = dot_nt(cot[tile, :], down_s_w[...])
        da, db = silu_grads(grad_hidden, gate_part, up_part, sigmoid_value, active)
        dgate_s[tile, :] = da
        dup_s[tile, :] = db
        grad_in = dot_nt(da, gate_s_w[...]) + dot_nt(db, up_s_w[...])
        for half in range(2):
            i = 2 * t + half
            rows_of = slice(half * rows, (half + 1) * rows)
            back = dot_tn(hots[i], slot_out[i * slots:(i + 1) * slots, :])
            grad_tokens[i] = (grad_in[rows_of, :] + back[:, :width]).astype(bf16)
            mix_tokens[i] = (mixed[rows_of, :] + back[:, width:]).astype(bf16)
        for i in (2 * t, 2 * t + 1):
            for source, targets in (
                (grad_tokens, (grad_keep_hbm, grad_send_hbm)), (mix_tokens, (mix_keep_hbm, mix_send_hbm))
            ):
                outs.append(copies.start(source.at[i], targets[i // 4].at[i % 4]))

    every = slice(None)
    shared_place, run_place = layout.shared_place, layout.run_place
    slab_rows = shared_place + run_place
    for mat, source in enumerate((dgate_s, dup_s)):
        offset = mat * layout.shared_blocks * layout.piece
        matrix_grads(bundle, field, source, offset, slab_rows, dp, n_context, n_dp)
    grad = dot_tn(hidden_s[...], cot[...]).astype(bf16)
    down_rows = layout.down_rows
    total_rows = bundle.shape[0] // n_context
    for z in range(n_context):
        for lane in range(width // 128):
            start = z * total_rows + n_dp * slab_rows + lane * down_rows
            bundle[start:start + down_rows, :] = grad[z * down_rows:(z + 1) * down_rows, lane * 128:(lane + 1) * 128]
    expert_grads(
        bundle, x_all, dz_all, hidden, dgate, dup, shared_place, total_rows - width, slab_rows, dp, n_context, n_dp
    )
    for copy in outs:
        copy.wait()


def store_grads(bundle, grad, part, offset, place_rows, dp, n_context, piece):
    total_rows = bundle.shape[0] // n_context
    slab = lax.bitwise_xor(part, dp) * place_rows
    for z in range(n_context):
        for lane in range(grad.shape[1] // 128):
            start = z * total_rows + slab + offset + lane * piece
            bundle[pl.ds(pl.multiple_of(start, 16), piece), :] = grad[
                z * piece:(z + 1) * piece, lane * 128:(lane + 1) * 128
            ]


def matrix_grads(bundle, left, right, offset, place_rows, dp, n_context, n_dp):
    block = left.shape[1] // n_dp
    tile = 2 * block
    for t in range(n_dp // 2):
        grad = dot_tn(left[:, t * tile:(t + 1) * tile], right[...]).astype(bf16)
        for half in range(2):
            store_grads(
                bundle, grad[half * block:(half + 1) * block], 2 * t + half, offset, place_rows, dp, n_context,
                block // n_context,
            )


def expert_grads(bundle, x, dz, hidden, dgate, dup, offset, down_at, place_rows, dp, n_context, n_dp):
    width, columns = x.shape[1], hidden.shape[1]
    tile = 2 * width // n_dp
    total_rows = bundle.shape[0] // n_context
    for mat, source in enumerate((dgate, dup)):
        matrix_grads(
            bundle, x, source, offset + mat * (columns // 128) * (width // n_dp // n_context), place_rows, dp,
            n_context, n_dp,
        )
    for t in range(n_dp // 2):
        grad = dot_tn(dz[:, t * tile:(t + 1) * tile], hidden[...]).astype(bf16)
        for z in range(n_context):
            start = z * total_rows + down_at + t * tile
            bundle[start:start + tile, :] = grad[:, z * 128:(z + 1) * 128]


class Layout:
    def __init__(self, width, hidden, n_dp, n_context):
        self.piece = width // n_dp // n_context
        self.shared_blocks, self.blocks = hidden // 8 // 128, hidden // 4 // 128
        self.shared_place = 2 * self.shared_blocks * self.piece
        self.run_place = 2 * self.blocks * self.piece
        self.down_rows = hidden // 8 // n_context
        self.shared_down = self.down_rows * (width // 128)


def feed_grads_kernel(n_dp, layout, place, *refs):
    refs = list(refs)

    def take(count):
        part = refs[:count]
        del refs[:count]
        return part

    runs = [take(n_dp), take(n_dp)]
    shared_far = take(n_dp)
    downs, got_downs = take(2), take(2)
    (gate, up, down, gate_s, up_s, down_s) = refs
    dp, side = place[1], place[5]
    core = place[3]
    piece = layout.piece
    hidden = gate.shape[2]
    columns = layout.blocks * 128
    width = down.shape[2]

    for mask in range(n_dp):
        source = lax.bitwise_xor(dp, mask)
        which = lax.bitwise_and(source, 1)
        for run in range(2):
            begin = (source // 2) * (2 * columns) + run * columns
            for mat, target in enumerate((gate, up)):
                for lane in range(layout.blocks):
                    start = run * layout.shared_place + (mat * layout.blocks + lane) * piece
                    target[which, :, pl.ds(pl.multiple_of(begin + lane * 128, 128), 128)] = runs[run][mask][
                        start:start + piece, :
                    ].astype(f32)
    shared_down = layout.shared_down
    kept = jnp.where(core == 0, downs[0][...], downs[1][shared_down:, :])
    got = jnp.where(core == 0, got_downs[0][...], got_downs[1][...])
    down[core] = kept.astype(f32).T
    down[1 - core] = got.astype(f32).T

    lane_of = lax.broadcasted_iota(jnp.int32, (piece, 128), 1)
    for mask in range(n_dp):
        source = lax.bitwise_xor(dp, mask)
        for mat, target in enumerate((gate_s, up_s)):
            for lane in range(layout.shared_blocks):
                start = (mat * layout.shared_blocks + lane) * piece
                own = runs[1][mask][start:start + piece, :].astype(f32)
                far = shared_far[mask][start:start + piece, :].astype(f32)
                first = jnp.where(side == 0, own, far)
                second = jnp.where(side == 0, far, own)
                begin = source * (hidden // n_dp) + lane * 256
                target[:, pl.ds(pl.multiple_of(begin, 128), 128)] = jnp.where(
                    lane_of < 64, first, pltpu.roll(second, 64, 1)
                )
                target[:, pl.ds(pl.multiple_of(begin + 128, 128), 128)] = jnp.where(
                    lane_of < 64, pltpu.roll(first, 64, 1), second
                )
    down_rows = layout.down_rows
    for lane in range(width // 128):
        rows = slice(lane * down_rows, (lane + 1) * down_rows)
        far_rows = slice(layout.shared_place + rows.start, layout.shared_place + rows.stop)
        lanes = slice(lane * 128, (lane + 1) * 128)
        down_s[pl.ds(pl.multiple_of(side * down_rows, 16), down_rows), lanes] = downs[1][rows, :].astype(f32)
        down_s[pl.ds(pl.multiple_of((1 - side) * down_rows, 16), down_rows), lanes] = shared_far[0][
            far_rows, :
        ].astype(f32)


def last_kernel(blocks, place, *refs):
    packs, (token, gain1, grad_own, grad_middle) = refs[:2], refs[2:6]
    pulled = refs[6:5 + blocks]
    (input_grad, qkv, out, norm1, norm2, router) = refs[5 + blocks:]
    side = place[5]
    piece, width = out.shape
    own, far_half = packs[0][...].astype(f32), packs[1][...].astype(f32)
    whole, start = [], 0
    for columns in ((3 * width // 2 + width + 128) // 2, (3 * width // 2 + 128) // 2):
        here, there = own[:, start:start + columns], far_half[:, start:start + columns]
        whole.append(jnp.concatenate([jnp.where(side == 0, here, there), jnp.where(side == 0, there, here)], axis=1))
        start += columns
    tile = width // 2
    for mat in range(3):
        for half in range(2):
            qkv[:, mat * width + half * tile:mat * width + (half + 1) * tile] = whole[half][
                :, mat * tile:(mat + 1) * tile
            ]
    out[...] = whole[0][:, 3 * tile:3 * tile + width]
    small = whole[1][:, 3 * tile:3 * tile + 128]
    small = jnp.concatenate([small, jnp.zeros((128 - piece, 128), f32)], axis=0).T
    router[...] = small[:router.shape[0], :piece]
    norm2[...] = small[8:9, :piece]
    norm1[...] = small[9:10, :piece]

    x = token[...].astype(f32)
    factor = lax.rsqrt(jnp.mean(x * x, axis=-1, keepdims=True) + norm_eps)
    normed = x * factor
    grad_entry = grad_own[...]
    for part in pulled:
        grad_entry = grad_entry + part[...].astype(f32)
    grad_norm = grad_entry * gain1[...]
    inner = jnp.mean(grad_norm * normed, axis=-1, keepdims=True)
    input_grad[...] = grad_middle[...] + factor * (grad_norm - normed * inner)


def load_turns(copies, sources, targets, blocks, rows, here):
    started = []
    for r in range(blocks):
        block = pl.ds(pl.multiple_of(jnp.maximum(here - r, 0) * rows, rows), rows)
        for source, target in zip(sources, targets):
            started.append(copies.start(source.at[block], target.at[r * rows:(r + 1) * rows]))
    return started


def attend_back(first, pairs, bias, queries, keys, values, log_total, grad_ctx, turns, grad_q, grad_kv):
    cos, sin_up, sin_down = turns
    rows = queries.shape[0]
    width = queries.shape[1]
    scale = HEAD_DIM ** (-0.5)
    half = lane_half(rows)

    def attend(pair, carry):
        lanes = pl.ds(pl.multiple_of(pair * 128, 128), 128)
        both_q = queries[:, lanes] * scale
        both_g = grad_ctx[:, pl.ds(pl.multiple_of((first + pair) * 128, 128), 128)]
        both_l = log_total[pair]
        dq = dk = dv = None
        for head in range(2):
            query = jnp.where(half == head, both_q, jnp.zeros_like(both_q))
            grad = jnp.where(half == head, both_g, jnp.zeros_like(both_g))
            log_row = both_l[:, head * HEAD_DIM:head * HEAD_DIM + 1]
            prob = jnp.exp(dot_nt(query, keys[:, lanes]) + bias - log_row)
            grad_prob = dot_nt(grad, values[:, lanes])
            delta = jnp.sum(prob * grad_prob, axis=-1, keepdims=True)
            grad_score = (prob * (grad_prob - delta)).astype(bf16)
            dq_head = dot_nn(grad_score, keys[:, lanes])
            dk_head = dot_tn(grad_score, query)
            dv_head = dot_tn(prob.astype(bf16), grad)
            if head == 0:
                dq, dk, dv = dq_head, dk_head, dv_head
            else:
                dq, dk, dv = jnp.where(half == 0, dq, dq_head), dk + dk_head, dv + dv_head
        grad_q[:, lanes] = spin_back(dq * scale, cos[:rows, :], sin_up[:rows, :], sin_down[:rows, :]).astype(bf16)
        far_lanes = pl.ds(pl.multiple_of(width + pair * 128, 128), 128)
        grad_kv[:, lanes] = spin_back(dk, cos[...], sin_up[...], sin_down[...]).astype(bf16)
        grad_kv[:, far_lanes] = dv.astype(bf16)
        return carry

    lax.fori_loop(0, pairs, attend, 0)


def store_pack(keep, send, value, start, dp, side, n_dp):
    n_half = keep.shape[-1]
    block = value.shape[0] // n_dp
    if start < n_half < start + value.shape[1]:
        store_pack(keep, send, value[:, :n_half - start], start, dp, side, n_dp)
        store_pack(keep, send, value[:, n_half - start:], n_half, dp, side, n_dp)
        return
    side_of = start // n_half
    lanes = slice(start - side_of * n_half, start - side_of * n_half + value.shape[1])
    flip_side = lax.bitwise_xor(side_of, side)
    for part in range(n_dp):
        piece = value[part * block:(part + 1) * block, :].astype(bf16)
        flip = lax.bitwise_xor(part, dp)

        @pl.when(lax.bitwise_and(flip, 1) == 0)
        def _():
            keep[flip // 2, flip_side, :, lanes] = piece

        @pl.when(lax.bitwise_and(flip, 1) == 1)
        def _():
            send[flip // 2, flip_side, :, lanes] = piece


def back_kernel(blocks, n_dp, place, *refs):
    parts = refs[:4]
    (
        middle, cot, gain2, out_w, queries_hbm, keys_hbm, values_hbm, log_hbm, context_hbm, entry_hbm, *turns_hbm
    ) = refs[4:17]
    (grad_middle, grad_ctx, grad_q, grad_kv, notes, keep, send) = refs[17:24]
    (queries, keys, values, log_total, context, entry, cos, sin_up, sin_down, sems) = refs[24:]
    rows, width = middle.shape
    here, dp, side = place[6], place[1], place[5]
    copies = Copies(sems)
    part = slice(0, queries.shape[1])
    turns = (cos, sin_up, sin_down)
    first_in = [
        copies.start(source, target)
        for source, target in (
            (queries_hbm.at[:, part], queries), (keys_hbm.at[:, part], keys), (values_hbm.at[:, part], values),
            (log_hbm.at[:log_total.shape[0]], log_total),
        )
    ]
    first_in += load_turns(copies, turns_hbm, turns, blocks, rows, here)
    late_in = [copies.start(context_hbm, context), copies.start(entry_hbm, entry)]

    grad_two = parts[0][...].astype(f32)
    for value in parts[1:]:
        grad_two = grad_two + value[...].astype(f32)
    mid = middle[...]
    factor = lax.rsqrt(jnp.mean(mid * mid, axis=-1, keepdims=True) + norm_eps)
    normed = mid * factor
    notes[...] = jnp.zeros_like(notes)
    notes[0:1, :] = jnp.sum(grad_two * normed, axis=0, keepdims=True)
    grad_norm = grad_two * gain2[...]
    inner = jnp.mean(grad_norm * normed, axis=-1, keepdims=True)
    grad_mid = cot[...].astype(f32) + factor * (grad_norm - normed * inner)
    grad_middle[...] = grad_mid
    grad_attn = grad_mid.astype(bf16)
    grad_ctx[...] = dot_nt(grad_attn, out_w[...]).astype(bf16)
    for copy in first_in:
        copy.wait()
    attend_back(
        0, log_total.shape[0], key_bias(blocks, rows, here), queries, keys, values, log_total, grad_ctx, turns, grad_q,
        grad_kv,
    )
    for copy in late_in:
        copy.wait()
    tile = queries.shape[1]
    store_pack(keep, send, dot_tn(entry[:rows, :], grad_q[...]), 0, dp, side, n_dp)
    for mat in range(2):
        grad = dot_tn(entry[...], grad_kv[:, mat * tile:(mat + 1) * tile])
        store_pack(keep, send, grad, (1 + mat) * tile, dp, side, n_dp)
    for start in range(0, width, tile):
        store_pack(keep, send, dot_tn(context[...], grad_attn[:, start:start + tile]), 3 * tile + start, dp, side, n_dp)
    used = 3 * tile + width
    store_pack(keep, send, jnp.zeros((width, 2 * keep.shape[-1] - used), f32), used, dp, side, n_dp)


def rest_kernel(blocks, n_dp, place, *refs):
    tokens_hbm = refs[:blocks]
    (notes, router_part, grad_ctx) = refs[blocks:blocks + 3]
    (
        queries_hbm, keys_hbm, values_hbm, log_hbm, entry_hbm, qkv_hbm, grad_q_hbm, grad_kv_hbm, *turns_hbm
    ) = refs[blocks + 3:blocks + 14]
    outs = refs[blocks + 14:]
    grad_own, grad_far, (keep, send) = outs[0], outs[1:blocks], outs[blocks:blocks + 2]
    (
        tokens, queries, keys, values, log_total, entry, qkv_w, grad_q0, grad_kv0, cos, sin_up, sin_down, grad_q,
        grad_kv, sems,
    ) = outs[blocks + 2:]
    rows, width = grad_ctx.shape
    here, dp, side = place[6], place[1], place[5]
    copies = Copies(sems)
    tile = queries.shape[1]
    pairs = log_total.shape[0]
    part = slice(tile, 2 * tile)
    turns = (cos, sin_up, sin_down)
    first_in = [
        copies.start(source, target)
        for source, target in (
            (queries_hbm.at[:, part], queries), (keys_hbm.at[:, part], keys), (values_hbm.at[:, part], values),
            (log_hbm.at[pairs:], log_total),
        )
    ]
    first_in += load_turns(copies, turns_hbm, turns, blocks, rows, here)
    late_in = [
        copies.start(source, target)
        for source, target in (
            (entry_hbm, entry), (qkv_hbm, qkv_w), (grad_q_hbm, grad_q0), (grad_kv_hbm, grad_kv0),
            *((tokens_hbm[r], tokens.at[r]) for r in range(blocks)),
        )
    ]
    for copy in first_in:
        copy.wait()
    attend_back(
        pairs, pairs, key_bias(blocks, rows, here), queries, keys, values, log_total, grad_ctx, turns, grad_q, grad_kv
    )
    for copy in late_in:
        copy.wait()
    store_pack(keep, send, dot_tn(entry[:rows, :], grad_q[...]), 0, dp, side, n_dp)
    for mat in range(2):
        grad = dot_tn(entry[...], grad_kv[:, mat * tile:(mat + 1) * tile])
        store_pack(keep, send, grad, (1 + mat) * tile, dp, side, n_dp)

    total = jnp.zeros((1, width), f32)
    for r in range(blocks):
        block = slice(r * rows, (r + 1) * rows)
        grad_entry = None
        for half, source in enumerate((grad_kv0, grad_kv)):
            for mat in range(2):
                start = (1 + mat) * width + half * tile
                term = dot_nt(source[block, mat * tile:(mat + 1) * tile], qkv_w[:, start:start + tile])
                grad_entry = term if grad_entry is None else grad_entry + term
        if r == 0:
            grad_entry = grad_entry + dot_nt(grad_q0[...], qkv_w[:, :tile]) + dot_nt(
                grad_q[...], qkv_w[:, tile:2 * tile]
            )
            grad_own[...] = grad_entry
        else:
            grad_far[r - 1][...] = grad_entry.astype(bf16)
        x = tokens[r].astype(f32)
        factor = lax.rsqrt(jnp.mean(x * x, axis=-1, keepdims=True) + norm_eps)
        total = total + jnp.sum(grad_entry * (x * factor), axis=0, keepdims=True)
    notes_t = notes[...].T
    total_t = jnp.broadcast_to(total, (8, width)).T
    lane = lax.broadcasted_iota(jnp.int32, (width, 128), 1)
    small = router_part[...] + jnp.where(lane == 8, notes_t[:, 0:1], 0.0) + jnp.where(
        lane == 9, total_t[:, 0:1], 0.0
    )
    store_pack(keep, send, small, 3 * tile, dp, side, n_dp)


def call(kernel, outs, scratch, scalars, operands, after=(), limit=60, aliases=None):
    whole = pl.BlockSpec(memory_space=pltpu.VMEM)
    anywhere = pl.BlockSpec(memory_space=pl.ANY)
    values, specs = [], []
    for value, kind in [*operands, *((value, far) for value in after)]:
        value = pltpu.with_memory_space_constraint(value, pltpu.VMEM if kind == held else pltpu.HBM)
        if isinstance(kind, int):
            kind = anywhere if kind == far else whole
        values.append(value)
        specs.append(kind)
    taken, ignored = len(operands), len(after)

    def body(place, *refs):
        kernel(place, *refs[:taken], *refs[taken + ignored:])

    return pl.pallas_call(
        body,
        grid_spec=pltpu.PrefetchScalarGridSpec(
            num_scalar_prefetch=1,
            grid=(1,),
            in_specs=specs,
            out_specs=[anywhere if kind == far else whole for _, _, kind in outs],
            scratch_shapes=scratch,
        ),
        out_shape=[
            pltpu.HBM(shape, dtype) for shape, dtype, _ in outs
        ],
        input_output_aliases=aliases or {},
        compiler_params=pltpu.CompilerParams(vmem_limit_bytes=limit * 2**20),
        cost_estimate=pl.CostEstimate(flops=10**8, bytes_accessed=0, transcendentals=0),
    )(scalars, *values)


def hold_until(scalars, values, after):
    return call(
        lambda place, *refs: None,
        [(value.shape, value.dtype, far) for value in values],
        [],
        scalars,
        [(value, far) for value in values],
        after,
        limit=1,
        aliases={1 + k: k for k in range(len(values))},
    )


def swap(value, mask):
    return lax.ppermute(value, group, [(i, i ^ mask) for i in range(8)])


def on_block(
    n_context,
    tokens,
    norm1_gain,
    qkv_weight,
    out_weight,
    norm2_gain,
    router_weight,
    expert_gate,
    expert_up,
    expert_down,
    shared_gate,
    shared_up,
    shared_down,
    routes,
    cotangent,
):
    rows, width = tokens.shape[1:]
    hidden = shared_gate.shape[1]
    n_experts = router_weight.shape[1]
    blocks = n_context
    n_dp = 4
    slots = rows * routes.shape[-1] * 5 // (4 * n_experts)
    dp = lax.axis_index(DP)
    here = lax.axis_index(CONTEXT)
    side = lax.axis_index(EXPERTS)
    core, chip = dp % 2, dp // 2
    index = dp * 2 + side
    expert = 2 * side + core
    pairs = width // 128

    own = tokens[0]
    cot = cotangent[0]
    cot_all = lax.all_gather(cot, group, axis=0)
    field = [own, lax.ppermute(own, CONTEXT, [(i, i + 1) for i in range(n_context - 1)])]
    field.append(lax.ppermute(field[1], CONTEXT, [(i, i + 1) for i in range(1, n_context - 1)]))
    field += [
        lax.ppermute(own, CONTEXT, [(i, i + r) for i in range(n_context - r)]) for r in range(3, blocks)
    ]
    tables = spin_tables(n_context * rows)
    gain1, gain2 = norm1_gain[None, :], norm2_gain[None, :]
    scalars = jnp.stack([index, dp, expert, core, chip, side, here])
    piece = width // n_dp // n_context
    half_columns = hidden // 2
    chunk_columns = hidden // 4
    shared_columns = hidden // 8
    quarter = hidden // n_dp

    def many(kind, *values):
        return [(value, kind) for value in values]

    router = jnp.pad(router_weight, ((0, 0), (0, 128 - n_experts)))
    router_t = jnp.pad(router_weight.T, ((0, 128 - n_experts), (0, 0)))

    picked_up = ((width, shared_columns), bf16, copied)
    picked = call(
        partial(pick_kernel, n_context),
        [picked_up, picked_up, ((shared_columns, width), bf16, copied)],
        [],
        scalars,
        [
            (shared_gate, pl.BlockSpec((width, quarter), lambda i, s: (0, s[1]))),
            (shared_up, pl.BlockSpec((width, quarter), lambda i, s: (0, s[1]))),
            (shared_down, pl.BlockSpec((quarter, width), lambda i, s: (s[1], 0))),
        ],
        [router, router_t],
        limit=10,
    )

    act = (rows, width)
    wide = (blocks * rows, width)
    sent = (rows + 16, width)
    logs = (pairs, rows, 128)
    turn = (blocks * rows, 128)
    entry, queries, keys, values, log_total, context, middle, entry_two = call(
        partial(attend_kernel, blocks),
        [
            (wide, bf16, far), (act, bf16, far), (wide, bf16, far), (wide, bf16, far), (logs, f32, far),
            (act, bf16, far), (act, f32, copied), (sent, bf16, copied),
        ],
        [
            *[pltpu.VMEM(turn, f32)] * 3, pltpu.VMEM(wide, bf16), pltpu.VMEM(act, bf16), pltpu.VMEM(wide, bf16),
            pltpu.VMEM(wide, bf16), pltpu.VMEM(logs, f32), pltpu.VMEM(act, bf16), pltpu.SemaphoreType.DMA((32,)),
        ],
        jnp.stack([here]),
        [
            *many(copied, *field, routes[0, 0].T, gain1), *many(held, qkv_weight, out_weight),
            (gain2, copied), *many(far, *tables),
        ],
        [picked[0]],
        limit=24,
    )

    near = {0: entry_two}
    near[1], near[4] = swap(entry_two, 1), swap(entry_two, 4)
    near[5] = swap(near[1], 4)
    for mask in keep_masks:
        near[mask ^ 2] = swap(near[mask], 2)

    slot_act, slot_chunk, slot_notes = (8 * slots, width), (8 * slots, chunk_columns), (8 * slots, 128)
    row_act, row_hidden = (8 * rows, width), (8 * rows, shared_columns)
    layout = Layout(width, hidden, n_dp, n_context)
    rows0 = n_context * (n_dp * layout.run_place + width)
    rows1 = n_context * (n_dp * (layout.shared_place + layout.run_place) + layout.shared_down + width)
    run_scratch = [
        *[pltpu.VMEM((width, chunk_columns), bf16)] * 2, pltpu.VMEM((chunk_columns, width), bf16),
    ]
    kept = [(slot_notes, f32), ((8, slots, rows), bf16), *[(slot_act, bf16)] * 2]
    every = [near[mask] for mask in all_masks]
    *entered, bundle0 = call(
        partial(enter_kernel, all_masks, n_context, n_dp, layout),
        [*[(*out, far) for out in kept], ((rows0, 128), bf16, copied)],
        [
            *[pltpu.VMEM(*out) for out in kept], *[pltpu.VMEM(slot_act, bf16)] * 2, *[pltpu.VMEM(row_act, bf16)] * 2,
            *run_scratch, *[pltpu.VMEM(slot_chunk, bf16)] * 3, pltpu.VMEM((8, 16, width), bf16),
            pltpu.SemaphoreType.DMA((40,)),
        ],
        scalars,
        [*many(far, *every, cot_all), (router, copied), *many(far, expert_gate, expert_up, expert_down)],
        limit=56,
    )
    sum0 = lax.psum_scatter(bundle0, CONTEXT, scatter_dimension=0, tiled=True)
    four = (4, rows, width)
    grad_keep, grad_send, mix_keep, mix_send, router_part, bundle1 = call(
        partial(leave_kernel, all_masks, n_context, n_dp, layout),
        [*[(four, bf16, far)] * 4, ((width, 128), f32, copied), ((rows1, 128), bf16, copied)],
        [
            *[pltpu.VMEM(*out) for out in kept], *[pltpu.VMEM(slot_act, bf16)] * 3, *[pltpu.VMEM(slot_act, f32)] * 2,
            *[pltpu.VMEM(row_act, bf16)] * 2, *run_scratch, *[pltpu.VMEM((width, shared_columns), bf16)] * 2, pltpu.VMEM((shared_columns, width), bf16),
            *[pltpu.VMEM(slot_chunk, bf16)] * 3, *[pltpu.VMEM(row_hidden, bf16)] * 3,
            *[pltpu.VMEM((8, rows, width), bf16)] * 2, pltpu.VMEM((8 * slots, 2 * width), bf16),
            pltpu.SemaphoreType.DMA((56,)),
        ],
        scalars,
        [
            *many(far, *entered, *every, cot_all), (router_t, copied),
            *many(far, *picked, expert_gate, expert_up, expert_down),
        ],
        limit=58,
    )
    sum1 = lax.psum_scatter(bundle1, CONTEXT, scatter_dimension=0, tiled=True)

    def add_blocks(left, right):
        return [
            (left[k].astype(f32) + right[k].astype(f32)).astype(bf16) for k in range(left.shape[0])
        ]

    grad_sums = add_blocks(grad_keep, swap(grad_send, 2))
    parts = [grad_sums[0], *[swap(value, mask) for value, mask in zip(grad_sums[1:], keep_masks[1:])]]

    mix_sums = add_blocks(mix_keep, swap(mix_send, 2))
    sent_mix = hold_until(scalars, mix_sums[1:], parts[1:])
    mix_parts = [middle, mix_sums[0], *[swap(value, mask) for value, mask in zip(sent_mix, keep_masks[1:])]]

    tile = width // 2
    pack_rows = width // n_dp
    half_act, half_wide, half_logs = (rows, tile), (blocks * rows, tile), (pairs // 2, rows, 128)
    pack0 = (2, 2, pack_rows, (3 * tile + width + 128) // 2)
    pack1 = (2, 2, pack_rows, (3 * tile + 128) // 2)
    half_heads = [
        pltpu.VMEM(half_act, bf16), pltpu.VMEM(half_wide, bf16), pltpu.VMEM(half_wide, bf16), pltpu.VMEM(half_logs, f32)
    ]
    turn_scratch = [pltpu.VMEM(turn, f32)] * 3
    grad_middle, grad_ctx, grad_q, grad_kv, notes, keep0, send0 = call(
        partial(back_kernel, blocks, n_dp),
        [
            (act, f32, copied), (act, bf16, copied), (half_act, bf16, copied), (wide, bf16, copied),
            ((8, width), f32, copied), (pack0, bf16, copied), (pack0, bf16, copied),
        ],
        [
            *half_heads, pltpu.VMEM(act, bf16), pltpu.VMEM(wide, bf16), *turn_scratch, pltpu.SemaphoreType.DMA((24,)),
        ],
        scalars,
        [
            *many(copied, *parts, middle, cot, gain2, out_weight),
            *many(far, queries, keys, values, log_total, context, entry, *tables),
        ],
        sent_mix,
        limit=44,
    )

    def by_chips(keep, send):
        other = swap(send, 2)
        sums = [(keep[i, j].astype(f32) + other[i, j].astype(f32)).astype(bf16) for i in range(2) for j in range(2)]
        return [sums[0], swap(sums[1], 1), swap(sums[2], 4), swap(sums[3], 5)]

    def by_context(sets, after):
        columns = sum(arrived[0].shape[1] for arrived in sets)
        shares = call(
            partial(sum_kernel, n_context, [len(arrived) for arrived in sets]),
            [((piece, columns), bf16, copied)] * n_context, [], scalars,
            many(copied, *[value for arrived in sets for value in arrived]), after, limit=16,
        )
        return [shares[0]] + [
            lax.ppermute(shares[r], CONTEXT, [(i, (i + r) % n_context) for i in range(n_context)])
            for r in range(1, n_context)
        ]

    def total(shares):
        value = sum(value.astype(f32) for value in shares).astype(bf16)
        return [value, swap(value, 1)]

    send0, = hold_until(scalars, [send0], mix_parts[2:])
    arrived0 = by_chips(keep0, send0)
    results = call(
        partial(rest_kernel, blocks, n_dp),
        [(act, f32, copied), *[(act, bf16, copied)] * (blocks - 1), *[(pack1, bf16, copied)] * 2],
        [
            pltpu.VMEM((blocks, rows, width), bf16), *half_heads, pltpu.VMEM(wide, bf16),
            pltpu.VMEM(qkv_weight.shape, bf16), pltpu.VMEM(half_act, bf16), pltpu.VMEM(wide, bf16), *turn_scratch,
            pltpu.VMEM(half_act, bf16), pltpu.VMEM(wide, bf16), pltpu.SemaphoreType.DMA((32,)),
        ],
        scalars,
        [
            *many(far, *field), *many(copied, notes, router_part, grad_ctx),
            *many(far, queries, keys, values, log_total, entry, qkv_weight, grad_q, grad_kv, *tables),
        ],
        [arrived0[0]],
        limit=44,
    )
    grad_own, keep1 = results[0], results[blocks]
    *grad_far, send1 = hold_until(scalars, [*results[1:blocks], results[blocks + 1]], arrived0[1:])
    run0 = [sum0[m * layout.run_place:(m + 1) * layout.run_place] for m in range(n_dp)]
    run0 = [run0[0]] + [swap(run0[m], 2 * m) for m in range(1, n_dp)]
    down0 = sum0[n_dp * layout.run_place:]
    got_down0 = lax.ppermute(down0, DP, [(i, i ^ 1) for i in range(n_dp) if i % 2 == 1])
    output = sum(value.astype(f32) for value in mix_parts).astype(bf16)[None]

    arrived1 = by_chips(keep1, send1)
    pulled = [
        lax.ppermute(grad_far[r - 1], CONTEXT, [(i, i - r) for i in range(r, n_context)])
        for r in range(1, blocks)
    ]
    sum1, = hold_until(scalars, [sum1], [arrived1[0], *pulled[2:]])
    slab_rows = layout.shared_place + layout.run_place
    run1 = [sum1[m * slab_rows:(m + 1) * slab_rows] for m in range(n_dp)]
    downs1 = sum1[n_dp * slab_rows:]
    shared = [slab[:layout.shared_place] for slab in run1]
    shared[0] = jnp.concatenate([shared[0], downs1[:layout.shared_down]], axis=0)
    shared_far = [swap(value, 2 * m + 1) for m, value in enumerate(shared)]
    run1 = [run1[0]] + [swap(run1[m], 2 * m) for m in range(1, n_dp)]
    got_down1 = lax.ppermute(
        downs1[layout.shared_down:], DP, [(i, i ^ 1) for i in range(n_dp) if i % 2 == 0]
    )

    shares = by_context([arrived0, arrived1], [pulled[1], *run0[1:], got_down0, *run1[1:], *shared_far, got_down1])
    gate_grad, up_grad, down_grad, gate_s_grad, up_s_grad, down_s_grad = call(
        partial(feed_grads_kernel, n_dp, layout),
        [
            (shape, f32, copied)
            for shape in (
                (2, piece, hidden), (2, piece, hidden), (2, 128, width), (piece, hidden), (piece, hidden),
                (hidden // n_dp // n_context, width),
            )
        ],
        [],
        scalars,
        many(copied, *run0, *run1, *shared_far, down0, downs1, got_down0, got_down1),
        [shares[0], *pulled],
        limit=32,
    )
    shares = [shares[0], *hold_until(scalars, shares[1:], [down_s_grad])]
    input_grad, qkv_grad, out_grad, norm1_grad, norm2_grad, router_grad = call(
        partial(last_kernel, blocks),
        [
            (shape, f32, copied)
            for shape in (act, (piece, 3 * width), (piece, width), (1, piece), (1, piece), (n_experts, piece))
        ],
        [],
        scalars,
        many(copied, *total(shares), own, gain1, grad_own, grad_middle, *pulled),
        limit=32,
    )
    return (
        output, input_grad[None], norm1_grad[0], qkv_grad, out_grad, norm2_grad[0], router_grad.T,
        gate_grad, up_grad, down_grad, gate_s_grad, up_s_grad, down_s_grad,
    )


def on_any(mesh, *args):
    tokens, router_weight, expert_gate, shared_gate = args[0], args[5], args[6], args[9]
    sizes = dict(mesh.shape)
    fits = (
        sizes[DP] == 4
        and sizes[EXPERTS] == 2
        and tokens.shape[0] == 1
        and tokens.shape[1] == BLOCK
        and expert_gate.shape[0] == 2
        and tokens.shape[2] % 128 == 0
        and tokens.shape[2] // sizes[DP] % (16 * sizes[CONTEXT]) == 0
        and shared_gate.shape[1] % (1024) == 0
        and sizes[CONTEXT] == 4
        and shared_gate.shape[1] == 128 * sizes[DP] * sizes[CONTEXT]
    )
    if fits:
        return on_block(sizes[CONTEXT], *args)
    return on_device(*args)


def solution(mesh):
    return jax.shard_map(
        partial(on_any, mesh),
        mesh=mesh,
        in_specs=(
            P((DP, EXPERTS), CONTEXT, None),
            P(),
            P(),
            P(),
            P(),
            P(),
            P(EXPERTS, None, None),
            P(EXPERTS, None, None),
            P(EXPERTS, None, None),
            P(),
            P(),
            P(),
            P(CONTEXT, (DP, EXPERTS), None, None),
            P((DP, EXPERTS), CONTEXT, None),
        ),
        out_specs=(
            P((DP, EXPERTS), CONTEXT, None),
            P((DP, EXPERTS), CONTEXT, None),
            P((DP, CONTEXT)),
            P((DP, CONTEXT), None),
            P((DP, CONTEXT), None),
            P((DP, CONTEXT)),
            P((DP, CONTEXT), None),
            P(EXPERTS, (DP, CONTEXT), None),
            P(EXPERTS, (DP, CONTEXT), None),
            P(EXPERTS, (DP, CONTEXT), None),
            P((DP, CONTEXT), None),
            P((DP, CONTEXT), None),
            P((DP, CONTEXT), None),
        ),
        check_vma=False,
    )
```

```python
from functools import partial
import math

import jax
import jax.numpy as jnp
import numpy as np
from jax import lax
from jax.experimental import pallas as pl
from jax.experimental.pallas import tpu as pltpu
from jax.sharding import PartitionSpec as P

HEAD_DIM = 64
BLOCK = 256
DP, CONTEXT, EXPERTS = "dp", "context", "experts"


norm_eps = 1e-05
masked_score = -1e30
highest = lax.Precision.HIGHEST


def matmul(left, right):
    return jnp.dot(left, right, preferred_element_type=jnp.float32)


def contract(spec, left, right):
    return jnp.einsum(spec, left, right, preferred_element_type=jnp.float32)


def normalize(field):
    factor = lax.rsqrt(jnp.mean(field * field, axis=-1, keepdims=True) + norm_eps)
    return (field * factor, factor)


def norm_back(grad_out, normed, factor, gain):
    grad_norm = grad_out * gain
    inner = jnp.mean(grad_norm * normed, axis=-1, keepdims=True)
    return (factor * (grad_norm - normed * inner), jnp.sum(grad_out * normed, axis=0))


def rotation(positions, head_dim):
    half = head_dim // 2
    freqs = 10000.0 ** (-2.0 * jnp.arange(half, dtype=jnp.float32) / head_dim)
    angles = positions.astype(jnp.float32)[:, None] * freqs[None, :]
    return (jnp.cos(angles)[:, None, None, :], jnp.sin(angles)[:, None, None, :])


def rotate(field, cosine, sine):
    half = field.shape[-1] // 2
    first = field[..., :half]
    second = field[..., half:]
    return jnp.concatenate(
        [first * cosine - second * sine, second * cosine + first * sine], axis=-1
    )


def rotate_back(grad, cosine, sine):
    half = grad.shape[-1] // 2
    first = grad[..., :half]
    second = grad[..., half:]
    return jnp.concatenate(
        [first * cosine + second * sine, second * cosine - first * sine], axis=-1
    )


def silu_back(grad_hidden, gate_part, up_part):
    sigmoid_value = jax.nn.sigmoid(gate_part)
    active = gate_part * sigmoid_value
    grad_gate = grad_hidden * up_part * sigmoid_value * (1.0 + gate_part * (1.0 - sigmoid_value))
    grad_up = grad_hidden * active
    return (grad_gate.astype(jnp.bfloat16), grad_up.astype(jnp.bfloat16))


def score_block(queries, keys_part, query_block, start):
    size = keys_part.shape[0]
    seqs, heads, head_dim = (queries.shape[1], queries.shape[2], queries.shape[3])
    keys_four = keys_part.reshape(size, seqs, heads, head_dim)
    scores = contract("qshd,kshd->shqk", queries, keys_four) * head_dim ** (-0.5)
    key_block = (start + jnp.arange(size)) // BLOCK
    visible = key_block[None, :] <= query_block[:, None]
    return (jnp.where(visible, scores, masked_score), visible, keys_four)


def attend_piece(queries, query_block, state, keys_part, values_part, start):
    size = keys_part.shape[0]
    seqs, heads, head_dim = (queries.shape[1], queries.shape[2], queries.shape[3])

    def compute(current):
        best, total, accum = current
        scores, visible, keys_four = score_block(queries, keys_part, query_block, start)
        new_best = jnp.maximum(best, jnp.max(scores, axis=-1))
        weights = jnp.where(visible, jnp.exp(scores - new_best[..., None]), 0.0)
        factor = jnp.exp(best - new_best)
        values_four = values_part.reshape(size, seqs, heads, head_dim)
        total = total * factor + jnp.sum(weights, axis=-1)
        accum = accum * factor[..., None] + contract(
            "shqk,kshd->shqd", weights.astype(jnp.bfloat16), values_four
        )
        return (new_best, total, accum)

    needed = start // BLOCK <= jnp.max(query_block)
    return lax.cond(needed, compute, lambda current: current, state)


def fold_keys(queries, query_block, state, pieces):
    keys_all, values_all = pieces
    length = keys_all.shape[0]
    size = math.gcd(length, 512)

    def step(index, current):
        first = index * size
        keys_part = lax.dynamic_slice_in_dim(keys_all, first, size, 0)
        values_part = lax.dynamic_slice_in_dim(values_all, first, size, 0)
        return attend_piece(queries, query_block, current, keys_part, values_part, first)

    return lax.fori_loop(0, length // size, step, state)


def block_grads(queries, query_block, grad_ctx, delta, log_total, keys_part, values_part, start):
    size = keys_part.shape[0]
    seqs, heads, head_dim = (queries.shape[1], queries.shape[2], queries.shape[3])
    scores, visible, keys_four = score_block(queries, keys_part, query_block, start)
    probs = jnp.where(visible, jnp.exp(scores - log_total[..., None]), 0.0)
    values_four = values_part.reshape(size, seqs, heads, head_dim)
    grad_probs = contract("qshd,kshd->shqk", grad_ctx, values_four)
    grad_scores = (probs * (grad_probs - delta[..., None])).astype(jnp.bfloat16)
    return (probs, grad_scores, keys_four)


def key_value_terms(
    queries, query_block, grad_ctx, delta, log_total, keys_part, values_part, start
):
    size = keys_part.shape[0]
    seqs, heads, head_dim = (queries.shape[1], queries.shape[2], queries.shape[3])
    width = heads * head_dim
    probs, grad_scores, keys_four = block_grads(
        queries, query_block, grad_ctx, delta, log_total, keys_part, values_part, start
    )
    grad_values = contract("shqk,qshd->kshd", probs.astype(jnp.bfloat16), grad_ctx)
    grad_keys = contract("shqk,qshd->kshd", grad_scores, queries) * head_dim ** (-0.5)
    return jnp.concatenate(
        [grad_keys.reshape(size, seqs, width), grad_values.reshape(size, seqs, width)], axis=-1
    )


def query_grads(queries, query_block, grad_ctx, delta, log_total, keys_all, values_all):
    length = keys_all.shape[0]
    size = math.gcd(length, 512)

    def step(index, accum):
        first = index * size
        keys_part = lax.dynamic_slice_in_dim(keys_all, first, size, 0)
        values_part = lax.dynamic_slice_in_dim(values_all, first, size, 0)

        def compute(current):
            probs, grad_scores, keys_four = block_grads(
                queries, query_block, grad_ctx, delta, log_total, keys_part, values_part, first
            )
            return current + contract("shqk,kshd->qshd", grad_scores, keys_four)

        return lax.cond(
            first // BLOCK <= jnp.max(query_block), compute, lambda current: current, accum
        )

    return lax.fori_loop(0, length // size, step, jnp.zeros(queries.shape, jnp.float32))


def query_side_fold(keys_local, values_local, key_start, accum, pieces, start):
    queries_all, grad_all, delta_all, log_all = pieces
    length = queries_all.shape[0]
    size = math.gcd(length, 512)

    def step(index, current):
        first = index * size
        queries_part = lax.dynamic_slice_in_dim(queries_all, first, size, 0)
        grad_part = lax.dynamic_slice_in_dim(grad_all, first, size, 0)
        delta_part = jnp.transpose(lax.dynamic_slice_in_dim(delta_all, first, size, 0), (1, 2, 0))
        log_part = jnp.transpose(lax.dynamic_slice_in_dim(log_all, first, size, 0), (1, 2, 0))
        block_rows = (first + jnp.arange(size)) // BLOCK

        def compute(inner):
            return inner + key_value_terms(
                queries_part,
                block_rows,
                grad_part,
                delta_part,
                log_part,
                keys_local,
                values_local,
                key_start,
            )

        return lax.cond(
            jnp.max(block_rows) >= key_start // BLOCK, compute, lambda inner: inner, current
        )

    return lax.fori_loop(0, length // size, step, accum)


def reduce_experts(gate_grad, up_grad, down_grad):
    return (
        lax.psum_scatter(gate_grad, (DP, CONTEXT), scatter_dimension=1, tiled=True),
        lax.psum_scatter(up_grad, (DP, CONTEXT), scatter_dimension=1, tiled=True),
        lax.psum_scatter(down_grad, (DP, CONTEXT), scatter_dimension=1, tiled=True),
    )


def on_device(
    tokens,
    norm1_gain,
    qkv_weight,
    out_weight,
    norm2_gain,
    router_weight,
    expert_gate,
    expert_up,
    expert_down,
    shared_gate,
    shared_up,
    shared_down,
    routes,
    cotangent,
):
    seqs, span, width = tokens.shape
    heads = width // HEAD_DIM
    rows = seqs * span
    local = jnp.swapaxes(tokens, 0, 1).reshape(rows, width).astype(jnp.float32)
    key_start = lax.axis_index(CONTEXT) * span
    positions = key_start + jnp.arange(span)
    query_block = positions // BLOCK
    cosine, sine = rotation(positions, HEAD_DIM)
    normed_one, factor_one = normalize(local)
    entry_one = (normed_one * norm1_gain).astype(jnp.bfloat16)
    projected = matmul(entry_one, qkv_weight).reshape(span, seqs, 3, heads, HEAD_DIM)
    queries = rotate(projected[:, :, 0], cosine, sine).astype(jnp.bfloat16)
    keys_local = (
        rotate(projected[:, :, 1], cosine, sine).astype(jnp.bfloat16).reshape(span, seqs, width)
    )
    values_local = projected[:, :, 2].astype(jnp.bfloat16).reshape(span, seqs, width)
    start_state = (
        jnp.full((seqs, heads, span), masked_score, jnp.float32),
        jnp.zeros((seqs, heads, span), jnp.float32),
        jnp.zeros((seqs, heads, span, HEAD_DIM), jnp.float32),
    )
    best, total, accum = fold_keys(
        queries,
        query_block,
        start_state,
        (
            lax.all_gather(keys_local, CONTEXT, axis=0, tiled=True),
            lax.all_gather(values_local, CONTEXT, axis=0, tiled=True),
        ),
    )
    context = jnp.transpose(accum / total[..., None], (2, 0, 1, 3))
    log_total = best + jnp.log(total)
    context_low = context.astype(jnp.bfloat16).reshape(rows, width)
    middle = local + matmul(context_low, out_weight)
    normed_two, factor_two = normalize(middle)
    entry_two = (normed_two * norm2_gain).astype(jnp.bfloat16)
    logits = matmul(entry_two, router_weight)
    total_experts = router_weight.shape[1]
    topk = routes.shape[-1]
    capacity = rows * topk * 5 // (4 * total_experts)
    route_rows = jnp.swapaxes(routes[0], 0, 1).reshape(rows, topk)
    chosen = route_rows[:, :, None] == jnp.arange(total_experts)[None, None, :]
    chosen_float = chosen.astype(jnp.float32)
    picked = jnp.sum(chosen_float * logits[:, None, :], axis=-1)
    picked = picked - jnp.max(picked, axis=-1, keepdims=True)
    raised = jnp.exp(picked)
    gates = raised / jnp.sum(raised, axis=-1, keepdims=True)
    counts = jnp.sum(chosen.astype(jnp.int32), axis=1)
    before = jnp.cumsum(counts, axis=0) - counts
    slots = jnp.sum(chosen.astype(jnp.int32) * before[:, None, :], axis=-1)
    targets = route_rows * capacity + slots
    placing = (
        jnp.transpose(targets)[:, :, None] == jnp.arange(total_experts * capacity)[None, None, :]
    ).astype(jnp.bfloat16)
    dispatch_hot = jnp.sum(placing, axis=0)
    buffer = (
        contract("mr,md->rd", dispatch_hot, entry_two)
        .astype(jnp.bfloat16)
        .reshape(total_experts, capacity, width)
    )
    received = lax.all_to_all(buffer, EXPERTS, split_axis=0, concat_axis=1, tiled=True)
    gate_part = contract("erd,edf->erf", received, expert_gate)
    up_part = contract("erd,edf->erf", received, expert_up)
    hidden = (gate_part * jax.nn.sigmoid(gate_part) * up_part).astype(jnp.bfloat16)
    produced = contract("erf,efd->erd", hidden, expert_down).astype(jnp.bfloat16)
    shared_gate_part = matmul(entry_two, shared_gate)
    shared_up_part = matmul(entry_two, shared_up)
    shared_hidden = (shared_gate_part * jax.nn.sigmoid(shared_gate_part) * shared_up_part).astype(
        jnp.bfloat16
    )
    shared_out = matmul(shared_hidden, shared_down)
    returned = lax.all_to_all(produced, EXPERTS, split_axis=1, concat_axis=0, tiled=True).reshape(
        total_experts * capacity, width
    )
    picked_rows = contract("kmr,rd->kmd", placing, returned)
    mixed = jnp.sum(jnp.transpose(gates)[:, :, None] * picked_rows, axis=0)
    result = (middle + mixed + shared_out).astype(jnp.bfloat16)
    output = jnp.swapaxes(result.reshape(span, seqs, width), 0, 1)
    grad_low = jnp.swapaxes(cotangent, 0, 1).reshape(rows, width)
    grad_out = grad_low.astype(jnp.float32)
    grad_gates = jnp.transpose(jnp.sum(picked_rows * grad_out[None], axis=-1))
    grad_rows = (jnp.transpose(gates)[:, :, None] * grad_out[None]).astype(jnp.bfloat16)
    grad_slots = (
        contract("kmr,kmd->rd", placing, grad_rows)
        .astype(jnp.bfloat16)
        .reshape(total_experts, capacity, width)
    )
    grad_produced = lax.all_to_all(grad_slots, EXPERTS, split_axis=0, concat_axis=1, tiled=True)
    expert_down_term = contract("erf,erd->efd", hidden, grad_produced)
    grad_hidden = contract("erd,efd->erf", grad_produced, expert_down)
    grad_gate_part, grad_up_part = silu_back(grad_hidden, gate_part, up_part)
    expert_gate_term = contract("erd,erf->edf", received, grad_gate_part)
    expert_up_term = contract("erd,erf->edf", received, grad_up_part)
    grad_received = (
        contract("erf,edf->erd", grad_gate_part, expert_gate)
        + contract("erf,edf->erd", grad_up_part, expert_up)
    ).astype(jnp.bfloat16)
    expert_parts = None
    shared_down_term = contract("mf,md->fd", shared_hidden, grad_low)
    grad_shared_hidden = contract("md,fd->mf", grad_low, shared_down)
    grad_shared_gate, grad_shared_up = silu_back(
        grad_shared_hidden, shared_gate_part, shared_up_part
    )
    shared_gate_term = contract("md,mf->df", entry_two, grad_shared_gate)
    shared_up_term = contract("md,mf->df", entry_two, grad_shared_up)
    grad_entry_two = contract("mf,df->md", grad_shared_gate, shared_gate) + contract(
        "mf,df->md", grad_shared_up, shared_up
    )
    grad_pick = gates * (grad_gates - jnp.sum(gates * grad_gates, axis=-1, keepdims=True))
    grad_logits = jnp.sum(chosen_float * grad_pick[:, :, None], axis=1)
    router_term = jnp.einsum(
        "md,me->de", entry_two.astype(jnp.float32), grad_logits, precision=highest
    )
    grad_entry_two = grad_entry_two + jnp.einsum(
        "me,de->md", grad_logits, router_weight.astype(jnp.float32), precision=highest
    )
    grad_returned = lax.all_to_all(
        grad_received, EXPERTS, split_axis=1, concat_axis=0, tiled=True
    ).reshape(total_experts * capacity, width)
    grad_entry_two = grad_entry_two + contract("mr,rd->md", dispatch_hot, grad_returned)
    grad_middle_norm, norm2_term = norm_back(grad_entry_two, normed_two, factor_two, norm2_gain)
    grad_middle = grad_out + grad_middle_norm
    grad_attn = grad_middle.astype(jnp.bfloat16)
    out_term = contract("md,me->de", context_low, grad_attn)
    grad_ctx = (
        contract("me,de->md", grad_attn, out_weight)
        .astype(jnp.bfloat16)
        .reshape(span, seqs, heads, HEAD_DIM)
    )
    delta = jnp.transpose(jnp.sum(grad_ctx.astype(jnp.float32) * context, axis=-1), (1, 2, 0))
    keys_all, values_all = (
        lax.all_gather(keys_local, CONTEXT, axis=0, tiled=True),
        lax.all_gather(values_local, CONTEXT, axis=0, tiled=True),
    )
    grad_queries = query_grads(
        queries, query_block, grad_ctx, delta, log_total, keys_all, values_all
    ) * HEAD_DIM ** (-0.5)
    delta_rows = jnp.transpose(delta, (2, 0, 1))
    log_rows = jnp.transpose(log_total, (2, 0, 1))
    pull_step = partial(query_side_fold, keys_local, values_local, key_start)
    empty_grads = jnp.zeros((span, seqs, 2 * width), jnp.float32)
    grad_kv = pull_step(
        empty_grads,
        (
            lax.all_gather(queries, CONTEXT, axis=0, tiled=True),
            lax.all_gather(grad_ctx, CONTEXT, axis=0, tiled=True),
            lax.all_gather(delta_rows.astype(jnp.bfloat16), CONTEXT, axis=0, tiled=True).astype(
                jnp.float32
            ),
            lax.all_gather(log_rows.astype(jnp.bfloat16), CONTEXT, axis=0, tiled=True).astype(
                jnp.float32
            ),
        ),
        jnp.int32(0),
    )
    grad_keys = grad_kv[..., :width].reshape(span, seqs, heads, HEAD_DIM)
    grad_values = grad_kv[..., width:].reshape(span, seqs, heads, HEAD_DIM)
    grad_projected = jnp.stack(
        [
            rotate_back(grad_queries, cosine, sine),
            rotate_back(grad_keys, cosine, sine),
            grad_values,
        ],
        axis=2,
    )
    grad_projected = grad_projected.astype(jnp.bfloat16).reshape(rows, 3 * width)
    qkv_term = contract("md,me->de", entry_one, grad_projected)
    grad_entry_one = contract("me,de->md", grad_projected, qkv_weight)
    grad_local_norm, norm1_term = norm_back(grad_entry_one, normed_one, factor_one, norm1_gain)
    input_grad = jnp.swapaxes((grad_middle + grad_local_norm).reshape(span, seqs, width), 0, 1)
    expert_parts = reduce_experts(expert_gate_term, expert_up_term, expert_down_term)
    spread = (
        lax.psum_scatter(norm1_term, (DP, CONTEXT), scatter_dimension=0, tiled=True),
        lax.psum_scatter(qkv_term, (DP, CONTEXT), scatter_dimension=0, tiled=True),
        lax.psum_scatter(out_term, (DP, CONTEXT), scatter_dimension=0, tiled=True),
        lax.psum_scatter(norm2_term, (DP, CONTEXT), scatter_dimension=0, tiled=True),
        lax.psum_scatter(router_term, (DP, CONTEXT), scatter_dimension=0, tiled=True),
        lax.psum_scatter(shared_gate_term, (DP, CONTEXT), scatter_dimension=0, tiled=True),
        lax.psum_scatter(shared_up_term, (DP, CONTEXT), scatter_dimension=0, tiled=True),
        lax.psum_scatter(shared_down_term, (DP, CONTEXT), scatter_dimension=0, tiled=True),
    )
    (
        norm1_part,
        qkv_part,
        out_part,
        norm2_part,
        router_part,
        shared_gate_piece,
        shared_up_piece,
        shared_down_piece,
    ) = spread
    summed = (
        lax.psum(norm1_part.astype(jnp.bfloat16), EXPERTS).astype(jnp.float32),
        lax.psum(qkv_part.astype(jnp.bfloat16), EXPERTS).astype(jnp.float32),
        lax.psum(out_part.astype(jnp.bfloat16), EXPERTS).astype(jnp.float32),
        lax.psum(norm2_part.astype(jnp.bfloat16), EXPERTS).astype(jnp.float32),
        lax.psum(router_part.astype(jnp.bfloat16), EXPERTS).astype(jnp.float32),
        lax.psum(shared_gate_piece.astype(jnp.bfloat16), EXPERTS).astype(jnp.float32),
        lax.psum(shared_up_piece.astype(jnp.bfloat16), EXPERTS).astype(jnp.float32),
        lax.psum(shared_down_piece.astype(jnp.bfloat16), EXPERTS).astype(jnp.float32),
    )
    return (
        output,
        input_grad,
        summed[0],
        summed[1],
        summed[2],
        summed[3],
        summed[4],
        expert_parts[0],
        expert_parts[1],
        expert_parts[2],
        summed[5],
        summed[6],
        summed[7],
    )


group = (DP, EXPERTS)
keep_masks = (0, 1, 4, 5)
all_masks = keep_masks + tuple(mask ^ 2 for mask in keep_masks)
f32 = jnp.float32
bf16 = jnp.bfloat16
far, copied, held = range(3)


def dot_nn(left, right):
    return lax.dot_general(left, right, (((1,), (0,)), ((), ())), preferred_element_type=f32)


def dot_nt(left, right):
    return lax.dot_general(left, right, (((1,), (1,)), ((), ())), preferred_element_type=f32)


def dot_tn(left, right):
    return lax.dot_general(left, right, (((0,), (0,)), ((), ())), preferred_element_type=f32)


def spin(field, cosine, sine_up, sine_down):
    up = pltpu.roll(field, 32, 1)
    down = pltpu.roll(field, 96, 1)
    return field * cosine + up * sine_up + down * sine_down


def spin_back(grad, cosine, sine_up, sine_down):
    up = pltpu.roll(grad, 32, 1)
    down = pltpu.roll(grad, 96, 1)
    return grad * cosine - up * sine_up - down * sine_down


def spin_tables(length):
    lane = np.arange(128)
    freqs = 10000.0 ** (-2.0 * (lane % 32) / HEAD_DIM)
    angles = np.arange(length)[:, None] * freqs[None, :]
    second = (lane % HEAD_DIM) >= HEAD_DIM // 2
    sine = np.sin(angles)
    tables = (np.cos(angles), np.where(second, sine, 0.0), np.where(second, 0.0, -sine))
    return [jnp.asarray(table, f32) for table in tables]


def lane_half(rows):
    return lax.broadcasted_iota(jnp.int32, (rows, 128), 1) // HEAD_DIM


def key_bias(blocks, rows, here):
    block = lax.broadcasted_iota(jnp.int32, (1, blocks * rows), 1) // rows
    return jnp.where(block <= here, 0.0, masked_score)


class Copies:
    def __init__(self, sems):
        self.sems, self.count = sems, 0

    def start(self, source, target):
        copy = pltpu.make_async_copy(source, target, self.sems.at[self.count])
        self.count += 1
        copy.start()
        return copy


def attend_kernel(blocks, place, *refs):
    tokens = refs[:blocks]
    (routes, gain1, qkv_w, out_w, gain2, cos_hbm, up_hbm, down_hbm) = refs[blocks:blocks + 8]
    (entry_hbm, queries_hbm, keys_hbm, values_hbm, log_hbm, context_hbm, middle, entry_two) = refs[
        blocks + 8:blocks + 16
    ]
    (cos, sin_up, sin_down, entry, queries, keys, values, log_total, context, sems) = refs[blocks + 16:]
    rows, width = middle.shape
    pairs = width // 128
    here = place[0]
    copies = Copies(sems)
    tables_in = []
    for r in range(blocks):
        block = pl.ds(pl.multiple_of(jnp.maximum(here - r, 0) * rows, rows), rows)
        for source, target in ((cos_hbm, cos), (up_hbm, sin_up), (down_hbm, sin_down)):
            tables_in.append(copies.start(source.at[block], target.at[r * rows:(r + 1) * rows]))

    for r in range(blocks):
        x = tokens[r][...].astype(f32)
        factor = lax.rsqrt(jnp.mean(x * x, axis=-1, keepdims=True) + norm_eps)
        entry[r * rows:(r + 1) * rows, :] = (x * factor * gain1[...]).astype(bf16)
    outs = [copies.start(entry, entry_hbm)]
    for copy in tables_in:
        copy.wait()

    tile = 384
    for start in range(0, width, tile):
        part = dot_nn(entry[:rows, :], qkv_w[:, start:start + tile])
        for lane in range(0, tile, 128):
            queries[:, start + lane:start + lane + 128] = spin(
                part[:, lane:lane + 128], cos[:rows, :], sin_up[:rows, :], sin_down[:rows, :]
            ).astype(bf16)
    for start in range(0, width, tile):
        part = dot_nn(entry[...], qkv_w[:, width + start:width + start + tile])
        for lane in range(0, tile, 128):
            keys[:, start + lane:start + lane + 128] = spin(
                part[:, lane:lane + 128], cos[...], sin_up[...], sin_down[...]
            ).astype(bf16)
        values[:, start:start + tile] = dot_nn(
            entry[...], qkv_w[:, 2 * width + start:2 * width + start + tile]
        ).astype(bf16)
    outs += [copies.start(queries, queries_hbm), copies.start(keys, keys_hbm), copies.start(values, values_hbm)]
    half = lane_half(rows)
    bias = key_bias(blocks, rows, here)

    def attend(pair, carry):
        lanes = pl.ds(pl.multiple_of(pair * 128, 128), 128)
        both = queries[:, lanes] * HEAD_DIM ** (-0.5)
        results, logs = [], []
        for head in range(2):
            query = jnp.where(half == head, both, jnp.zeros_like(both))
            scores = dot_nt(query, keys[:, lanes]) + bias
            best = jnp.max(scores, axis=-1, keepdims=True)
            weights = jnp.exp(scores - best)
            total = jnp.sum(weights, axis=-1, keepdims=True)
            results.append(dot_nn(weights.astype(bf16), values[:, lanes]) / total)
            logs.append(best + jnp.log(total))
        context[:, lanes] = jnp.where(half == 0, results[0], results[1]).astype(bf16)
        log_total[pair] = jnp.where(half == 0, logs[0], logs[1])
        return carry

    lax.fori_loop(0, pairs, attend, 0)
    outs += [copies.start(log_total, log_hbm), copies.start(context, context_hbm)]
    mid = tokens[0][...].astype(f32) + dot_nn(context[...], out_w[...])
    middle[...] = mid
    factor = lax.rsqrt(jnp.mean(mid * mid, axis=-1, keepdims=True) + norm_eps)
    entry_two[:rows, :] = (mid * factor * gain2[...]).astype(bf16)
    entry_two[rows:, :] = jnp.zeros((entry_two.shape[0] - rows, width), bf16)
    entry_two[rows:rows + 8, :rows] = jnp.concatenate(
        [routes[...].astype(f32), jnp.zeros((8 - routes.shape[0], rows), f32)], axis=0
    ).astype(bf16)
    for copy in outs:
        copy.wait()


def pick_kernel(n_context, place, gate, up, down, gate_out, up_out, down_out):
    side = place[5]
    lane = lax.broadcasted_iota(jnp.int32, (gate.shape[0], 128), 1)
    for source, target in ((gate, gate_out), (up, up_out)):
        for z in range(0, n_context, 2):
            one = source[:, z * 128:(z + 1) * 128].astype(f32)
            two = source[:, (z + 1) * 128:(z + 2) * 128].astype(f32)
            left = jnp.where(side == 0, one, pltpu.roll(one, 64, 1))
            right = jnp.where(side == 0, pltpu.roll(two, 64, 1), two)
            target[:, z * 64:z * 64 + 128] = jnp.where(lane < 64, left, right).astype(bf16)
    for z in range(n_context):
        start = pl.multiple_of(z * 128 + side * 64, 64)
        down_out[z * 64:(z + 1) * 64, :] = down[pl.ds(start, 64), :]


def sum_kernel(n_context, counts, place, *refs):
    outs = refs[-n_context:]
    here = place[6]
    piece = outs[0].shape[0]
    for r, out in enumerate(outs):
        block = lax.rem(here + r, n_context)
        rows = pl.ds(pl.multiple_of(block * piece, piece), piece)
        first, start = 0, 0
        for count in counts:
            total = refs[first][rows, :].astype(f32)
            for value in refs[first + 1:first + count]:
                total = total + value[rows, :].astype(f32)
            out[:, start:start + total.shape[1]] = total.astype(bf16)
            first, start = first + count, start + total.shape[1]


def silu_parts(gate_part, up_part):
    sigmoid_value = jax.nn.sigmoid(gate_part)
    active = gate_part * sigmoid_value
    return sigmoid_value, active, (active * up_part).astype(bf16)


def silu_grads(grad_hidden, gate_part, up_part, sigmoid_value, active):
    grad_gate = grad_hidden * up_part * sigmoid_value * (1.0 + gate_part * (1.0 - sigmoid_value))
    return grad_gate.astype(bf16), (grad_hidden * active).astype(bf16)


def feed_kernel(masks, n_context, n_dp, layout, place, *refs):
    inputs = refs[:8]
    (cot_hbm, router, router_t, gate_s_hbm, up_s_hbm, down_s_hbm, gate_hbm, up_hbm, down_hbm) = refs[8:17]
    (grad_keep_hbm, grad_send_hbm, mix_keep_hbm, mix_send_hbm, router_grad, bundle_hbm) = refs[17:23]
    (
        aux, hots, x_all, dz_all, g_all, produced, received, field, cot, gate_w, up_w, down_w, gate_s_w, up_s_w,
        down_s_w, hidden, dgate, dup, hidden_s, dgate_s, dup_s, grad_tokens, mix_tokens, bundle, notes, sems,
    ) = refs[23:]
    index, dp, expert, core, chip = place[0], place[1], place[2], place[3], place[4]
    rows = cot.shape[0] // 8
    width = field.shape[1]
    slots = hots.shape[1]
    copies = Copies(sems)
    ins = []
    for i in range(8):
        rows_of = slice(i * rows, (i + 1) * rows)
        ins.append((
            copies.start(inputs[i].at[rows:], notes.at[i]),
            copies.start(inputs[i].at[:rows], field.at[rows_of]),
            copies.start(cot_hbm.at[lax.bitwise_xor(index, masks[i])], cot.at[rows_of]),
        ))
    columns = layout.blocks * 128
    weights_in = []
    for run in range(2):
        part = pl.ds(pl.multiple_of((2 * chip + run) * columns, columns), columns)
        weights_in.append([
            copies.start(gate_hbm.at[core, :, part], gate_w.at[run]),
            copies.start(up_hbm.at[core, :, part], up_w.at[run]),
            copies.start(down_hbm.at[core, part, :], down_w.at[run]),
        ])
    shared_in = [
        copies.start(source, target)
        for source, target in ((gate_s_hbm, gate_s_w), (up_s_hbm, up_s_w), (down_s_hbm, down_s_w))
    ]

    lanes = lax.broadcasted_iota(jnp.int32, (slots, 128), 1)
    mine = (lanes == expert).astype(f32)
    expert_row = expert.astype(f32)
    before = (
        lax.broadcasted_iota(jnp.int32, (rows, rows), 0) < lax.broadcasted_iota(jnp.int32, (rows, rows), 1)
    ).astype(bf16)
    slot_of = lax.broadcasted_iota(jnp.int32, (slots, rows), 0).astype(f32)
    for i in range(8):
        rows_of = slice(i * rows, (i + 1) * rows)
        slots_of = slice(i * slots, (i + 1) * slots)
        if i % 4 == 0:
            for copy in sum(ins[i:i + 4], ()):
                copy.wait()
        routes = notes[i, :, :rows].astype(f32)
        first, second = routes[0:1, :], routes[1:2, :]
        named = jnp.logical_or(first == expert_row, second == expert_row).astype(f32)
        slot = dot_nn(jnp.broadcast_to(named, (16, rows)).astype(bf16), before)[0:1, :]
        hot_f = jnp.where(slot_of == slot, named, 0.0)
        partner = jnp.where(first == expert_row, second, first)
        other = jnp.sum(hot_f * partner, axis=-1, keepdims=True)
        hot = hot_f.astype(bf16)
        hots[i] = hot
        x = dot_nn(hot, field[rows_of, :]).astype(bf16)
        x_all[slots_of, :] = x
        g_slot = dot_nn(hot, cot[rows_of, :])
        logits = dot_nn(x, router[...])
        theirs = (lanes.astype(f32) == other).astype(f32)
        gate = jax.nn.sigmoid(jnp.sum((mine - theirs) * logits, axis=-1, keepdims=True))
        dz_all[slots_of, :] = (gate * g_slot).astype(bf16)
        g_all[slots_of, :] = g_slot.astype(bf16)
        aux[slots_of, :] = jnp.where(lanes == 64, gate, gate * (1.0 - gate) * (mine - theirs))

    tile = x_all.shape[0] // 2
    for run in range(2):
        for copy in weights_in[run]:
            copy.wait()
        for t in range(2):
            part = slice(t * tile, (t + 1) * tile)
            gate_part = dot_nn(x_all[part, :], gate_w[run])
            up_part = dot_nn(x_all[part, :], up_w[run])
            sigmoid_value, active, u = silu_parts(gate_part, up_part)
            hidden[part, :] = u
            out = dot_nn(u, down_w[run])
            grad_hidden = dot_nt(dz_all[part, :], down_w[run])
            da, db = silu_grads(grad_hidden, gate_part, up_part, sigmoid_value, active)
            dgate[part, :] = da
            dup[part, :] = db
            grad = dot_nt(da, gate_w[run]) + dot_nt(db, up_w[run])
            if run == 0:
                produced[part, :] = out
                received[part, :] = grad
            else:
                produced[part, :] += out
                received[part, :] += grad
        expert_grads(bundle, x_all, dz_all, hidden, dgate, dup, layout, run, dp, n_context, n_dp)

    for copy in shared_in:
        copy.wait()
    router_sum = jnp.zeros((width, 128), f32)
    outs, last = [], {}
    for t in range(4):
        tile = slice(2 * t * rows, 2 * (t + 1) * rows)
        gate_part = dot_nn(field[tile, :], gate_s_w[...])
        up_part = dot_nn(field[tile, :], up_s_w[...])
        sigmoid_value, active, u = silu_parts(gate_part, up_part)
        hidden_s[tile, :] = u
        mixed = dot_nn(u, down_s_w[...])
        grad_hidden = dot_nt(cot[tile, :], down_s_w[...])
        da, db = silu_grads(grad_hidden, gate_part, up_part, sigmoid_value, active)
        dgate_s[tile, :] = da
        dup_s[tile, :] = db
        grad_in = dot_nt(da, gate_s_w[...]) + dot_nt(db, up_s_w[...])
        for copy in last.pop(t - 2, []):
            copy.wait()
        for half in range(2):
            i = 2 * t + half
            rows_of = slice(half * rows, (half + 1) * rows)
            slots_of = slice(i * slots, (i + 1) * slots)
            z = produced[slots_of, :]
            extra = aux[slots_of, :]
            gate = extra[:, 64:65]
            pick = jnp.sum(z.astype(bf16).astype(f32) * g_all[slots_of, :].astype(f32), axis=-1, keepdims=True)
            dlogits = (jnp.where(lanes < 64, extra, 0.0) * pick).astype(bf16)
            router_sum = router_sum + dot_tn(x_all[slots_of, :], dlogits)
            grad = (received[slots_of, :] + dot_nn(dlogits, router_t[...])).astype(bf16)
            back = dot_tn(hots[i], jnp.concatenate([grad, (gate * z).astype(bf16)], axis=1))
            slot = (2 * t + half) % 4
            grad_tokens[slot] = (grad_in[rows_of, :] + back[:, :width]).astype(bf16)
            mix_tokens[slot] = (mixed[rows_of, :] + back[:, width:]).astype(bf16)
        last[t] = []
        for half in range(2):
            i = 2 * t + half
            for source, targets in (
                (grad_tokens, (grad_keep_hbm, grad_send_hbm)), (mix_tokens, (mix_keep_hbm, mix_send_hbm))
            ):
                last[t].append(copies.start(source.at[i % 4], targets[i // 4].at[i % 4]))
    router_grad[...] = router_sum

    for mat, source in enumerate((dgate_s, dup_s)):
        offset = mat * layout.shared_blocks * layout.piece
        matrix_grads(bundle, field, source, offset, layout, dp, n_context, n_dp)
    outs += [
        copies.start(bundle.at[start:start + layout.shared_down_at], bundle_hbm.at[start:start + layout.shared_down_at])
        for start in range(0, n_context * layout.total, layout.total)
    ]
    grad = dot_tn(hidden_s[...], cot[...]).astype(bf16)
    down_rows = layout.down_rows
    for z in range(n_context):
        for lane in range(width // 128):
            start = z * layout.total + layout.shared_down_at + lane * down_rows
            bundle[start:start + down_rows, :] = grad[z * down_rows:(z + 1) * down_rows, lane * 128:(lane + 1) * 128]
    for z in range(n_context):
        part = slice(z * layout.total + layout.shared_down_at, (z + 1) * layout.total)
        outs.append(copies.start(bundle.at[part], bundle_hbm.at[part]))
    for copy in sum(last.values(), outs):
        copy.wait()


def matrix_grads(bundle, left, right, offset, layout, dp, n_context, n_dp):
    block = left.shape[1] // n_dp
    piece = block // n_context
    tile = 2 * block
    for t in range(n_dp // 2):
        grad = dot_tn(left[:, t * tile:(t + 1) * tile], right[...]).astype(bf16)
        for half in range(2):
            slab = lax.bitwise_xor(2 * t + half, dp) * layout.place
            for z in range(n_context):
                for lane in range(grad.shape[1] // 128):
                    start = z * layout.total + slab + offset + lane * piece
                    bundle[pl.ds(pl.multiple_of(start, 16), piece), :] = grad[
                        half * block + z * piece:half * block + (z + 1) * piece, lane * 128:(lane + 1) * 128
                    ]


def expert_grads(bundle, x, dz, hidden, dgate, dup, layout, run, dp, n_context, n_dp):
    width = x.shape[1]
    tile = 2 * width // n_dp
    for mat, source in enumerate((dgate, dup)):
        offset = layout.shared_place + run * layout.run_place + mat * layout.blocks * layout.piece
        matrix_grads(bundle, x, source, offset, layout, dp, n_context, n_dp)
    for t in range(n_dp // 2):
        grad = dot_tn(dz[:, t * tile:(t + 1) * tile], hidden[...]).astype(bf16)
        for z in range(n_context):
            start = z * layout.total + layout.down_at + run * width + t * tile
            bundle[start:start + tile, :] = grad[:, z * 128:(z + 1) * 128]


class Layout:
    def __init__(self, width, hidden, n_dp, n_context):
        self.piece = width // n_dp // n_context
        self.shared_blocks, self.blocks = hidden // 8 // 128, hidden // 4 // 128
        self.shared_place = 2 * self.shared_blocks * self.piece
        self.run_place = 2 * self.blocks * self.piece
        self.place = self.shared_place + 2 * self.run_place
        self.shared_down_at = n_dp * self.place
        self.down_rows = hidden // 8 // n_context
        self.down_at = self.shared_down_at + self.down_rows * (width // 128)
        self.total = self.down_at + 2 * width


def feed_grads_kernel(n_dp, layout, place, *refs):
    refs = list(refs)

    def take(count):
        part = refs[:count]
        del refs[:count]
        return part

    slabs = take(n_dp)
    shared_far = take(n_dp)
    downs = take(1)[0]
    got_downs = take(2)
    (gate, up, down, gate_s, up_s, down_s) = refs
    dp, side = place[1], place[5]
    core = place[3]
    piece = layout.piece
    hidden = gate.shape[2]
    columns = layout.blocks * 128
    width = down.shape[2]

    for mask in range(n_dp):
        source = lax.bitwise_xor(dp, mask)
        which = lax.bitwise_and(source, 1)
        for run in range(2):
            begin = (source // 2) * (2 * columns) + run * columns
            for mat, target in enumerate((gate, up)):
                for lane in range(layout.blocks):
                    start = layout.shared_place + run * layout.run_place + (mat * layout.blocks + lane) * piece
                    target[which, :, pl.ds(pl.multiple_of(begin + lane * 128, 128), 128)] = slabs[mask][
                        start:start + piece, :
                    ].astype(f32)
    base = layout.down_at - layout.shared_down_at
    kept = jnp.where(core == 0, downs[base:base + width, :], downs[base + width:, :])
    got = jnp.where(core == 0, got_downs[0][...], got_downs[1][...])
    down[core] = kept.astype(f32).T
    down[1 - core] = got.astype(f32).T

    lane_of = lax.broadcasted_iota(jnp.int32, (piece, 128), 1)
    for mask in range(n_dp):
        source = lax.bitwise_xor(dp, mask)
        for mat, target in enumerate((gate_s, up_s)):
            for lane in range(layout.shared_blocks):
                start = (mat * layout.shared_blocks + lane) * piece
                own = slabs[mask][start:start + piece, :].astype(f32)
                far = shared_far[mask][start:start + piece, :].astype(f32)
                first = jnp.where(side == 0, own, far)
                second = jnp.where(side == 0, far, own)
                begin = source * (hidden // n_dp) + lane * 256
                target[:, pl.ds(pl.multiple_of(begin, 128), 128)] = jnp.where(
                    lane_of < 64, first, pltpu.roll(second, 64, 1)
                )
                target[:, pl.ds(pl.multiple_of(begin + 128, 128), 128)] = jnp.where(
                    lane_of < 64, pltpu.roll(first, 64, 1), second
                )
    down_rows = layout.down_rows
    for lane in range(width // 128):
        rows = slice(lane * down_rows, (lane + 1) * down_rows)
        far_rows = slice(layout.shared_place + rows.start, layout.shared_place + rows.stop)
        lanes = slice(lane * 128, (lane + 1) * 128)
        down_s[pl.ds(pl.multiple_of(side * down_rows, 16), down_rows), lanes] = downs[rows, :].astype(f32)
        down_s[pl.ds(pl.multiple_of((1 - side) * down_rows, 16), down_rows), lanes] = shared_far[0][
            far_rows, :
        ].astype(f32)


def last_kernel(blocks, place, *refs):
    packs, (token, gain1, grad_own, grad_middle) = refs[:2], refs[2:6]
    pulled = refs[6:4 + blocks]
    (input_grad, qkv, out, norm1, norm2, router) = refs[4 + blocks:]
    side = place[5]
    piece, width = out.shape
    own, far_half = packs[0][...].astype(f32), packs[1][...].astype(f32)
    whole, start = [], 0
    for columns in ((3 * width // 2 + width + 128) // 2, (3 * width // 2 + 128) // 2):
        here, there = own[:, start:start + columns], far_half[:, start:start + columns]
        whole.append(jnp.concatenate([jnp.where(side == 0, here, there), jnp.where(side == 0, there, here)], axis=1))
        start += columns
    tile = width // 2
    for mat in range(3):
        for half in range(2):
            qkv[:, mat * width + half * tile:mat * width + (half + 1) * tile] = whole[half][
                :, mat * tile:(mat + 1) * tile
            ]
    out[...] = whole[0][:, 3 * tile:3 * tile + width]
    small = whole[1][:, 3 * tile:3 * tile + 128]
    small = jnp.concatenate([small, jnp.zeros((128 - piece, 128), f32)], axis=0).T
    router[...] = small[:router.shape[0], :piece]
    norm2[...] = small[8:9, :piece]
    norm1[...] = small[9:10, :piece]

    x = token[...].astype(f32)
    factor = lax.rsqrt(jnp.mean(x * x, axis=-1, keepdims=True) + norm_eps)
    normed = x * factor
    grad_entry = grad_own[...]
    for part in pulled:
        grad_entry = grad_entry + part[...].astype(f32)
    grad_norm = grad_entry * gain1[...]
    inner = jnp.mean(grad_norm * normed, axis=-1, keepdims=True)
    input_grad[...] = grad_middle[...] + factor * (grad_norm - normed * inner)


def load_turns(copies, sources, targets, blocks, rows, here):
    started = []
    for r in range(blocks):
        block = pl.ds(pl.multiple_of(jnp.maximum(here - r, 0) * rows, rows), rows)
        for source, target in zip(sources, targets):
            started.append(copies.start(source.at[block], target.at[r * rows:(r + 1) * rows]))
    return started


def attend_back(first, pairs, bias, queries, keys, values, log_total, grad_ctx, turns, grad_q, grad_kv):
    cos, sin_up, sin_down = turns
    rows = queries.shape[0]
    width = queries.shape[1]
    scale = HEAD_DIM ** (-0.5)
    half = lane_half(rows)

    def attend(pair, carry):
        lanes = pl.ds(pl.multiple_of(pair * 128, 128), 128)
        both_q = queries[:, lanes] * scale
        both_g = grad_ctx[:, pl.ds(pl.multiple_of((first + pair) * 128, 128), 128)]
        both_l = log_total[pair]
        dq = dk = dv = None
        for head in range(2):
            query = jnp.where(half == head, both_q, jnp.zeros_like(both_q))
            grad = jnp.where(half == head, both_g, jnp.zeros_like(both_g))
            log_row = both_l[:, head * HEAD_DIM:head * HEAD_DIM + 1]
            prob = jnp.exp(dot_nt(query, keys[:, lanes]) + bias - log_row)
            grad_prob = dot_nt(grad, values[:, lanes])
            delta = jnp.sum(prob * grad_prob, axis=-1, keepdims=True)
            grad_score = (prob * (grad_prob - delta)).astype(bf16)
            dq_head = dot_nn(grad_score, keys[:, lanes])
            dk_head = dot_tn(grad_score, query)
            dv_head = dot_tn(prob.astype(bf16), grad)
            if head == 0:
                dq, dk, dv = dq_head, dk_head, dv_head
            else:
                dq, dk, dv = jnp.where(half == 0, dq, dq_head), dk + dk_head, dv + dv_head
        grad_q[:, lanes] = spin_back(dq * scale, cos[:rows, :], sin_up[:rows, :], sin_down[:rows, :]).astype(bf16)
        far_lanes = pl.ds(pl.multiple_of(width + pair * 128, 128), 128)
        grad_kv[:, lanes] = spin_back(dk, cos[...], sin_up[...], sin_down[...]).astype(bf16)
        grad_kv[:, far_lanes] = dv.astype(bf16)
        return carry

    lax.fori_loop(0, pairs, attend, 0)


def store_pack(keep, send, value, start, dp, side, n_dp):
    n_half = keep.shape[-1]
    block = value.shape[0] // n_dp
    if start < n_half < start + value.shape[1]:
        store_pack(keep, send, value[:, :n_half - start], start, dp, side, n_dp)
        store_pack(keep, send, value[:, n_half - start:], n_half, dp, side, n_dp)
        return
    side_of = start // n_half
    lanes = slice(start - side_of * n_half, start - side_of * n_half + value.shape[1])
    flip_side = lax.bitwise_xor(side_of, side)
    for part in range(n_dp):
        piece = value[part * block:(part + 1) * block, :].astype(bf16)
        flip = lax.bitwise_xor(part, dp)

        @pl.when(lax.bitwise_and(flip, 1) == 0)
        def _():
            keep[flip // 2, flip_side, :, lanes] = piece

        @pl.when(lax.bitwise_and(flip, 1) == 1)
        def _():
            send[flip // 2, flip_side, :, lanes] = piece


def back_kernel(blocks, n_dp, place, *refs):
    parts = refs[:4]
    (
        middle, cot, gain2, out_w, queries_hbm, keys_hbm, values_hbm, log_hbm, context_hbm, entry_hbm, *turns_hbm
    ) = refs[4:17]
    (grad_middle, grad_ctx, grad_q, grad_kv, notes, keep, send) = refs[17:24]
    (queries, keys, values, log_total, context, entry, cos, sin_up, sin_down, sems) = refs[24:]
    rows, width = middle.shape
    here, dp, side = place[6], place[1], place[5]
    copies = Copies(sems)
    part = slice(0, queries.shape[1])
    turns = (cos, sin_up, sin_down)
    first_in = [
        copies.start(source, target)
        for source, target in (
            (queries_hbm.at[:, part], queries), (keys_hbm.at[:, part], keys), (values_hbm.at[:, part], values),
            (log_hbm.at[:log_total.shape[0]], log_total),
        )
    ]
    first_in += load_turns(copies, turns_hbm, turns, blocks, rows, here)
    late_in = [copies.start(context_hbm, context), copies.start(entry_hbm, entry)]

    grad_two = parts[0][...].astype(f32)
    for value in parts[1:]:
        grad_two = grad_two + value[...].astype(f32)
    mid = middle[...]
    factor = lax.rsqrt(jnp.mean(mid * mid, axis=-1, keepdims=True) + norm_eps)
    normed = mid * factor
    notes[...] = jnp.zeros_like(notes)
    notes[0:1, :] = jnp.sum(grad_two * normed, axis=0, keepdims=True)
    grad_norm = grad_two * gain2[...]
    inner = jnp.mean(grad_norm * normed, axis=-1, keepdims=True)
    grad_mid = cot[...].astype(f32) + factor * (grad_norm - normed * inner)
    grad_middle[...] = grad_mid
    grad_attn = grad_mid.astype(bf16)
    grad_ctx[...] = dot_nt(grad_attn, out_w[...]).astype(bf16)
    for copy in first_in:
        copy.wait()
    attend_back(
        0, log_total.shape[0], key_bias(blocks, rows, here), queries, keys, values, log_total, grad_ctx, turns, grad_q,
        grad_kv,
    )
    for copy in late_in:
        copy.wait()
    tile = queries.shape[1]
    store_pack(keep, send, dot_tn(entry[:rows, :], grad_q[...]), 0, dp, side, n_dp)
    for mat in range(2):
        grad = dot_tn(entry[...], grad_kv[:, mat * tile:(mat + 1) * tile])
        store_pack(keep, send, grad, (1 + mat) * tile, dp, side, n_dp)
    for start in range(0, width, tile):
        store_pack(keep, send, dot_tn(context[...], grad_attn[:, start:start + tile]), 3 * tile + start, dp, side, n_dp)
    used = 3 * tile + width
    store_pack(keep, send, jnp.zeros((width, 2 * keep.shape[-1] - used), f32), used, dp, side, n_dp)


def rest_kernel(blocks, n_dp, place, *refs):
    tokens_hbm = refs[:blocks]
    (notes, router_part, grad_ctx) = refs[blocks:blocks + 3]
    (
        queries_hbm, keys_hbm, values_hbm, log_hbm, entry_hbm, qkv_hbm, grad_q_hbm, grad_kv_hbm, *turns_hbm
    ) = refs[blocks + 3:blocks + 14]
    outs = refs[blocks + 14:]
    grad_own, grad_far, (keep, send) = outs[0], outs[1:blocks], outs[blocks:blocks + 2]
    (
        tokens, queries, keys, values, log_total, entry, qkv_w, grad_q0, grad_kv0, cos, sin_up, sin_down, grad_q,
        grad_kv, sems,
    ) = outs[blocks + 2:]
    rows, width = grad_ctx.shape
    here, dp, side = place[6], place[1], place[5]
    copies = Copies(sems)
    tile = queries.shape[1]
    pairs = log_total.shape[0]
    part = slice(tile, 2 * tile)
    turns = (cos, sin_up, sin_down)
    first_in = [
        copies.start(source, target)
        for source, target in (
            (queries_hbm.at[:, part], queries), (keys_hbm.at[:, part], keys), (values_hbm.at[:, part], values),
            (log_hbm.at[pairs:], log_total),
        )
    ]
    first_in += load_turns(copies, turns_hbm, turns, blocks, rows, here)
    late_in = [
        copies.start(source, target)
        for source, target in (
            (entry_hbm, entry), (qkv_hbm, qkv_w), (grad_q_hbm, grad_q0), (grad_kv_hbm, grad_kv0),
            *((tokens_hbm[r], tokens.at[r]) for r in range(blocks)),
        )
    ]
    for copy in first_in:
        copy.wait()
    attend_back(
        pairs, pairs, key_bias(blocks, rows, here), queries, keys, values, log_total, grad_ctx, turns, grad_q, grad_kv
    )
    for copy in late_in:
        copy.wait()
    store_pack(keep, send, dot_tn(entry[:rows, :], grad_q[...]), 0, dp, side, n_dp)
    for mat in range(2):
        grad = dot_tn(entry[...], grad_kv[:, mat * tile:(mat + 1) * tile])
        store_pack(keep, send, grad, (1 + mat) * tile, dp, side, n_dp)

    total = jnp.zeros((1, width), f32)
    for r in range(blocks):
        block = slice(r * rows, (r + 1) * rows)
        grad_entry = None
        for half, source in enumerate((grad_kv0, grad_kv)):
            for mat in range(2):
                start = (1 + mat) * width + half * tile
                term = dot_nt(source[block, mat * tile:(mat + 1) * tile], qkv_w[:, start:start + tile])
                grad_entry = term if grad_entry is None else grad_entry + term
        if r == 0:
            grad_entry = grad_entry + dot_nt(grad_q0[...], qkv_w[:, :tile]) + dot_nt(
                grad_q[...], qkv_w[:, tile:2 * tile]
            )
            grad_own[...] = grad_entry
        else:
            grad_far[r - 1][...] = grad_entry.astype(bf16)
        x = tokens[r].astype(f32)
        factor = lax.rsqrt(jnp.mean(x * x, axis=-1, keepdims=True) + norm_eps)
        total = total + jnp.sum(grad_entry * (x * factor), axis=0, keepdims=True)
    notes_t = notes[...].T
    total_t = jnp.broadcast_to(total, (8, width)).T
    lane = lax.broadcasted_iota(jnp.int32, (width, 128), 1)
    small = router_part[...] + jnp.where(lane == 8, notes_t[:, 0:1], 0.0) + jnp.where(
        lane == 9, total_t[:, 0:1], 0.0
    )
    store_pack(keep, send, small, 3 * tile, dp, side, n_dp)


def call(kernel, outs, scratch, scalars, operands, after=(), limit=60, aliases=None):
    whole = pl.BlockSpec(memory_space=pltpu.VMEM)
    anywhere = pl.BlockSpec(memory_space=pl.ANY)
    values, specs = [], []
    for value, kind in [*operands, *((value, far) for value in after)]:
        value = pltpu.with_memory_space_constraint(value, pltpu.VMEM if kind == held else pltpu.HBM)
        if isinstance(kind, int):
            kind = anywhere if kind == far else whole
        values.append(value)
        specs.append(kind)
    taken, ignored = len(operands), len(after)

    def body(place, *refs):
        kernel(place, *refs[:taken], *refs[taken + ignored:])

    return pl.pallas_call(
        body,
        grid_spec=pltpu.PrefetchScalarGridSpec(
            num_scalar_prefetch=1,
            grid=(1,),
            in_specs=specs,
            out_specs=[anywhere if kind == far else whole for _, _, kind in outs],
            scratch_shapes=scratch,
        ),
        out_shape=[
            pltpu.HBM(shape, dtype) for shape, dtype, _ in outs
        ],
        input_output_aliases=aliases or {},
        compiler_params=pltpu.CompilerParams(vmem_limit_bytes=limit * 2**20),
        cost_estimate=pl.CostEstimate(flops=10**8, bytes_accessed=0, transcendentals=0),
    )(scalars, *values)


def hold_until(scalars, values, after):
    return call(
        lambda place, *refs: None,
        [(value.shape, value.dtype, far) for value in values],
        [],
        scalars,
        [(value, far) for value in values],
        after,
        limit=1,
        aliases={1 + k: k for k in range(len(values))},
    )


def swap(value, mask):
    return lax.ppermute(value, group, [(i, i ^ mask) for i in range(8)])


def on_block(
    n_context,
    tokens,
    norm1_gain,
    qkv_weight,
    out_weight,
    norm2_gain,
    router_weight,
    expert_gate,
    expert_up,
    expert_down,
    shared_gate,
    shared_up,
    shared_down,
    routes,
    cotangent,
):
    rows, width = tokens.shape[1:]
    hidden = shared_gate.shape[1]
    n_experts = router_weight.shape[1]
    blocks = n_context
    n_dp = 4
    slots = rows * routes.shape[-1] * 5 // (4 * n_experts)
    dp = lax.axis_index(DP)
    here = lax.axis_index(CONTEXT)
    side = lax.axis_index(EXPERTS)
    core, chip = dp % 2, dp // 2
    index = dp * 2 + side
    expert = 2 * side + core
    pairs = width // 128

    own = tokens[0]
    cot = cotangent[0]
    cot_all = lax.all_gather(cot, group, axis=0)
    field = [own, lax.ppermute(own, CONTEXT, [(i, i + 1) for i in range(n_context - 1)])]
    field.append(lax.ppermute(field[1], CONTEXT, [(i, i + 1) for i in range(1, n_context - 1)]))
    field += [
        lax.ppermute(own, CONTEXT, [(i, i + r) for i in range(n_context - r)]) for r in range(3, blocks)
    ]
    tables = spin_tables(n_context * rows)
    gain1, gain2 = norm1_gain[None, :], norm2_gain[None, :]
    scalars = jnp.stack([index, dp, expert, core, chip, side, here])
    piece = width // n_dp // n_context
    half_columns = hidden // 2
    chunk_columns = hidden // 4
    shared_columns = hidden // 8
    quarter = hidden // n_dp

    def many(kind, *values):
        return [(value, kind) for value in values]

    router = jnp.pad(router_weight, ((0, 0), (0, 128 - n_experts)))
    router_t = jnp.pad(router_weight.T, ((0, 128 - n_experts), (0, 0)))

    picked_up = ((width, shared_columns), bf16, copied)
    picked = call(
        partial(pick_kernel, n_context),
        [picked_up, picked_up, ((shared_columns, width), bf16, copied)],
        [],
        scalars,
        [
            (shared_gate, pl.BlockSpec((width, quarter), lambda i, s: (0, s[1]))),
            (shared_up, pl.BlockSpec((width, quarter), lambda i, s: (0, s[1]))),
            (shared_down, pl.BlockSpec((quarter, width), lambda i, s: (s[1], 0))),
        ],
        [router, router_t],
        limit=10,
    )

    act = (rows, width)
    wide = (blocks * rows, width)
    sent = (rows + 16, width)
    logs = (pairs, rows, 128)
    turn = (blocks * rows, 128)
    entry, queries, keys, values, log_total, context, middle, entry_two = call(
        partial(attend_kernel, blocks),
        [
            (wide, bf16, far), (act, bf16, far), (wide, bf16, far), (wide, bf16, far), (logs, f32, far),
            (act, bf16, far), (act, f32, copied), (sent, bf16, copied),
        ],
        [
            *[pltpu.VMEM(turn, f32)] * 3, pltpu.VMEM(wide, bf16), pltpu.VMEM(act, bf16), pltpu.VMEM(wide, bf16),
            pltpu.VMEM(wide, bf16), pltpu.VMEM(logs, f32), pltpu.VMEM(act, bf16), pltpu.SemaphoreType.DMA((32,)),
        ],
        jnp.stack([here]),
        [
            *many(copied, *field, routes[0, 0].T, gain1), *many(held, qkv_weight, out_weight),
            (gain2, copied), *many(far, *tables),
        ],
        [picked[0]],
        limit=24,
    )

    near = {0: entry_two}
    near[1], near[4] = swap(entry_two, 1), swap(entry_two, 4)
    near[5] = swap(near[1], 4)
    for mask in keep_masks:
        near[mask ^ 2] = swap(near[mask], 2)

    layout = Layout(width, hidden, n_dp, n_context)
    slot_act, row_act, four = (8 * slots, width), (8 * rows, width), (4, rows, width)
    bundle_rows = n_context * layout.total
    grad_keep, grad_send, mix_keep, mix_send, router_part, bundle = call(
        partial(feed_kernel, all_masks, n_context, n_dp, layout),
        [*[(four, bf16, far)] * 4, ((width, 128), f32, copied), ((bundle_rows, 128), bf16, far)],
        [
            pltpu.VMEM((8 * slots, 128), f32), pltpu.VMEM((8, slots, rows), bf16), *[pltpu.VMEM(slot_act, bf16)] * 3,
            *[pltpu.VMEM(slot_act, f32)] * 2, *[pltpu.VMEM(row_act, bf16)] * 2,
            *[pltpu.VMEM((2, width, chunk_columns), bf16)] * 2, pltpu.VMEM((2, chunk_columns, width), bf16),
            *[pltpu.VMEM((width, shared_columns), bf16)] * 2, pltpu.VMEM((shared_columns, width), bf16),
            *[pltpu.VMEM((8 * slots, chunk_columns), bf16)] * 3, *[pltpu.VMEM((8 * rows, shared_columns), bf16)] * 3,
            *[pltpu.VMEM(four, bf16)] * 2, pltpu.VMEM((bundle_rows, 128), bf16), pltpu.VMEM((8, 16, width), bf16),
            pltpu.SemaphoreType.DMA((64,)),
        ],
        scalars,
        [
            *many(far, *[near[mask] for mask in all_masks], cot_all), *many(copied, router, router_t),
            *many(far, *picked, expert_gate, expert_up, expert_down),
        ],
        limit=60,
    )
    reduced = lax.psum_scatter(bundle, CONTEXT, scatter_dimension=0, tiled=True)

    def add_blocks(left, right):
        return [
            (left[k].astype(f32) + right[k].astype(f32)).astype(bf16) for k in range(left.shape[0])
        ]

    grad_sums = add_blocks(grad_keep, swap(grad_send, 2))
    parts = [grad_sums[0], *[swap(value, mask) for value, mask in zip(grad_sums[1:], keep_masks[1:])]]

    mix_sums = add_blocks(mix_keep, swap(mix_send, 2))
    sent_mix = hold_until(scalars, mix_sums[1:], parts[1:])
    mix_parts = [middle, mix_sums[0], *[swap(value, mask) for value, mask in zip(sent_mix, keep_masks[1:])]]

    tile = width // 2
    pack_rows = width // n_dp
    half_act, half_wide, half_logs = (rows, tile), (blocks * rows, tile), (pairs // 2, rows, 128)
    pack0 = (2, 2, pack_rows, (3 * tile + width + 128) // 2)
    pack1 = (2, 2, pack_rows, (3 * tile + 128) // 2)
    half_heads = [
        pltpu.VMEM(half_act, bf16), pltpu.VMEM(half_wide, bf16), pltpu.VMEM(half_wide, bf16), pltpu.VMEM(half_logs, f32)
    ]
    turn_scratch = [pltpu.VMEM(turn, f32)] * 3
    grad_middle, grad_ctx, grad_q, grad_kv, notes, keep0, send0 = call(
        partial(back_kernel, blocks, n_dp),
        [
            (act, f32, copied), (act, bf16, copied), (half_act, bf16, copied), (wide, bf16, copied),
            ((8, width), f32, copied), (pack0, bf16, copied), (pack0, bf16, copied),
        ],
        [
            *half_heads, pltpu.VMEM(act, bf16), pltpu.VMEM(wide, bf16), *turn_scratch, pltpu.SemaphoreType.DMA((24,)),
        ],
        scalars,
        [
            *many(copied, *parts, middle, cot, gain2, out_weight),
            *many(far, queries, keys, values, log_total, context, entry, *tables),
        ],
        sent_mix,
        limit=44,
    )

    def by_chips(keep, send):
        other = swap(send, 2)
        sums = [(keep[i, j].astype(f32) + other[i, j].astype(f32)).astype(bf16) for i in range(2) for j in range(2)]
        return [sums[0], swap(sums[1], 1), swap(sums[2], 4), swap(sums[3], 5)]

    def by_context(sets, after):
        columns = sum(arrived[0].shape[1] for arrived in sets)
        shares = call(
            partial(sum_kernel, n_context, [len(arrived) for arrived in sets]),
            [((piece, columns), bf16, copied)] * n_context, [], scalars,
            many(copied, *[value for arrived in sets for value in arrived]), after, limit=16,
        )
        return [shares[0]] + [
            lax.ppermute(shares[r], CONTEXT, [(i, (i + r) % n_context) for i in range(n_context)])
            for r in range(1, n_context)
        ]

    def total(shares):
        value = sum(value.astype(f32) for value in shares).astype(bf16)
        return [value, swap(value, 1)]

    send0, = hold_until(scalars, [send0], mix_parts[2:])
    arrived0 = by_chips(keep0, send0)
    results = call(
        partial(rest_kernel, blocks, n_dp),
        [(act, f32, copied), *[(act, bf16, copied)] * (blocks - 1), *[(pack1, bf16, copied)] * 2],
        [
            pltpu.VMEM((blocks, rows, width), bf16), *half_heads, pltpu.VMEM(wide, bf16),
            pltpu.VMEM(qkv_weight.shape, bf16), pltpu.VMEM(half_act, bf16), pltpu.VMEM(wide, bf16), *turn_scratch,
            pltpu.VMEM(half_act, bf16), pltpu.VMEM(wide, bf16), pltpu.SemaphoreType.DMA((32,)),
        ],
        scalars,
        [
            *many(far, *field), *many(copied, notes, router_part, grad_ctx),
            *many(far, queries, keys, values, log_total, entry, qkv_weight, grad_q, grad_kv, *tables),
        ],
        [arrived0[0]],
        limit=44,
    )
    grad_own, keep1 = results[0], results[blocks]
    *grad_far, send1 = hold_until(scalars, [*results[1:blocks], results[blocks + 1]], arrived0[1:])
    output = sum(value.astype(f32) for value in mix_parts).astype(bf16)[None]

    arrived1 = by_chips(keep1, send1)
    passed = lax.ppermute(grad_far[1], CONTEXT, [(i, i - 1) for i in range(2, n_context)])
    farther = [
        lax.ppermute(grad_far[r - 1], CONTEXT, [(i, i - r) for i in range(r, n_context)]) for r in range(3, blocks)
    ]
    nearest = (grad_far[0].astype(f32) + passed.astype(f32)).astype(bf16)
    pulled = [lax.ppermute(nearest, CONTEXT, [(i, i - 1) for i in range(1, n_context)]), *farther]
    shares = by_context([arrived0, arrived1], [passed, *farther])
    reduced, = hold_until(scalars, [reduced], [shares[0]])
    slabs = [reduced[m * layout.place:(m + 1) * layout.place] for m in range(n_dp)]
    downs = reduced[layout.shared_down_at:]
    base = layout.down_at - layout.shared_down_at
    shared = [slab[:layout.shared_place] for slab in slabs]
    shared[0] = jnp.concatenate([shared[0], downs[:base]], axis=0)
    shared_far = [swap(value, 2 * m + 1) for m, value in enumerate(shared)]
    slabs = [slabs[0]] + [swap(slabs[m], 2 * m) for m in range(1, n_dp)]
    got_downs = [
        lax.ppermute(
            downs[base + run * width:base + (run + 1) * width], DP, [(i, i ^ 1) for i in range(n_dp) if i % 2 != run]
        )
        for run in range(2)
    ]

    shares = [shares[0], *hold_until(scalars, shares[1:], [pulled[0], *slabs[1:], *shared_far, *got_downs])]
    spread = total(shares)
    gate_grad, up_grad, down_grad, gate_s_grad, up_s_grad, down_s_grad = call(
        partial(feed_grads_kernel, n_dp, layout),
        [
            (shape, f32, copied)
            for shape in (
                (2, piece, hidden), (2, piece, hidden), (2, 128, width), (piece, hidden), (piece, hidden),
                (hidden // n_dp // n_context, width),
            )
        ],
        [],
        scalars,
        many(copied, *slabs, *shared_far, downs, *got_downs),
        [spread[0]],
        limit=32,
    )
    input_grad, qkv_grad, out_grad, norm1_grad, norm2_grad, router_grad = call(
        partial(last_kernel, blocks),
        [
            (shape, f32, copied)
            for shape in (act, (piece, 3 * width), (piece, width), (1, piece), (1, piece), (n_experts, piece))
        ],
        [],
        scalars,
        many(copied, *spread, own, gain1, grad_own, grad_middle, *pulled),
        limit=32,
    )
    return (
        output, input_grad[None], norm1_grad[0], qkv_grad, out_grad, norm2_grad[0], router_grad.T,
        gate_grad, up_grad, down_grad, gate_s_grad, up_s_grad, down_s_grad,
    )


def on_any(mesh, *args):
    tokens, router_weight, expert_gate, shared_gate = args[0], args[5], args[6], args[9]
    sizes = dict(mesh.shape)
    fits = (
        sizes[DP] == 4
        and sizes[EXPERTS] == 2
        and tokens.shape[0] == 1
        and tokens.shape[1] == BLOCK
        and expert_gate.shape[0] == 2
        and tokens.shape[2] % 128 == 0
        and tokens.shape[2] // sizes[DP] % (16 * sizes[CONTEXT]) == 0
        and shared_gate.shape[1] % (1024) == 0
        and sizes[CONTEXT] == 4
        and shared_gate.shape[1] == 128 * sizes[DP] * sizes[CONTEXT]
    )
    if fits:
        return on_block(sizes[CONTEXT], *args)
    return on_device(*args)


def solution(mesh):
    return jax.shard_map(
        partial(on_any, mesh),
        mesh=mesh,
        in_specs=(
            P((DP, EXPERTS), CONTEXT, None),
            P(),
            P(),
            P(),
            P(),
            P(),
            P(EXPERTS, None, None),
            P(EXPERTS, None, None),
            P(EXPERTS, None, None),
            P(),
            P(),
            P(),
            P(CONTEXT, (DP, EXPERTS), None, None),
            P((DP, EXPERTS), CONTEXT, None),
        ),
        out_specs=(
            P((DP, EXPERTS), CONTEXT, None),
            P((DP, EXPERTS), CONTEXT, None),
            P((DP, CONTEXT)),
            P((DP, CONTEXT), None),
            P((DP, CONTEXT), None),
            P((DP, CONTEXT)),
            P((DP, CONTEXT), None),
            P(EXPERTS, (DP, CONTEXT), None),
            P(EXPERTS, (DP, CONTEXT), None),
            P(EXPERTS, (DP, CONTEXT), None),
            P((DP, CONTEXT), None),
            P((DP, CONTEXT), None),
            P((DP, CONTEXT), None),
        ),
        check_vma=False,
    )
```

```python
from functools import partial
import math

import jax
import jax.numpy as jnp
import numpy as np
from jax import lax
from jax.experimental import pallas as pl
from jax.experimental.pallas import tpu as pltpu
from jax.sharding import PartitionSpec as P

HEAD_DIM = 64
BLOCK = 256
DP, CONTEXT, EXPERTS = "dp", "context", "experts"


norm_eps = 1e-05
masked_score = -1e30
highest = lax.Precision.HIGHEST


def matmul(left, right):
    return jnp.dot(left, right, preferred_element_type=jnp.float32)


def contract(spec, left, right):
    return jnp.einsum(spec, left, right, preferred_element_type=jnp.float32)


def normalize(field):
    factor = lax.rsqrt(jnp.mean(field * field, axis=-1, keepdims=True) + norm_eps)
    return (field * factor, factor)


def norm_back(grad_out, normed, factor, gain):
    grad_norm = grad_out * gain
    inner = jnp.mean(grad_norm * normed, axis=-1, keepdims=True)
    return (factor * (grad_norm - normed * inner), jnp.sum(grad_out * normed, axis=0))


def rotation(positions, head_dim):
    half = head_dim // 2
    freqs = 10000.0 ** (-2.0 * jnp.arange(half, dtype=jnp.float32) / head_dim)
    angles = positions.astype(jnp.float32)[:, None] * freqs[None, :]
    return (jnp.cos(angles)[:, None, None, :], jnp.sin(angles)[:, None, None, :])


def rotate(field, cosine, sine):
    half = field.shape[-1] // 2
    first = field[..., :half]
    second = field[..., half:]
    return jnp.concatenate(
        [first * cosine - second * sine, second * cosine + first * sine], axis=-1
    )


def rotate_back(grad, cosine, sine):
    half = grad.shape[-1] // 2
    first = grad[..., :half]
    second = grad[..., half:]
    return jnp.concatenate(
        [first * cosine + second * sine, second * cosine - first * sine], axis=-1
    )


def silu_back(grad_hidden, gate_part, up_part):
    sigmoid_value = jax.nn.sigmoid(gate_part)
    active = gate_part * sigmoid_value
    grad_gate = grad_hidden * up_part * sigmoid_value * (1.0 + gate_part * (1.0 - sigmoid_value))
    grad_up = grad_hidden * active
    return (grad_gate.astype(jnp.bfloat16), grad_up.astype(jnp.bfloat16))


def score_block(queries, keys_part, query_block, start):
    size = keys_part.shape[0]
    seqs, heads, head_dim = (queries.shape[1], queries.shape[2], queries.shape[3])
    keys_four = keys_part.reshape(size, seqs, heads, head_dim)
    scores = contract("qshd,kshd->shqk", queries, keys_four) * head_dim ** (-0.5)
    key_block = (start + jnp.arange(size)) // BLOCK
    visible = key_block[None, :] <= query_block[:, None]
    return (jnp.where(visible, scores, masked_score), visible, keys_four)


def attend_piece(queries, query_block, state, keys_part, values_part, start):
    size = keys_part.shape[0]
    seqs, heads, head_dim = (queries.shape[1], queries.shape[2], queries.shape[3])

    def compute(current):
        best, total, accum = current
        scores, visible, keys_four = score_block(queries, keys_part, query_block, start)
        new_best = jnp.maximum(best, jnp.max(scores, axis=-1))
        weights = jnp.where(visible, jnp.exp(scores - new_best[..., None]), 0.0)
        factor = jnp.exp(best - new_best)
        values_four = values_part.reshape(size, seqs, heads, head_dim)
        total = total * factor + jnp.sum(weights, axis=-1)
        accum = accum * factor[..., None] + contract(
            "shqk,kshd->shqd", weights.astype(jnp.bfloat16), values_four
        )
        return (new_best, total, accum)

    needed = start // BLOCK <= jnp.max(query_block)
    return lax.cond(needed, compute, lambda current: current, state)


def fold_keys(queries, query_block, state, pieces):
    keys_all, values_all = pieces
    length = keys_all.shape[0]
    size = math.gcd(length, 512)

    def step(index, current):
        first = index * size
        keys_part = lax.dynamic_slice_in_dim(keys_all, first, size, 0)
        values_part = lax.dynamic_slice_in_dim(values_all, first, size, 0)
        return attend_piece(queries, query_block, current, keys_part, values_part, first)

    return lax.fori_loop(0, length // size, step, state)


def block_grads(queries, query_block, grad_ctx, delta, log_total, keys_part, values_part, start):
    size = keys_part.shape[0]
    seqs, heads, head_dim = (queries.shape[1], queries.shape[2], queries.shape[3])
    scores, visible, keys_four = score_block(queries, keys_part, query_block, start)
    probs = jnp.where(visible, jnp.exp(scores - log_total[..., None]), 0.0)
    values_four = values_part.reshape(size, seqs, heads, head_dim)
    grad_probs = contract("qshd,kshd->shqk", grad_ctx, values_four)
    grad_scores = (probs * (grad_probs - delta[..., None])).astype(jnp.bfloat16)
    return (probs, grad_scores, keys_four)


def key_value_terms(
    queries, query_block, grad_ctx, delta, log_total, keys_part, values_part, start
):
    size = keys_part.shape[0]
    seqs, heads, head_dim = (queries.shape[1], queries.shape[2], queries.shape[3])
    width = heads * head_dim
    probs, grad_scores, keys_four = block_grads(
        queries, query_block, grad_ctx, delta, log_total, keys_part, values_part, start
    )
    grad_values = contract("shqk,qshd->kshd", probs.astype(jnp.bfloat16), grad_ctx)
    grad_keys = contract("shqk,qshd->kshd", grad_scores, queries) * head_dim ** (-0.5)
    return jnp.concatenate(
        [grad_keys.reshape(size, seqs, width), grad_values.reshape(size, seqs, width)], axis=-1
    )


def query_grads(queries, query_block, grad_ctx, delta, log_total, keys_all, values_all):
    length = keys_all.shape[0]
    size = math.gcd(length, 512)

    def step(index, accum):
        first = index * size
        keys_part = lax.dynamic_slice_in_dim(keys_all, first, size, 0)
        values_part = lax.dynamic_slice_in_dim(values_all, first, size, 0)

        def compute(current):
            probs, grad_scores, keys_four = block_grads(
                queries, query_block, grad_ctx, delta, log_total, keys_part, values_part, first
            )
            return current + contract("shqk,kshd->qshd", grad_scores, keys_four)

        return lax.cond(
            first // BLOCK <= jnp.max(query_block), compute, lambda current: current, accum
        )

    return lax.fori_loop(0, length // size, step, jnp.zeros(queries.shape, jnp.float32))


def query_side_fold(keys_local, values_local, key_start, accum, pieces, start):
    queries_all, grad_all, delta_all, log_all = pieces
    length = queries_all.shape[0]
    size = math.gcd(length, 512)

    def step(index, current):
        first = index * size
        queries_part = lax.dynamic_slice_in_dim(queries_all, first, size, 0)
        grad_part = lax.dynamic_slice_in_dim(grad_all, first, size, 0)
        delta_part = jnp.transpose(lax.dynamic_slice_in_dim(delta_all, first, size, 0), (1, 2, 0))
        log_part = jnp.transpose(lax.dynamic_slice_in_dim(log_all, first, size, 0), (1, 2, 0))
        block_rows = (first + jnp.arange(size)) // BLOCK

        def compute(inner):
            return inner + key_value_terms(
                queries_part,
                block_rows,
                grad_part,
                delta_part,
                log_part,
                keys_local,
                values_local,
                key_start,
            )

        return lax.cond(
            jnp.max(block_rows) >= key_start // BLOCK, compute, lambda inner: inner, current
        )

    return lax.fori_loop(0, length // size, step, accum)


def reduce_experts(gate_grad, up_grad, down_grad):
    return (
        lax.psum_scatter(gate_grad, (DP, CONTEXT), scatter_dimension=1, tiled=True),
        lax.psum_scatter(up_grad, (DP, CONTEXT), scatter_dimension=1, tiled=True),
        lax.psum_scatter(down_grad, (DP, CONTEXT), scatter_dimension=1, tiled=True),
    )


def on_device(
    tokens,
    norm1_gain,
    qkv_weight,
    out_weight,
    norm2_gain,
    router_weight,
    expert_gate,
    expert_up,
    expert_down,
    shared_gate,
    shared_up,
    shared_down,
    routes,
    cotangent,
):
    seqs, span, width = tokens.shape
    heads = width // HEAD_DIM
    rows = seqs * span
    local = jnp.swapaxes(tokens, 0, 1).reshape(rows, width).astype(jnp.float32)
    key_start = lax.axis_index(CONTEXT) * span
    positions = key_start + jnp.arange(span)
    query_block = positions // BLOCK
    cosine, sine = rotation(positions, HEAD_DIM)
    normed_one, factor_one = normalize(local)
    entry_one = (normed_one * norm1_gain).astype(jnp.bfloat16)
    projected = matmul(entry_one, qkv_weight).reshape(span, seqs, 3, heads, HEAD_DIM)
    queries = rotate(projected[:, :, 0], cosine, sine).astype(jnp.bfloat16)
    keys_local = (
        rotate(projected[:, :, 1], cosine, sine).astype(jnp.bfloat16).reshape(span, seqs, width)
    )
    values_local = projected[:, :, 2].astype(jnp.bfloat16).reshape(span, seqs, width)
    start_state = (
        jnp.full((seqs, heads, span), masked_score, jnp.float32),
        jnp.zeros((seqs, heads, span), jnp.float32),
        jnp.zeros((seqs, heads, span, HEAD_DIM), jnp.float32),
    )
    best, total, accum = fold_keys(
        queries,
        query_block,
        start_state,
        (
            lax.all_gather(keys_local, CONTEXT, axis=0, tiled=True),
            lax.all_gather(values_local, CONTEXT, axis=0, tiled=True),
        ),
    )
    context = jnp.transpose(accum / total[..., None], (2, 0, 1, 3))
    log_total = best + jnp.log(total)
    context_low = context.astype(jnp.bfloat16).reshape(rows, width)
    middle = local + matmul(context_low, out_weight)
    normed_two, factor_two = normalize(middle)
    entry_two = (normed_two * norm2_gain).astype(jnp.bfloat16)
    logits = matmul(entry_two, router_weight)
    total_experts = router_weight.shape[1]
    topk = routes.shape[-1]
    capacity = rows * topk * 5 // (4 * total_experts)
    route_rows = jnp.swapaxes(routes[0], 0, 1).reshape(rows, topk)
    chosen = route_rows[:, :, None] == jnp.arange(total_experts)[None, None, :]
    chosen_float = chosen.astype(jnp.float32)
    picked = jnp.sum(chosen_float * logits[:, None, :], axis=-1)
    picked = picked - jnp.max(picked, axis=-1, keepdims=True)
    raised = jnp.exp(picked)
    gates = raised / jnp.sum(raised, axis=-1, keepdims=True)
    counts = jnp.sum(chosen.astype(jnp.int32), axis=1)
    before = jnp.cumsum(counts, axis=0) - counts
    slots = jnp.sum(chosen.astype(jnp.int32) * before[:, None, :], axis=-1)
    targets = route_rows * capacity + slots
    placing = (
        jnp.transpose(targets)[:, :, None] == jnp.arange(total_experts * capacity)[None, None, :]
    ).astype(jnp.bfloat16)
    dispatch_hot = jnp.sum(placing, axis=0)
    buffer = (
        contract("mr,md->rd", dispatch_hot, entry_two)
        .astype(jnp.bfloat16)
        .reshape(total_experts, capacity, width)
    )
    received = lax.all_to_all(buffer, EXPERTS, split_axis=0, concat_axis=1, tiled=True)
    gate_part = contract("erd,edf->erf", received, expert_gate)
    up_part = contract("erd,edf->erf", received, expert_up)
    hidden = (gate_part * jax.nn.sigmoid(gate_part) * up_part).astype(jnp.bfloat16)
    produced = contract("erf,efd->erd", hidden, expert_down).astype(jnp.bfloat16)
    shared_gate_part = matmul(entry_two, shared_gate)
    shared_up_part = matmul(entry_two, shared_up)
    shared_hidden = (shared_gate_part * jax.nn.sigmoid(shared_gate_part) * shared_up_part).astype(
        jnp.bfloat16
    )
    shared_out = matmul(shared_hidden, shared_down)
    returned = lax.all_to_all(produced, EXPERTS, split_axis=1, concat_axis=0, tiled=True).reshape(
        total_experts * capacity, width
    )
    picked_rows = contract("kmr,rd->kmd", placing, returned)
    mixed = jnp.sum(jnp.transpose(gates)[:, :, None] * picked_rows, axis=0)
    result = (middle + mixed + shared_out).astype(jnp.bfloat16)
    output = jnp.swapaxes(result.reshape(span, seqs, width), 0, 1)
    grad_low = jnp.swapaxes(cotangent, 0, 1).reshape(rows, width)
    grad_out = grad_low.astype(jnp.float32)
    grad_gates = jnp.transpose(jnp.sum(picked_rows * grad_out[None], axis=-1))
    grad_rows = (jnp.transpose(gates)[:, :, None] * grad_out[None]).astype(jnp.bfloat16)
    grad_slots = (
        contract("kmr,kmd->rd", placing, grad_rows)
        .astype(jnp.bfloat16)
        .reshape(total_experts, capacity, width)
    )
    grad_produced = lax.all_to_all(grad_slots, EXPERTS, split_axis=0, concat_axis=1, tiled=True)
    expert_down_term = contract("erf,erd->efd", hidden, grad_produced)
    grad_hidden = contract("erd,efd->erf", grad_produced, expert_down)
    grad_gate_part, grad_up_part = silu_back(grad_hidden, gate_part, up_part)
    expert_gate_term = contract("erd,erf->edf", received, grad_gate_part)
    expert_up_term = contract("erd,erf->edf", received, grad_up_part)
    grad_received = (
        contract("erf,edf->erd", grad_gate_part, expert_gate)
        + contract("erf,edf->erd", grad_up_part, expert_up)
    ).astype(jnp.bfloat16)
    expert_parts = None
    shared_down_term = contract("mf,md->fd", shared_hidden, grad_low)
    grad_shared_hidden = contract("md,fd->mf", grad_low, shared_down)
    grad_shared_gate, grad_shared_up = silu_back(
        grad_shared_hidden, shared_gate_part, shared_up_part
    )
    shared_gate_term = contract("md,mf->df", entry_two, grad_shared_gate)
    shared_up_term = contract("md,mf->df", entry_two, grad_shared_up)
    grad_entry_two = contract("mf,df->md", grad_shared_gate, shared_gate) + contract(
        "mf,df->md", grad_shared_up, shared_up
    )
    grad_pick = gates * (grad_gates - jnp.sum(gates * grad_gates, axis=-1, keepdims=True))
    grad_logits = jnp.sum(chosen_float * grad_pick[:, :, None], axis=1)
    router_term = jnp.einsum(
        "md,me->de", entry_two.astype(jnp.float32), grad_logits, precision=highest
    )
    grad_entry_two = grad_entry_two + jnp.einsum(
        "me,de->md", grad_logits, router_weight.astype(jnp.float32), precision=highest
    )
    grad_returned = lax.all_to_all(
        grad_received, EXPERTS, split_axis=1, concat_axis=0, tiled=True
    ).reshape(total_experts * capacity, width)
    grad_entry_two = grad_entry_two + contract("mr,rd->md", dispatch_hot, grad_returned)
    grad_middle_norm, norm2_term = norm_back(grad_entry_two, normed_two, factor_two, norm2_gain)
    grad_middle = grad_out + grad_middle_norm
    grad_attn = grad_middle.astype(jnp.bfloat16)
    out_term = contract("md,me->de", context_low, grad_attn)
    grad_ctx = (
        contract("me,de->md", grad_attn, out_weight)
        .astype(jnp.bfloat16)
        .reshape(span, seqs, heads, HEAD_DIM)
    )
    delta = jnp.transpose(jnp.sum(grad_ctx.astype(jnp.float32) * context, axis=-1), (1, 2, 0))
    keys_all, values_all = (
        lax.all_gather(keys_local, CONTEXT, axis=0, tiled=True),
        lax.all_gather(values_local, CONTEXT, axis=0, tiled=True),
    )
    grad_queries = query_grads(
        queries, query_block, grad_ctx, delta, log_total, keys_all, values_all
    ) * HEAD_DIM ** (-0.5)
    delta_rows = jnp.transpose(delta, (2, 0, 1))
    log_rows = jnp.transpose(log_total, (2, 0, 1))
    pull_step = partial(query_side_fold, keys_local, values_local, key_start)
    empty_grads = jnp.zeros((span, seqs, 2 * width), jnp.float32)
    grad_kv = pull_step(
        empty_grads,
        (
            lax.all_gather(queries, CONTEXT, axis=0, tiled=True),
            lax.all_gather(grad_ctx, CONTEXT, axis=0, tiled=True),
            lax.all_gather(delta_rows.astype(jnp.bfloat16), CONTEXT, axis=0, tiled=True).astype(
                jnp.float32
            ),
            lax.all_gather(log_rows.astype(jnp.bfloat16), CONTEXT, axis=0, tiled=True).astype(
                jnp.float32
            ),
        ),
        jnp.int32(0),
    )
    grad_keys = grad_kv[..., :width].reshape(span, seqs, heads, HEAD_DIM)
    grad_values = grad_kv[..., width:].reshape(span, seqs, heads, HEAD_DIM)
    grad_projected = jnp.stack(
        [
            rotate_back(grad_queries, cosine, sine),
            rotate_back(grad_keys, cosine, sine),
            grad_values,
        ],
        axis=2,
    )
    grad_projected = grad_projected.astype(jnp.bfloat16).reshape(rows, 3 * width)
    qkv_term = contract("md,me->de", entry_one, grad_projected)
    grad_entry_one = contract("me,de->md", grad_projected, qkv_weight)
    grad_local_norm, norm1_term = norm_back(grad_entry_one, normed_one, factor_one, norm1_gain)
    input_grad = jnp.swapaxes((grad_middle + grad_local_norm).reshape(span, seqs, width), 0, 1)
    expert_parts = reduce_experts(expert_gate_term, expert_up_term, expert_down_term)
    spread = (
        lax.psum_scatter(norm1_term, (DP, CONTEXT), scatter_dimension=0, tiled=True),
        lax.psum_scatter(qkv_term, (DP, CONTEXT), scatter_dimension=0, tiled=True),
        lax.psum_scatter(out_term, (DP, CONTEXT), scatter_dimension=0, tiled=True),
        lax.psum_scatter(norm2_term, (DP, CONTEXT), scatter_dimension=0, tiled=True),
        lax.psum_scatter(router_term, (DP, CONTEXT), scatter_dimension=0, tiled=True),
        lax.psum_scatter(shared_gate_term, (DP, CONTEXT), scatter_dimension=0, tiled=True),
        lax.psum_scatter(shared_up_term, (DP, CONTEXT), scatter_dimension=0, tiled=True),
        lax.psum_scatter(shared_down_term, (DP, CONTEXT), scatter_dimension=0, tiled=True),
    )
    (
        norm1_part,
        qkv_part,
        out_part,
        norm2_part,
        router_part,
        shared_gate_piece,
        shared_up_piece,
        shared_down_piece,
    ) = spread
    summed = (
        lax.psum(norm1_part.astype(jnp.bfloat16), EXPERTS).astype(jnp.float32),
        lax.psum(qkv_part.astype(jnp.bfloat16), EXPERTS).astype(jnp.float32),
        lax.psum(out_part.astype(jnp.bfloat16), EXPERTS).astype(jnp.float32),
        lax.psum(norm2_part.astype(jnp.bfloat16), EXPERTS).astype(jnp.float32),
        lax.psum(router_part.astype(jnp.bfloat16), EXPERTS).astype(jnp.float32),
        lax.psum(shared_gate_piece.astype(jnp.bfloat16), EXPERTS).astype(jnp.float32),
        lax.psum(shared_up_piece.astype(jnp.bfloat16), EXPERTS).astype(jnp.float32),
        lax.psum(shared_down_piece.astype(jnp.bfloat16), EXPERTS).astype(jnp.float32),
    )
    return (
        output,
        input_grad,
        summed[0],
        summed[1],
        summed[2],
        summed[3],
        summed[4],
        expert_parts[0],
        expert_parts[1],
        expert_parts[2],
        summed[5],
        summed[6],
        summed[7],
    )


group = (DP, EXPERTS)
keep_masks = (0, 1, 4, 5)
all_masks = keep_masks + tuple(mask ^ 2 for mask in keep_masks)
f32 = jnp.float32
bf16 = jnp.bfloat16
far, copied, held = range(3)


def dot_nn(left, right):
    return lax.dot_general(left, right, (((1,), (0,)), ((), ())), preferred_element_type=f32)


def dot_nt(left, right):
    return lax.dot_general(left, right, (((1,), (1,)), ((), ())), preferred_element_type=f32)


def dot_tn(left, right):
    return lax.dot_general(left, right, (((0,), (0,)), ((), ())), preferred_element_type=f32)


def spin(field, cosine, sine_up, sine_down):
    up = pltpu.roll(field, 32, 1)
    down = pltpu.roll(field, 96, 1)
    return field * cosine + up * sine_up + down * sine_down


def spin_back(grad, cosine, sine_up, sine_down):
    up = pltpu.roll(grad, 32, 1)
    down = pltpu.roll(grad, 96, 1)
    return grad * cosine - up * sine_up - down * sine_down


def spin_tables(length):
    lane = np.arange(128)
    freqs = 10000.0 ** (-2.0 * (lane % 32) / HEAD_DIM)
    angles = np.arange(length)[:, None] * freqs[None, :]
    second = (lane % HEAD_DIM) >= HEAD_DIM // 2
    sine = np.sin(angles)
    tables = (np.cos(angles), np.where(second, sine, 0.0), np.where(second, 0.0, -sine))
    return [jnp.asarray(table, f32) for table in tables]


def lane_half(rows):
    return lax.broadcasted_iota(jnp.int32, (rows, 128), 1) // HEAD_DIM


def key_bias(blocks, rows, here):
    block = lax.broadcasted_iota(jnp.int32, (1, blocks * rows), 1) // rows
    return jnp.where(block <= here, 0.0, masked_score)


class Copies:
    def __init__(self, sems):
        self.sems, self.count = sems, 0

    def start(self, source, target):
        copy = pltpu.make_async_copy(source, target, self.sems.at[self.count])
        self.count += 1
        copy.start()
        return copy


def attend_kernel(blocks, place, *refs):
    tokens = refs[:blocks]
    (routes, gain1, qkv_w, out_w, gain2, cos_hbm, up_hbm, down_hbm) = refs[blocks:blocks + 8]
    (entry_hbm, queries_hbm, keys_hbm, values_hbm, log_hbm, context_hbm, middle, entry_two) = refs[
        blocks + 8:blocks + 16
    ]
    (cos, sin_up, sin_down, entry, queries, keys, values, log_total, context, sems) = refs[blocks + 16:]
    rows, width = middle.shape
    pairs = width // 128
    here = place[0]
    copies = Copies(sems)
    tables_in = []
    for r in range(blocks):
        block = pl.ds(pl.multiple_of(jnp.maximum(here - r, 0) * rows, rows), rows)
        for source, target in ((cos_hbm, cos), (up_hbm, sin_up), (down_hbm, sin_down)):
            tables_in.append(copies.start(source.at[block], target.at[r * rows:(r + 1) * rows]))

    for r in range(blocks):
        x = tokens[r][...].astype(f32)
        factor = lax.rsqrt(jnp.mean(x * x, axis=-1, keepdims=True) + norm_eps)
        entry[r * rows:(r + 1) * rows, :] = (x * factor * gain1[...]).astype(bf16)
    outs = [copies.start(entry, entry_hbm)]
    for copy in tables_in:
        copy.wait()

    tile = 384
    for start in range(0, width, tile):
        part = dot_nn(entry[:rows, :], qkv_w[:, start:start + tile])
        for lane in range(0, tile, 128):
            queries[:, start + lane:start + lane + 128] = spin(
                part[:, lane:lane + 128], cos[:rows, :], sin_up[:rows, :], sin_down[:rows, :]
            ).astype(bf16)
    for start in range(0, width, tile):
        part = dot_nn(entry[...], qkv_w[:, width + start:width + start + tile])
        for lane in range(0, tile, 128):
            keys[:, start + lane:start + lane + 128] = spin(
                part[:, lane:lane + 128], cos[...], sin_up[...], sin_down[...]
            ).astype(bf16)
        values[:, start:start + tile] = dot_nn(
            entry[...], qkv_w[:, 2 * width + start:2 * width + start + tile]
        ).astype(bf16)
    outs += [copies.start(queries, queries_hbm), copies.start(keys, keys_hbm), copies.start(values, values_hbm)]
    half = lane_half(rows)
    bias = key_bias(blocks, rows, here)

    def attend(pair, carry):
        lanes = pl.ds(pl.multiple_of(pair * 128, 128), 128)
        both = queries[:, lanes] * HEAD_DIM ** (-0.5)
        results, logs = [], []
        for head in range(2):
            query = jnp.where(half == head, both, jnp.zeros_like(both))
            scores = dot_nt(query, keys[:, lanes]) + bias
            best = jnp.max(scores, axis=-1, keepdims=True)
            weights = jnp.exp(scores - best)
            total = jnp.sum(weights, axis=-1, keepdims=True)
            results.append(dot_nn(weights.astype(bf16), values[:, lanes]) / total)
            logs.append(best + jnp.log(total))
        context[:, lanes] = jnp.where(half == 0, results[0], results[1]).astype(bf16)
        log_total[pair] = jnp.where(half == 0, logs[0], logs[1])
        return carry

    lax.fori_loop(0, pairs, attend, 0)
    outs += [copies.start(log_total, log_hbm), copies.start(context, context_hbm)]
    mid = tokens[0][...].astype(f32) + dot_nn(context[...], out_w[...])
    middle[...] = mid
    factor = lax.rsqrt(jnp.mean(mid * mid, axis=-1, keepdims=True) + norm_eps)
    entry_two[:rows, :] = (mid * factor * gain2[...]).astype(bf16)
    entry_two[rows:, :] = jnp.zeros((entry_two.shape[0] - rows, width), bf16)
    entry_two[rows:rows + 8, :rows] = jnp.concatenate(
        [routes[...].astype(f32), jnp.zeros((8 - routes.shape[0], rows), f32)], axis=0
    ).astype(bf16)
    for copy in outs:
        copy.wait()


def pick_kernel(n_context, place, gate, up, down, gate_out, up_out, down_out):
    side = place[5]
    lane = lax.broadcasted_iota(jnp.int32, (gate.shape[0], 128), 1)
    for source, target in ((gate, gate_out), (up, up_out)):
        for z in range(0, n_context, 2):
            one = source[:, z * 128:(z + 1) * 128].astype(f32)
            two = source[:, (z + 1) * 128:(z + 2) * 128].astype(f32)
            left = jnp.where(side == 0, one, pltpu.roll(one, 64, 1))
            right = jnp.where(side == 0, pltpu.roll(two, 64, 1), two)
            target[:, z * 64:z * 64 + 128] = jnp.where(lane < 64, left, right).astype(bf16)
    for z in range(n_context):
        start = pl.multiple_of(z * 128 + side * 64, 64)
        down_out[z * 64:(z + 1) * 64, :] = down[pl.ds(start, 64), :]


def sum_kernel(n_context, counts, place, *refs):
    outs = refs[-n_context:]
    here = place[6]
    piece = outs[0].shape[0]
    for r, out in enumerate(outs):
        block = lax.rem(here + r, n_context)
        rows = pl.ds(pl.multiple_of(block * piece, piece), piece)
        first, start = 0, 0
        for count in counts:
            total = refs[first][rows, :].astype(f32)
            for value in refs[first + 1:first + count]:
                total = total + value[rows, :].astype(f32)
            out[:, start:start + total.shape[1]] = total.astype(bf16)
            first, start = first + count, start + total.shape[1]


def silu_parts(gate_part, up_part):
    sigmoid_value = jax.nn.sigmoid(gate_part)
    active = gate_part * sigmoid_value
    return sigmoid_value, active, (active * up_part).astype(bf16)


def silu_grads(grad_hidden, gate_part, up_part, sigmoid_value, active):
    grad_gate = grad_hidden * up_part * sigmoid_value * (1.0 + gate_part * (1.0 - sigmoid_value))
    return grad_gate.astype(bf16), (grad_hidden * active).astype(bf16)


def feed_kernel(masks, n_context, n_dp, layout, place, *refs):
    inputs = refs[:8]
    (cot_hbm, router, router_t, gate_s_hbm, up_s_hbm, down_s_hbm, gate_hbm, up_hbm, down_hbm) = refs[8:17]
    (grad_keep_hbm, grad_send_hbm, mix_keep_hbm, mix_send_hbm, router_grad, bundle_hbm) = refs[17:23]
    (
        aux, hots, x_all, dz_all, g_all, produced, received, field, cot, gate_w, up_w, down_w, gate_s_w, up_s_w,
        down_s_w, hidden, dgate, dup, hidden_s, dgate_s, dup_s, grad_tokens, mix_tokens, bundle, notes, sems,
    ) = refs[23:]
    index, dp, expert, core, chip = place[0], place[1], place[2], place[3], place[4]
    rows = cot.shape[0] // 8
    width = field.shape[1]
    slots = hots.shape[1]
    copies = Copies(sems)
    ins = []
    for i in range(8):
        rows_of = slice(i * rows, (i + 1) * rows)
        ins.append((
            copies.start(inputs[i].at[rows:], notes.at[i]),
            copies.start(inputs[i].at[:rows], field.at[rows_of]),
            copies.start(cot_hbm.at[lax.bitwise_xor(index, masks[i])], cot.at[rows_of]),
        ))
    columns = layout.blocks * 128
    weights_in = []
    for run in range(2):
        part = pl.ds(pl.multiple_of((2 * chip + run) * columns, columns), columns)
        weights_in.append([
            copies.start(gate_hbm.at[core, :, part], gate_w.at[run]),
            copies.start(up_hbm.at[core, :, part], up_w.at[run]),
            copies.start(down_hbm.at[core, part, :], down_w.at[run]),
        ])
    shared_in = [
        copies.start(source, target)
        for source, target in ((gate_s_hbm, gate_s_w), (up_s_hbm, up_s_w), (down_s_hbm, down_s_w))
    ]

    lanes = lax.broadcasted_iota(jnp.int32, (slots, 128), 1)
    mine = (lanes == expert).astype(f32)
    expert_row = expert.astype(f32)
    before = (
        lax.broadcasted_iota(jnp.int32, (rows, rows), 0) < lax.broadcasted_iota(jnp.int32, (rows, rows), 1)
    ).astype(bf16)
    slot_of = lax.broadcasted_iota(jnp.int32, (slots, rows), 0).astype(f32)
    for i in range(8):
        rows_of = slice(i * rows, (i + 1) * rows)
        slots_of = slice(i * slots, (i + 1) * slots)
        if i % 4 == 0:
            for copy in sum(ins[i:i + 4], ()):
                copy.wait()
        routes = notes[i, :, :rows].astype(f32)
        first, second = routes[0:1, :], routes[1:2, :]
        named = jnp.logical_or(first == expert_row, second == expert_row).astype(f32)
        slot = dot_nn(jnp.broadcast_to(named, (16, rows)).astype(bf16), before)[0:1, :]
        hot_f = jnp.where(slot_of == slot, named, 0.0)
        partner = jnp.where(first == expert_row, second, first)
        other = jnp.sum(hot_f * partner, axis=-1, keepdims=True)
        hot = hot_f.astype(bf16)
        hots[i] = hot
        x = dot_nn(hot, field[rows_of, :]).astype(bf16)
        x_all[slots_of, :] = x
        g_slot = dot_nn(hot, cot[rows_of, :])
        logits = dot_nn(x, router[...])
        theirs = (lanes.astype(f32) == other).astype(f32)
        gate = jax.nn.sigmoid(jnp.sum((mine - theirs) * logits, axis=-1, keepdims=True))
        dz_all[slots_of, :] = (gate * g_slot).astype(bf16)
        g_all[slots_of, :] = g_slot.astype(bf16)
        aux[slots_of, :] = jnp.where(lanes == 64, gate, gate * (1.0 - gate) * (mine - theirs))

    tile = x_all.shape[0] // 2
    for run in range(2):
        for copy in weights_in[run]:
            copy.wait()
        for t in range(2):
            part = slice(t * tile, (t + 1) * tile)
            gate_part = dot_nn(x_all[part, :], gate_w[run])
            up_part = dot_nn(x_all[part, :], up_w[run])
            sigmoid_value, active, u = silu_parts(gate_part, up_part)
            hidden[part, :] = u
            out = dot_nn(u, down_w[run])
            grad_hidden = dot_nt(dz_all[part, :], down_w[run])
            da, db = silu_grads(grad_hidden, gate_part, up_part, sigmoid_value, active)
            dgate[part, :] = da
            dup[part, :] = db
            grad = dot_nt(da, gate_w[run]) + dot_nt(db, up_w[run])
            if run == 0:
                produced[part, :] = out
                received[part, :] = grad
            else:
                produced[part, :] += out
                received[part, :] += grad
        expert_grads(bundle, x_all, dz_all, hidden, dgate, dup, layout, run, dp, n_context, n_dp)

    for copy in shared_in:
        copy.wait()
    router_sum = jnp.zeros((width, 128), f32)
    outs, last = [], {}
    for t in range(4):
        tile = slice(2 * t * rows, 2 * (t + 1) * rows)
        gate_part = dot_nn(field[tile, :], gate_s_w[...])
        up_part = dot_nn(field[tile, :], up_s_w[...])
        sigmoid_value, active, u = silu_parts(gate_part, up_part)
        hidden_s[tile, :] = u
        mixed = dot_nn(u, down_s_w[...])
        grad_hidden = dot_nt(cot[tile, :], down_s_w[...])
        da, db = silu_grads(grad_hidden, gate_part, up_part, sigmoid_value, active)
        dgate_s[tile, :] = da
        dup_s[tile, :] = db
        grad_in = dot_nt(da, gate_s_w[...]) + dot_nt(db, up_s_w[...])
        for copy in last.pop(t - 2, []):
            copy.wait()
        for half in range(2):
            i = 2 * t + half
            rows_of = slice(half * rows, (half + 1) * rows)
            slots_of = slice(i * slots, (i + 1) * slots)
            z = produced[slots_of, :]
            extra = aux[slots_of, :]
            gate = extra[:, 64:65]
            pick = jnp.sum(z.astype(bf16).astype(f32) * g_all[slots_of, :].astype(f32), axis=-1, keepdims=True)
            dlogits = (jnp.where(lanes < 64, extra, 0.0) * pick).astype(bf16)
            router_sum = router_sum + dot_tn(x_all[slots_of, :], dlogits)
            grad = (received[slots_of, :] + dot_nn(dlogits, router_t[...])).astype(bf16)
            back = dot_tn(hots[i], jnp.concatenate([grad, (gate * z).astype(bf16)], axis=1))
            slot = (2 * t + half) % 4
            grad_tokens[slot] = (grad_in[rows_of, :] + back[:, :width]).astype(bf16)
            mix_tokens[slot] = (mixed[rows_of, :] + back[:, width:]).astype(bf16)
        last[t] = []
        for half in range(2):
            i = 2 * t + half
            for source, targets in (
                (grad_tokens, (grad_keep_hbm, grad_send_hbm)), (mix_tokens, (mix_keep_hbm, mix_send_hbm))
            ):
                last[t].append(copies.start(source.at[i % 4], targets[i // 4].at[i % 4]))
    router_grad[...] = router_sum

    for mat, source in enumerate((dgate_s, dup_s)):
        offset = mat * layout.shared_blocks * layout.piece
        matrix_grads(bundle, field, source, offset, layout, dp, n_context, n_dp)
    outs += [
        copies.start(bundle.at[start:start + layout.shared_down_at], bundle_hbm.at[start:start + layout.shared_down_at])
        for start in range(0, n_context * layout.total, layout.total)
    ]
    grad = dot_tn(hidden_s[...], cot[...]).astype(bf16)
    down_rows = layout.down_rows
    for z in range(n_context):
        for lane in range(width // 128):
            start = z * layout.total + layout.shared_down_at + lane * down_rows
            bundle[start:start + down_rows, :] = grad[z * down_rows:(z + 1) * down_rows, lane * 128:(lane + 1) * 128]
    for z in range(n_context):
        part = slice(z * layout.total + layout.shared_down_at, (z + 1) * layout.total)
        outs.append(copies.start(bundle.at[part], bundle_hbm.at[part]))
    for copy in sum(last.values(), outs):
        copy.wait()


def matrix_grads(bundle, left, right, offset, layout, dp, n_context, n_dp):
    block = left.shape[1] // n_dp
    piece = block // n_context
    tile = 2 * block
    for t in range(n_dp // 2):
        grad = dot_tn(left[:, t * tile:(t + 1) * tile], right[...]).astype(bf16)
        for half in range(2):
            slab = lax.bitwise_xor(2 * t + half, dp) * layout.place
            for z in range(n_context):
                for lane in range(grad.shape[1] // 128):
                    start = z * layout.total + slab + offset + lane * piece
                    bundle[pl.ds(pl.multiple_of(start, 16), piece), :] = grad[
                        half * block + z * piece:half * block + (z + 1) * piece, lane * 128:(lane + 1) * 128
                    ]


def expert_grads(bundle, x, dz, hidden, dgate, dup, layout, run, dp, n_context, n_dp):
    width = x.shape[1]
    tile = 2 * width // n_dp
    for mat, source in enumerate((dgate, dup)):
        offset = layout.shared_place + run * layout.run_place + mat * layout.blocks * layout.piece
        matrix_grads(bundle, x, source, offset, layout, dp, n_context, n_dp)
    for t in range(n_dp // 2):
        grad = dot_tn(dz[:, t * tile:(t + 1) * tile], hidden[...]).astype(bf16)
        for z in range(n_context):
            start = z * layout.total + layout.down_at + run * width + t * tile
            bundle[start:start + tile, :] = grad[:, z * 128:(z + 1) * 128]


class Layout:
    def __init__(self, width, hidden, n_dp, n_context):
        self.piece = width // n_dp // n_context
        self.shared_blocks, self.blocks = hidden // 8 // 128, hidden // 4 // 128
        self.shared_place = 2 * self.shared_blocks * self.piece
        self.run_place = 2 * self.blocks * self.piece
        self.place = self.shared_place + 2 * self.run_place
        self.shared_down_at = n_dp * self.place
        self.down_rows = hidden // 8 // n_context
        self.down_at = self.shared_down_at + self.down_rows * (width // 128)
        self.total = self.down_at + 2 * width


def feed_grads_kernel(n_dp, layout, place, *refs):
    refs = list(refs)

    def take(count):
        part = refs[:count]
        del refs[:count]
        return part

    slabs = take(n_dp)
    shared_far = take(n_dp)
    downs = take(1)[0]
    got_downs = take(2)
    (gate, up, down, gate_s, up_s, down_s) = refs
    dp, side = place[1], place[5]
    core = place[3]
    piece = layout.piece
    hidden = gate.shape[2]
    columns = layout.blocks * 128
    width = down.shape[2]

    for mask in range(n_dp):
        source = lax.bitwise_xor(dp, mask)
        which = lax.bitwise_and(source, 1)
        for run in range(2):
            begin = (source // 2) * (2 * columns) + run * columns
            for mat, target in enumerate((gate, up)):
                for lane in range(layout.blocks):
                    start = layout.shared_place + run * layout.run_place + (mat * layout.blocks + lane) * piece
                    target[which, :, pl.ds(pl.multiple_of(begin + lane * 128, 128), 128)] = slabs[mask][
                        start:start + piece, :
                    ].astype(f32)
    base = layout.down_at - layout.shared_down_at
    kept = jnp.where(core == 0, downs[base:base + width, :], downs[base + width:, :])
    got = jnp.where(core == 0, got_downs[0][...], got_downs[1][...])
    down[core] = kept.astype(f32).T
    down[1 - core] = got.astype(f32).T

    lane_of = lax.broadcasted_iota(jnp.int32, (piece, 128), 1)
    for mask in range(n_dp):
        source = lax.bitwise_xor(dp, mask)
        for mat, target in enumerate((gate_s, up_s)):
            for lane in range(layout.shared_blocks):
                start = (mat * layout.shared_blocks + lane) * piece
                own = slabs[mask][start:start + piece, :].astype(f32)
                far = shared_far[mask][start:start + piece, :].astype(f32)
                first = jnp.where(side == 0, own, far)
                second = jnp.where(side == 0, far, own)
                begin = source * (hidden // n_dp) + lane * 256
                target[:, pl.ds(pl.multiple_of(begin, 128), 128)] = jnp.where(
                    lane_of < 64, first, pltpu.roll(second, 64, 1)
                )
                target[:, pl.ds(pl.multiple_of(begin + 128, 128), 128)] = jnp.where(
                    lane_of < 64, pltpu.roll(first, 64, 1), second
                )
    down_rows = layout.down_rows
    for lane in range(width // 128):
        rows = slice(lane * down_rows, (lane + 1) * down_rows)
        far_rows = slice(layout.shared_place + rows.start, layout.shared_place + rows.stop)
        lanes = slice(lane * 128, (lane + 1) * 128)
        down_s[pl.ds(pl.multiple_of(side * down_rows, 16), down_rows), lanes] = downs[rows, :].astype(f32)
        down_s[pl.ds(pl.multiple_of((1 - side) * down_rows, 16), down_rows), lanes] = shared_far[0][
            far_rows, :
        ].astype(f32)


def last_kernel(blocks, place, *refs):
    packs, (token, gain1, grad_own, grad_middle) = refs[:2], refs[2:6]
    pulled = refs[6:4 + blocks]
    (input_grad, qkv, out, norm1, norm2, router) = refs[4 + blocks:]
    side = place[5]
    piece, width = out.shape
    own, far_half = packs[0][...].astype(f32), packs[1][...].astype(f32)
    whole, start = [], 0
    for columns in ((3 * width // 2 + width + 128) // 2, (3 * width // 2 + 128) // 2):
        here, there = own[:, start:start + columns], far_half[:, start:start + columns]
        whole.append(jnp.concatenate([jnp.where(side == 0, here, there), jnp.where(side == 0, there, here)], axis=1))
        start += columns
    tile = width // 2
    for mat in range(3):
        for half in range(2):
            qkv[:, mat * width + half * tile:mat * width + (half + 1) * tile] = whole[half][
                :, mat * tile:(mat + 1) * tile
            ]
    out[...] = whole[0][:, 3 * tile:3 * tile + width]
    small = whole[1][:, 3 * tile:3 * tile + 128]
    small = jnp.concatenate([small, jnp.zeros((128 - piece, 128), f32)], axis=0).T
    router[...] = small[:router.shape[0], :piece]
    norm2[...] = small[8:9, :piece]
    norm1[...] = small[9:10, :piece]

    x = token[...].astype(f32)
    factor = lax.rsqrt(jnp.mean(x * x, axis=-1, keepdims=True) + norm_eps)
    normed = x * factor
    grad_entry = grad_own[...]
    for part in pulled:
        grad_entry = grad_entry + part[...].astype(f32)
    grad_norm = grad_entry * gain1[...]
    inner = jnp.mean(grad_norm * normed, axis=-1, keepdims=True)
    input_grad[...] = grad_middle[...] + factor * (grad_norm - normed * inner)


def load_turns(copies, sources, targets, blocks, rows, here):
    started = []
    for r in range(blocks):
        block = pl.ds(pl.multiple_of(jnp.maximum(here - r, 0) * rows, rows), rows)
        for source, target in zip(sources, targets):
            started.append(copies.start(source.at[block], target.at[r * rows:(r + 1) * rows]))
    return started


def attend_back(first, pairs, bias, queries, keys, values, log_total, grad_ctx, turns, grad_q, grad_kv):
    cos, sin_up, sin_down = turns
    rows = queries.shape[0]
    width = queries.shape[1]
    scale = HEAD_DIM ** (-0.5)
    half = lane_half(rows)

    def attend(pair, carry):
        lanes = pl.ds(pl.multiple_of(pair * 128, 128), 128)
        both_q = queries[:, lanes] * scale
        both_g = grad_ctx[:, pl.ds(pl.multiple_of((first + pair) * 128, 128), 128)]
        both_l = log_total[pair]
        dq = dk = dv = None
        for head in range(2):
            query = jnp.where(half == head, both_q, jnp.zeros_like(both_q))
            grad = jnp.where(half == head, both_g, jnp.zeros_like(both_g))
            log_row = both_l[:, head * HEAD_DIM:head * HEAD_DIM + 1]
            prob = jnp.exp(dot_nt(query, keys[:, lanes]) + bias - log_row)
            grad_prob = dot_nt(grad, values[:, lanes])
            delta = jnp.sum(prob * grad_prob, axis=-1, keepdims=True)
            grad_score = (prob * (grad_prob - delta)).astype(bf16)
            dq_head = dot_nn(grad_score, keys[:, lanes])
            dk_head = dot_tn(grad_score, query)
            dv_head = dot_tn(prob.astype(bf16), grad)
            if head == 0:
                dq, dk, dv = dq_head, dk_head, dv_head
            else:
                dq, dk, dv = jnp.where(half == 0, dq, dq_head), dk + dk_head, dv + dv_head
        grad_q[:, lanes] = spin_back(dq * scale, cos[:rows, :], sin_up[:rows, :], sin_down[:rows, :]).astype(bf16)
        far_lanes = pl.ds(pl.multiple_of(width + pair * 128, 128), 128)
        grad_kv[:, lanes] = spin_back(dk, cos[...], sin_up[...], sin_down[...]).astype(bf16)
        grad_kv[:, far_lanes] = dv.astype(bf16)
        return carry

    lax.fori_loop(0, pairs, attend, 0)


def store_pack(keep, send, value, start, dp, side, n_dp):
    n_half = keep.shape[-1]
    block = value.shape[0] // n_dp
    if start < n_half < start + value.shape[1]:
        store_pack(keep, send, value[:, :n_half - start], start, dp, side, n_dp)
        store_pack(keep, send, value[:, n_half - start:], n_half, dp, side, n_dp)
        return
    side_of = start // n_half
    lanes = slice(start - side_of * n_half, start - side_of * n_half + value.shape[1])
    flip_side = lax.bitwise_xor(side_of, side)
    for part in range(n_dp):
        piece = value[part * block:(part + 1) * block, :].astype(bf16)
        flip = lax.bitwise_xor(part, dp)

        @pl.when(lax.bitwise_and(flip, 1) == 0)
        def _():
            keep[flip // 2, flip_side, :, lanes] = piece

        @pl.when(lax.bitwise_and(flip, 1) == 1)
        def _():
            send[flip // 2, flip_side, :, lanes] = piece


def back_kernel(blocks, n_dp, place, *refs):
    parts = refs[:4]
    (
        middle, cot, gain2, out_w, queries_hbm, keys_hbm, values_hbm, log_hbm, context_hbm, entry_hbm, *turns_hbm
    ) = refs[4:17]
    (grad_middle, grad_ctx, grad_q, grad_kv, notes, keep, send) = refs[17:24]
    (queries, keys, values, log_total, context, entry, cos, sin_up, sin_down, sems) = refs[24:]
    rows, width = middle.shape
    here, dp, side = place[6], place[1], place[5]
    copies = Copies(sems)
    part = slice(0, queries.shape[1])
    turns = (cos, sin_up, sin_down)
    first_in = [
        copies.start(source, target)
        for source, target in (
            (queries_hbm.at[:, part], queries), (keys_hbm.at[:, part], keys), (values_hbm.at[:, part], values),
            (log_hbm.at[:log_total.shape[0]], log_total),
        )
    ]
    first_in += load_turns(copies, turns_hbm, turns, blocks, rows, here)
    late_in = [copies.start(context_hbm, context), copies.start(entry_hbm, entry)]

    grad_two = parts[0][...].astype(f32)
    for value in parts[1:]:
        grad_two = grad_two + value[...].astype(f32)
    mid = middle[...]
    factor = lax.rsqrt(jnp.mean(mid * mid, axis=-1, keepdims=True) + norm_eps)
    normed = mid * factor
    notes[...] = jnp.zeros_like(notes)
    notes[0:1, :] = jnp.sum(grad_two * normed, axis=0, keepdims=True)
    grad_norm = grad_two * gain2[...]
    inner = jnp.mean(grad_norm * normed, axis=-1, keepdims=True)
    grad_mid = cot[...].astype(f32) + factor * (grad_norm - normed * inner)
    grad_middle[...] = grad_mid
    grad_attn = grad_mid.astype(bf16)
    grad_ctx[...] = dot_nt(grad_attn, out_w[...]).astype(bf16)
    for copy in first_in:
        copy.wait()
    attend_back(
        0, log_total.shape[0], key_bias(blocks, rows, here), queries, keys, values, log_total, grad_ctx, turns, grad_q,
        grad_kv,
    )
    for copy in late_in:
        copy.wait()
    tile = queries.shape[1]
    store_pack(keep, send, dot_tn(entry[:rows, :], grad_q[...]), 0, dp, side, n_dp)
    for mat in range(2):
        grad = dot_tn(entry[...], grad_kv[:, mat * tile:(mat + 1) * tile])
        store_pack(keep, send, grad, (1 + mat) * tile, dp, side, n_dp)
    for start in range(0, width, tile):
        store_pack(keep, send, dot_tn(context[...], grad_attn[:, start:start + tile]), 3 * tile + start, dp, side, n_dp)
    used = 3 * tile + width
    store_pack(keep, send, jnp.zeros((width, 2 * keep.shape[-1] - used), f32), used, dp, side, n_dp)


def rest_kernel(blocks, n_dp, place, *refs):
    tokens_hbm = refs[:blocks]
    (notes, router_part, grad_ctx) = refs[blocks:blocks + 3]
    (
        queries_hbm, keys_hbm, values_hbm, log_hbm, entry_hbm, qkv_hbm, grad_q_hbm, grad_kv_hbm, *turns_hbm
    ) = refs[blocks + 3:blocks + 14]
    outs = refs[blocks + 14:]
    grad_own, grad_far, (keep, send) = outs[0], outs[1:blocks], outs[blocks:blocks + 2]
    (
        tokens, queries, keys, values, log_total, entry, qkv_w, grad_q0, grad_kv0, cos, sin_up, sin_down, grad_q,
        grad_kv, sems,
    ) = outs[blocks + 2:]
    rows, width = grad_ctx.shape
    here, dp, side = place[6], place[1], place[5]
    copies = Copies(sems)
    tile = queries.shape[1]
    pairs = log_total.shape[0]
    part = slice(tile, 2 * tile)
    turns = (cos, sin_up, sin_down)
    first_in = [
        copies.start(source, target)
        for source, target in (
            (queries_hbm.at[:, part], queries), (keys_hbm.at[:, part], keys), (values_hbm.at[:, part], values),
            (log_hbm.at[pairs:], log_total),
        )
    ]
    first_in += load_turns(copies, turns_hbm, turns, blocks, rows, here)
    late_in = [
        copies.start(source, target)
        for source, target in (
            (entry_hbm, entry), (qkv_hbm, qkv_w), (grad_q_hbm, grad_q0), (grad_kv_hbm, grad_kv0),
            *((tokens_hbm[r], tokens.at[r]) for r in range(blocks)),
        )
    ]
    for copy in first_in:
        copy.wait()
    attend_back(
        pairs, pairs, key_bias(blocks, rows, here), queries, keys, values, log_total, grad_ctx, turns, grad_q, grad_kv
    )
    for copy in late_in:
        copy.wait()
    store_pack(keep, send, dot_tn(entry[:rows, :], grad_q[...]), 0, dp, side, n_dp)
    for mat in range(2):
        grad = dot_tn(entry[...], grad_kv[:, mat * tile:(mat + 1) * tile])
        store_pack(keep, send, grad, (1 + mat) * tile, dp, side, n_dp)

    total = jnp.zeros((1, width), f32)
    for r in range(blocks):
        block = slice(r * rows, (r + 1) * rows)
        grad_entry = None
        for half, source in enumerate((grad_kv0, grad_kv)):
            for mat in range(2):
                start = (1 + mat) * width + half * tile
                term = dot_nt(source[block, mat * tile:(mat + 1) * tile], qkv_w[:, start:start + tile])
                grad_entry = term if grad_entry is None else grad_entry + term
        if r == 0:
            grad_entry = grad_entry + dot_nt(grad_q0[...], qkv_w[:, :tile]) + dot_nt(
                grad_q[...], qkv_w[:, tile:2 * tile]
            )
            grad_own[...] = grad_entry
        else:
            grad_far[r - 1][...] = grad_entry.astype(bf16)
        x = tokens[r].astype(f32)
        factor = lax.rsqrt(jnp.mean(x * x, axis=-1, keepdims=True) + norm_eps)
        total = total + jnp.sum(grad_entry * (x * factor), axis=0, keepdims=True)
    notes_t = notes[...].T
    total_t = jnp.broadcast_to(total, (8, width)).T
    lane = lax.broadcasted_iota(jnp.int32, (width, 128), 1)
    small = router_part[...] + jnp.where(lane == 8, notes_t[:, 0:1], 0.0) + jnp.where(
        lane == 9, total_t[:, 0:1], 0.0
    )
    store_pack(keep, send, small, 3 * tile, dp, side, n_dp)


def call(kernel, outs, scratch, scalars, operands, after=(), limit=60, aliases=None):
    whole = pl.BlockSpec(memory_space=pltpu.VMEM)
    anywhere = pl.BlockSpec(memory_space=pl.ANY)
    values, specs = [], []
    for value, kind in [*operands, *((value, far) for value in after)]:
        value = pltpu.with_memory_space_constraint(value, pltpu.VMEM if kind == held else pltpu.HBM)
        if isinstance(kind, int):
            kind = anywhere if kind == far else whole
        values.append(value)
        specs.append(kind)
    taken, ignored = len(operands), len(after)

    def body(place, *refs):
        kernel(place, *refs[:taken], *refs[taken + ignored:])

    return pl.pallas_call(
        body,
        grid_spec=pltpu.PrefetchScalarGridSpec(
            num_scalar_prefetch=1,
            grid=(1,),
            in_specs=specs,
            out_specs=[anywhere if kind == far else whole for _, _, kind in outs],
            scratch_shapes=scratch,
        ),
        out_shape=[
            pltpu.HBM(shape, dtype) for shape, dtype, _ in outs
        ],
        input_output_aliases=aliases or {},
        compiler_params=pltpu.CompilerParams(vmem_limit_bytes=limit * 2**20),
        cost_estimate=pl.CostEstimate(flops=10**8, bytes_accessed=0, transcendentals=0),
    )(scalars, *values)


def hold_until(scalars, values, after):
    return call(
        lambda place, *refs: None,
        [(value.shape, value.dtype, far) for value in values],
        [],
        scalars,
        [(value, far) for value in values],
        after,
        limit=1,
        aliases={1 + k: k for k in range(len(values))},
    )


def swap(value, mask):
    return lax.ppermute(value, group, [(i, i ^ mask) for i in range(8)])


def on_block(
    n_context,
    tokens,
    norm1_gain,
    qkv_weight,
    out_weight,
    norm2_gain,
    router_weight,
    expert_gate,
    expert_up,
    expert_down,
    shared_gate,
    shared_up,
    shared_down,
    routes,
    cotangent,
):
    rows, width = tokens.shape[1:]
    hidden = shared_gate.shape[1]
    n_experts = router_weight.shape[1]
    blocks = n_context
    n_dp = 4
    slots = rows * routes.shape[-1] * 5 // (4 * n_experts)
    dp = lax.axis_index(DP)
    here = lax.axis_index(CONTEXT)
    side = lax.axis_index(EXPERTS)
    core, chip = dp % 2, dp // 2
    index = dp * 2 + side
    expert = 2 * side + core
    pairs = width // 128

    own = tokens[0]
    cot = cotangent[0]
    cot_all = lax.all_gather(cot, group, axis=0)
    field = [own, lax.ppermute(own, CONTEXT, [(i, i + 1) for i in range(n_context - 1)])]
    field.append(lax.ppermute(field[1], CONTEXT, [(i, i + 1) for i in range(1, n_context - 1)]))
    field += [
        lax.ppermute(own, CONTEXT, [(i, i + r) for i in range(n_context - r)]) for r in range(3, blocks)
    ]
    tables = spin_tables(n_context * rows)
    gain1, gain2 = norm1_gain[None, :], norm2_gain[None, :]
    scalars = jnp.stack([index, dp, expert, core, chip, side, here])
    piece = width // n_dp // n_context
    half_columns = hidden // 2
    chunk_columns = hidden // 4
    shared_columns = hidden // 8
    quarter = hidden // n_dp

    def many(kind, *values):
        return [(value, kind) for value in values]

    router = jnp.pad(router_weight, ((0, 0), (0, 128 - n_experts)))
    router_t = jnp.pad(router_weight.T, ((0, 128 - n_experts), (0, 0)))

    picked_up = ((width, shared_columns), bf16, copied)
    picked = call(
        partial(pick_kernel, n_context),
        [picked_up, picked_up, ((shared_columns, width), bf16, copied)],
        [],
        scalars,
        [
            (shared_gate, pl.BlockSpec((width, quarter), lambda i, s: (0, s[1]))),
            (shared_up, pl.BlockSpec((width, quarter), lambda i, s: (0, s[1]))),
            (shared_down, pl.BlockSpec((quarter, width), lambda i, s: (s[1], 0))),
        ],
        [router, router_t],
        limit=10,
    )

    act = (rows, width)
    wide = (blocks * rows, width)
    sent = (rows + 16, width)
    logs = (pairs, rows, 128)
    turn = (blocks * rows, 128)
    entry, queries, keys, values, log_total, context, middle, entry_two = call(
        partial(attend_kernel, blocks),
        [
            (wide, bf16, far), (act, bf16, far), (wide, bf16, far), (wide, bf16, far), (logs, f32, far),
            (act, bf16, far), (act, f32, copied), (sent, bf16, copied),
        ],
        [
            *[pltpu.VMEM(turn, f32)] * 3, pltpu.VMEM(wide, bf16), pltpu.VMEM(act, bf16), pltpu.VMEM(wide, bf16),
            pltpu.VMEM(wide, bf16), pltpu.VMEM(logs, f32), pltpu.VMEM(act, bf16), pltpu.SemaphoreType.DMA((32,)),
        ],
        jnp.stack([here]),
        [
            *many(copied, *field, routes[0, 0].T, gain1), *many(held, qkv_weight, out_weight),
            (gain2, copied), *many(far, *tables),
        ],
        [picked[0]],
        limit=24,
    )

    near = {0: entry_two}
    near[1], near[4] = swap(entry_two, 1), swap(entry_two, 4)
    near[5] = swap(near[1], 4)
    for mask in keep_masks:
        near[mask ^ 2] = swap(near[mask], 2)

    layout = Layout(width, hidden, n_dp, n_context)
    slot_act, row_act, four = (8 * slots, width), (8 * rows, width), (4, rows, width)
    bundle_rows = n_context * layout.total
    grad_keep, grad_send, mix_keep, mix_send, router_part, bundle = call(
        partial(feed_kernel, all_masks, n_context, n_dp, layout),
        [*[(four, bf16, far)] * 4, ((width, 128), f32, copied), ((bundle_rows, 128), bf16, far)],
        [
            pltpu.VMEM((8 * slots, 128), f32), pltpu.VMEM((8, slots, rows), bf16), *[pltpu.VMEM(slot_act, bf16)] * 3,
            *[pltpu.VMEM(slot_act, f32)] * 2, *[pltpu.VMEM(row_act, bf16)] * 2,
            *[pltpu.VMEM((2, width, chunk_columns), bf16)] * 2, pltpu.VMEM((2, chunk_columns, width), bf16),
            *[pltpu.VMEM((width, shared_columns), bf16)] * 2, pltpu.VMEM((shared_columns, width), bf16),
            *[pltpu.VMEM((8 * slots, chunk_columns), bf16)] * 3, *[pltpu.VMEM((8 * rows, shared_columns), bf16)] * 3,
            *[pltpu.VMEM(four, bf16)] * 2, pltpu.VMEM((bundle_rows, 128), bf16), pltpu.VMEM((8, 16, width), bf16),
            pltpu.SemaphoreType.DMA((64,)),
        ],
        scalars,
        [
            *many(far, *[near[mask] for mask in all_masks], cot_all), *many(copied, router, router_t),
            *many(far, *picked, expert_gate, expert_up, expert_down),
        ],
        limit=60,
    )
    reduced = lax.psum_scatter(bundle, CONTEXT, scatter_dimension=0, tiled=True)

    def add_blocks(left, right):
        return [
            (left[k].astype(f32) + right[k].astype(f32)).astype(bf16) for k in range(left.shape[0])
        ]

    grad_sums = add_blocks(grad_keep, swap(grad_send, 2))
    parts = [grad_sums[0], *[swap(value, mask) for value, mask in zip(grad_sums[1:], keep_masks[1:])]]

    mix_sums = add_blocks(mix_keep, swap(mix_send, 2))
    sent_mix = hold_until(scalars, mix_sums[1:], parts[1:])
    mix_parts = [middle, mix_sums[0], *[swap(value, mask) for value, mask in zip(sent_mix, keep_masks[1:])]]

    tile = width // 2
    pack_rows = width // n_dp
    half_act, half_wide, half_logs = (rows, tile), (blocks * rows, tile), (pairs // 2, rows, 128)
    pack0 = (2, 2, pack_rows, (3 * tile + width + 128) // 2)
    pack1 = (2, 2, pack_rows, (3 * tile + 128) // 2)
    half_heads = [
        pltpu.VMEM(half_act, bf16), pltpu.VMEM(half_wide, bf16), pltpu.VMEM(half_wide, bf16), pltpu.VMEM(half_logs, f32)
    ]
    turn_scratch = [pltpu.VMEM(turn, f32)] * 3
    grad_middle, grad_ctx, grad_q, grad_kv, notes, keep0, send0 = call(
        partial(back_kernel, blocks, n_dp),
        [
            (act, f32, copied), (act, bf16, copied), (half_act, bf16, copied), (wide, bf16, copied),
            ((8, width), f32, copied), (pack0, bf16, copied), (pack0, bf16, copied),
        ],
        [
            *half_heads, pltpu.VMEM(act, bf16), pltpu.VMEM(wide, bf16), *turn_scratch, pltpu.SemaphoreType.DMA((24,)),
        ],
        scalars,
        [
            *many(copied, *parts, middle, cot, gain2, out_weight),
            *many(far, queries, keys, values, log_total, context, entry, *tables),
        ],
        sent_mix,
        limit=44,
    )

    def by_chips(keep, send):
        other = swap(send, 2)
        sums = [(keep[i, j].astype(f32) + other[i, j].astype(f32)).astype(bf16) for i in range(2) for j in range(2)]
        return [sums[0], swap(sums[1], 1), swap(sums[2], 4), swap(sums[3], 5)]

    def by_context(sets, after):
        columns = sum(arrived[0].shape[1] for arrived in sets)
        shares = call(
            partial(sum_kernel, n_context, [len(arrived) for arrived in sets]),
            [((piece, columns), bf16, copied)] * n_context, [], scalars,
            many(copied, *[value for arrived in sets for value in arrived]), after, limit=16,
        )
        return [shares[0]] + [
            lax.ppermute(shares[r], CONTEXT, [(i, (i + r) % n_context) for i in range(n_context)])
            for r in range(1, n_context)
        ]

    def total(shares):
        value = sum(value.astype(f32) for value in shares).astype(bf16)
        return [value, swap(value, 1)]

    send0, = hold_until(scalars, [send0], mix_parts[2:])
    arrived0 = by_chips(keep0, send0)
    results = call(
        partial(rest_kernel, blocks, n_dp),
        [(act, f32, copied), *[(act, bf16, copied)] * (blocks - 1), *[(pack1, bf16, copied)] * 2],
        [
            pltpu.VMEM((blocks, rows, width), bf16), *half_heads, pltpu.VMEM(wide, bf16),
            pltpu.VMEM(qkv_weight.shape, bf16), pltpu.VMEM(half_act, bf16), pltpu.VMEM(wide, bf16), *turn_scratch,
            pltpu.VMEM(half_act, bf16), pltpu.VMEM(wide, bf16), pltpu.SemaphoreType.DMA((32,)),
        ],
        scalars,
        [
            *many(far, *field), *many(copied, notes, router_part, grad_ctx),
            *many(far, queries, keys, values, log_total, entry, qkv_weight, grad_q, grad_kv, *tables),
        ],
        [arrived0[0]],
        limit=44,
    )
    grad_own, keep1 = results[0], results[blocks]
    *grad_far, send1 = hold_until(scalars, [*results[1:blocks], results[blocks + 1]], arrived0[1:])
    output = sum(value.astype(f32) for value in mix_parts).astype(bf16)[None]

    arrived1 = by_chips(keep1, send1)
    passed = lax.ppermute(grad_far[1], CONTEXT, [(i, i - 1) for i in range(2, n_context)])
    farther = [
        lax.ppermute(grad_far[r - 1], CONTEXT, [(i, i - r) for i in range(r, n_context)]) for r in range(3, blocks)
    ]
    nearest = (grad_far[0].astype(f32) + passed.astype(f32)).astype(bf16)
    pulled = [lax.ppermute(nearest, CONTEXT, [(i, i - 1) for i in range(1, n_context)]), *farther]
    shares = by_context([arrived0, arrived1], [passed, *farther])
    reduced, = hold_until(scalars, [reduced], [shares[0]])
    slabs = [reduced[m * layout.place:(m + 1) * layout.place] for m in range(n_dp)]
    downs = reduced[layout.shared_down_at:]
    base = layout.down_at - layout.shared_down_at
    shared = [slab[:layout.shared_place] for slab in slabs]
    shared[0] = jnp.concatenate([shared[0], downs[:base]], axis=0)
    shared_far = [swap(value, 2 * m + 1) for m, value in enumerate(shared)]
    slabs = [slabs[0]] + [swap(slabs[m], 2 * m) for m in range(1, n_dp)]
    got_downs = [
        lax.ppermute(
            downs[base + run * width:base + (run + 1) * width], DP, [(i, i ^ 1) for i in range(n_dp) if i % 2 != run]
        )
        for run in range(2)
    ]

    shares = [shares[0], *hold_until(scalars, shares[1:], [pulled[0]])]
    spread = total(shares)
    gate_grad, up_grad, down_grad, gate_s_grad, up_s_grad, down_s_grad = call(
        partial(feed_grads_kernel, n_dp, layout),
        [
            (shape, f32, copied)
            for shape in (
                (2, piece, hidden), (2, piece, hidden), (2, 128, width), (piece, hidden), (piece, hidden),
                (hidden // n_dp // n_context, width),
            )
        ],
        [],
        scalars,
        many(copied, *slabs, *shared_far, downs, *got_downs),
        [spread[0]],
        limit=32,
    )
    input_grad, qkv_grad, out_grad, norm1_grad, norm2_grad, router_grad = call(
        partial(last_kernel, blocks),
        [
            (shape, f32, copied)
            for shape in (act, (piece, 3 * width), (piece, width), (1, piece), (1, piece), (n_experts, piece))
        ],
        [],
        scalars,
        many(copied, *spread, own, gain1, grad_own, grad_middle, *pulled),
        limit=32,
    )
    return (
        output, input_grad[None], norm1_grad[0], qkv_grad, out_grad, norm2_grad[0], router_grad.T,
        gate_grad, up_grad, down_grad, gate_s_grad, up_s_grad, down_s_grad,
    )


def on_any(mesh, *args):
    tokens, router_weight, expert_gate, shared_gate = args[0], args[5], args[6], args[9]
    sizes = dict(mesh.shape)
    fits = (
        sizes[DP] == 4
        and sizes[EXPERTS] == 2
        and tokens.shape[0] == 1
        and tokens.shape[1] == BLOCK
        and expert_gate.shape[0] == 2
        and tokens.shape[2] % 128 == 0
        and tokens.shape[2] // sizes[DP] % (16 * sizes[CONTEXT]) == 0
        and shared_gate.shape[1] % (1024) == 0
        and sizes[CONTEXT] == 4
        and shared_gate.shape[1] == 128 * sizes[DP] * sizes[CONTEXT]
    )
    if fits:
        return on_block(sizes[CONTEXT], *args)
    return on_device(*args)


def solution(mesh):
    return jax.shard_map(
        partial(on_any, mesh),
        mesh=mesh,
        in_specs=(
            P((DP, EXPERTS), CONTEXT, None),
            P(),
            P(),
            P(),
            P(),
            P(),
            P(EXPERTS, None, None),
            P(EXPERTS, None, None),
            P(EXPERTS, None, None),
            P(),
            P(),
            P(),
            P(CONTEXT, (DP, EXPERTS), None, None),
            P((DP, EXPERTS), CONTEXT, None),
        ),
        out_specs=(
            P((DP, EXPERTS), CONTEXT, None),
            P((DP, EXPERTS), CONTEXT, None),
            P((DP, CONTEXT)),
            P((DP, CONTEXT), None),
            P((DP, CONTEXT), None),
            P((DP, CONTEXT)),
            P((DP, CONTEXT), None),
            P(EXPERTS, (DP, CONTEXT), None),
            P(EXPERTS, (DP, CONTEXT), None),
            P(EXPERTS, (DP, CONTEXT), None),
            P((DP, CONTEXT), None),
            P((DP, CONTEXT), None),
            P((DP, CONTEXT), None),
        ),
        check_vma=False,
    )
```
